32 devices in a mesh: scene: 4 (over y, core), tp: 8 (over z, x).
Axes of the slice: x: 2, y: 2, z: 4, core: 2. Of those that a mesh axis runs over, the one named last changes fastest.
Arguments:
- frames_in: bfloat16 [4, 2048, 1024], P('scene', 'tp'), may hold values from -6 to 6
- qkv_weight: bfloat16 [2, 1024, 3072], P(None, None, 'tp'), may hold values from -0.1875 to 0.1875
- qkv_bias: bfloat16 [2, 3072], P(None, 'tp'), may hold values from -1.796875 to 1.796875
- out_weight: bfloat16 [2, 1024, 1024], P(None, 'tp'), may hold values from -0.75 to 0.75
- up_weight: bfloat16 [2, 1024, 4096], P(None, None, 'tp'), may hold values from -0.1875 to 0.1875
- up_bias: bfloat16 [2, 4096], P(None, 'tp'), may hold values from -1.796875 to 1.796875
- down_weight: bfloat16 [2, 4096, 1024], P(None, 'tp'), may hold values from -0.09375 to 0.09375
- norm_gain: float32 [2, 4, 1024], replicated, may hold values from 0.5 to 1.5
- norm_offset: float32 [2, 4, 1024], replicated, may hold values from -1.8 to 1.8
- head_gain: float32 [2, 2, 64], replicated, may hold values from 0.5 to 1.5
- head_offset: float32 [2, 2, 64], replicated, may hold values from -1.8 to 1.8
- cotangent: bfloat16 [4, 2048, 1024], P('scene', 'tp'), may hold values from -6 to 6
- visible: int32 [4, 2048], P('scene', 'tp'), may hold values 0 or 1
- query_count: int32 [4], P('scene'), may hold values from 128 to 512
Outputs:
- layer_out: bfloat16 [4, 2048, 1024], P('scene', 'tp')
- input_grad: bfloat16 [4, 2048, 1024], P('scene', 'tp')
- qkv_weight_grad: float32 [2, 1024, 3072], P(None, None, 'tp')
- qkv_bias_grad: float32 [2, 3072], P(None, 'tp')
- out_weight_grad: float32 [2, 1024, 1024], P(None, 'tp')
- up_weight_grad: float32 [2, 1024, 4096], P(None, None, 'tp')
- up_bias_grad: float32 [2, 4096], P(None, 'tp')
- down_weight_grad: float32 [2, 4096, 1024], P(None, 'tp')
- norm_gain_grad: float32 [2, 4, 1024], replicated
- norm_offset_grad: float32 [2, 4, 1024], replicated
- head_gain_grad: float32 [2, 2, 64], replicated
- head_offset_grad: float32 [2, 2, 64], replicated
The draws below stay inside these ranges and needn't reach their ends.
All inputs are finite; a program needn't handle non-finite values. No bound on the sum of `visible` on one device may be relied on, other than what follows from the above.
Results may differ from the reference program's by a relative error of at most 0.03.
Values may be sent and summed in bfloat16 or wider, within the bound.
A program may use at most 256 MiB of HBM per device.

```python
import jax
import jax.numpy as jnp
from jax import lax

D = 1024
HEADS = 16
HD = 64
FF = 4096
QMAX = 512
FRAME_TOK = 1024
SCENE_TOK = 2048
SCENES = 4
N_TP = 8


def place_ends(drawn, stream_key, smallest, top_value):
    longest = drawn.shape.index(max(drawn.shape))
    spots = []
    for shift in (0, 1):
        where = [jax.random.randint(jax.random.fold_in(stream_key, axis), (), 0, length) for axis, length in enumerate(drawn.shape)]
        where[longest] = (where[longest] + shift) % drawn.shape[longest]
        spots.append(tuple(where))
    return drawn.at[spots[0]].set(smallest).at[spots[1]].set(top_value)


def level_of(rng, shape, pieces, least, high):
    level = 1.0
    for position, blocks in pieces:
        heights = jax.random.uniform(jax.random.fold_in(jax.random.fold_in(rng, 6), position), (blocks,), jnp.float32, least / len(pieces), high / len(pieces))
        level = level * jnp.repeat(jnp.exp(heights), shape[position] // blocks).reshape((-1,) + (1,) * (len(shape) - 1 - position))
    return level


def scatter_about(key, shape, scale, reach, shards=(), kind=jnp.bfloat16):
    loudness = level_of(key, shape, shards, -0.22, 0.18) if shards else 1.0
    entries = jax.random.normal(key, shape, jnp.float32) * scale * loudness
    return jnp.minimum(jnp.maximum(entries, -reach), reach).astype(kind)


def setup_inputs(seed: int = 0) -> dict:
    keys = jax.random.split(jax.random.key(seed), 15)
    frames_in = scatter_about(keys[0], (SCENES, SCENE_TOK, D), 1.0, 6.0, ((0, 4), (1, 8)))
    qkv_weight = scatter_about(keys[1], (2, D, 3 * D), D ** -0.5, 0.1875, ((2, 8),))
    qkv_bias = scatter_about(keys[2], (2, 3 * D), 0.3, 1.796875, ((1, 8),))
    out_weight = scatter_about(keys[3], (2, D, D), HD ** -0.5, 0.75, ((1, 8),))
    up_weight = scatter_about(keys[4], (2, D, FF), D ** -0.5, 0.1875, ((2, 8),))
    up_bias = scatter_about(keys[5], (2, FF), 0.3, 1.796875, ((1, 8),))
    down_weight = scatter_about(keys[6], (2, FF, D), FF ** -0.5, 0.09375, ((1, 8),))
    norm_gain = jnp.clip(1.0 + 0.1 * jax.random.normal(keys[7], (2, 4, D), jnp.float32), 0.5, 1.5)
    norm_offset = scatter_about(keys[8], (2, 4, D), 0.3, 1.8, (), jnp.float32)
    head_gain = jnp.clip(1.0 + 0.1 * jax.random.normal(keys[9], (2, 2, HD), jnp.float32), 0.5, 1.5)
    head_offset = scatter_about(keys[10], (2, 2, HD), 0.3, 1.8, (), jnp.float32)
    cotangent = scatter_about(keys[11], (SCENES, SCENE_TOK, D), 1.0, 6.0, ((0, 4), (1, 8)))
    visible = place_ends((jax.random.randint(keys[12], (SCENES, SCENE_TOK), 0, 4) < 3).astype(jnp.int32), jax.random.fold_in(keys[12], 1), 0, 1)
    query_count = place_ends(jax.random.randint(keys[13], (SCENES,), QMAX // 4, QMAX + 1), jax.random.fold_in(keys[13], 1), QMAX // 4, QMAX).astype(jnp.int32)
    return {"frames_in": frames_in, "qkv_weight": qkv_weight, "qkv_bias": qkv_bias, "out_weight": out_weight, "up_weight": up_weight, "up_bias": up_bias, "down_weight": down_weight, "norm_gain": norm_gain, "norm_offset": norm_offset, "head_gain": head_gain, "head_offset": head_offset, "cotangent": cotangent, "visible": visible, "query_count": query_count}


@jax.custom_vjp
def low(v):
    return lax.optimization_barrier(v.astype(jnp.bfloat16)).astype(jnp.float32)

@jax.custom_vjp
def low_back(v):
    return v

def low_keep(v):
    return (low(v), None)

def low_pass(kept, grad):
    return (grad,)

def back_keep(v):
    return (v, None)

def back_low(kept, grad):
    return (low(grad),)
low.defvjp(low_keep, low_pass)
low_back.defvjp(back_keep, back_low)
EPSILON = 1e-06
HIGHEST = lax.Precision.HIGHEST

def layer_norm(values, norm_scale, norm_bias):
    average = lax.optimization_barrier(jnp.mean(values, axis=-1, keepdims=True))
    centered = values - average
    variance = lax.optimization_barrier(jnp.mean(centered * centered, axis=-1, keepdims=True))
    return centered * lax.rsqrt(variance + EPSILON) * norm_scale + norm_bias

def attend(query_rows, key_rows, value_rows):
    scores = jnp.einsum('qhe,khe->hqk', query_rows, key_rows, precision=HIGHEST) * HD ** (-0.5)
    scores = low_back(scores)
    largest = lax.optimization_barrier(jnp.max(scores, axis=-1, keepdims=True))
    unnormed = jnp.exp(scores - largest)
    probs = low(unnormed / lax.optimization_barrier(jnp.sum(unnormed, axis=-1, keepdims=True)))
    return jnp.einsum('hqk,khe->qhe', probs, value_rows, precision=HIGHEST)

def attention(queries, key_all, value_all, frame_only):
    frame_shape = (queries.shape[0] // FRAME_TOK, FRAME_TOK) + queries.shape[1:]
    query_frames = queries.reshape(frame_shape)
    checked = jax.checkpoint(attend)
    if frame_only:
        mixed = lax.map(lambda triple: checked(triple[0], triple[1], triple[2]), (query_frames, key_all.reshape(frame_shape), value_all.reshape(frame_shape)))
    else:
        mixed = lax.map(lambda query_block: checked(query_block, key_all, value_all), query_frames)
    return mixed.reshape(queries.shape)

def layer(hidden, params, frame_only):
    qkv_weight, qkv_bias, out_weight, up_weight, up_bias, down_weight, norm_gain, norm_offset, head_gain, head_offset = params
    tokens = hidden.shape[0]
    normed = low(layer_norm(hidden, norm_gain[0], norm_offset[0]))
    spread = low_back(jnp.broadcast_to(normed, (N_TP,) + normed.shape))
    projected = jnp.einsum('gtd,dgc->gtc', spread, qkv_weight.reshape(D, N_TP, -1), precision=HIGHEST)
    projected = low_back(projected + qkv_bias.reshape(N_TP, 1, -1))
    projected = jnp.transpose(projected.reshape(N_TP, tokens, HEADS // N_TP, 3, HD), (1, 0, 2, 3, 4))
    projected = projected.reshape(tokens, HEADS, 3, HD)
    queries = low(layer_norm(projected[:, :, 0], head_gain[0], head_offset[0]))
    key_all = low(layer_norm(projected[:, :, 1], head_gain[1], head_offset[1]))
    value_all = low(projected[:, :, 2])
    mixed = low(low_back(attention(queries, key_all, value_all, frame_only)))
    partial_attn = low(jnp.einsum('tgc,gcd->gtd', mixed.reshape(tokens, N_TP, D // N_TP), out_weight.reshape(N_TP, D // N_TP, D), precision=HIGHEST))
    branch = low_back(lax.optimization_barrier(jnp.sum(partial_attn, axis=0))) + norm_offset[2]
    middle = hidden + norm_gain[2] * branch
    second = low(layer_norm(middle, norm_gain[1], norm_offset[1]))
    spread_two = low_back(jnp.broadcast_to(second, (N_TP,) + second.shape))
    hidden_up = jnp.einsum('gtd,dgf->gtf', spread_two, up_weight.reshape(D, N_TP, FF // N_TP), precision=HIGHEST)
    hidden_up = low_back(hidden_up + up_bias.reshape(N_TP, 1, -1))
    activated = low(jax.nn.gelu(hidden_up, approximate=False))
    partial_mlp = low(jnp.einsum('gtf,gfd->gtd', activated, down_weight.reshape(N_TP, FF // N_TP, D), precision=HIGHEST))
    branch_two = low_back(lax.optimization_barrier(jnp.sum(partial_mlp, axis=0))) + norm_offset[3]
    return middle + norm_gain[3] * branch_two

def forward(frames_in, params):
    hidden = frames_in
    for block_index in range(2):
        hidden = layer(hidden, tuple((stacked[block_index] for stacked in params)), block_index == 0)
    return hidden

def reference(frames_in, qkv_weight, qkv_bias, out_weight, up_weight, up_bias, down_weight, norm_gain, norm_offset, head_gain, head_offset, cotangent, visible, query_count):
    params = tuple((stacked.astype(jnp.float32) for stacked in (qkv_weight, qkv_bias, out_weight, up_weight, up_bias, down_weight, norm_gain, norm_offset, head_gain, head_offset)))

    def scene_step(gradient_sum, scene_item):
        scene_in, scene_cot, scene_vis, scene_count = scene_item
        result, pull = jax.vjp(forward, scene_in.astype(jnp.float32), params)
        weighting = scene_cot.astype(jnp.float32) * scene_vis.astype(jnp.float32)[:, None] * (scene_count.astype(jnp.float32) / QMAX)
        grad_in, grad_params = pull(weighting)
        gradient_sum = jax.tree.map(jnp.add, gradient_sum, grad_params)
        return (gradient_sum, (result.astype(jnp.bfloat16), grad_in.astype(jnp.bfloat16)))
    zero_grads = jax.tree.map(jnp.zeros_like, params)
    gradient_sum, (layer_out, input_grad) = lax.scan(scene_step, zero_grads, (frames_in, cotangent, visible, query_count))
    return (layer_out, input_grad, gradient_sum[0], gradient_sum[1], gradient_sum[2], gradient_sum[3], gradient_sum[4], gradient_sum[5], gradient_sum[6], gradient_sum[7], gradient_sum[8], gradient_sum[9])
```

```python
import functools

import jax
import jax.numpy as jnp
from jax import lax
from jax.experimental import pallas as pl
from jax.experimental.pallas import tpu as pltpu
from jax.sharding import PartitionSpec as P

HD = 64
QMAX = 512
FRAME_TOK = 1024
EPSILON = 1e-06
BF = jnp.bfloat16
F32 = jnp.float32
MESH = pl.DeviceIdType.MESH
VMEM_LIMIT = 60 * 1024 * 1024

AXES = ("sy", "c", "h", "zl", "x")


def dot(left, right):
    return lax.dot_general(left, right, (((1,), (0,)), ((), ())), preferred_element_type=F32)


def dot_rt(left, right):
    return lax.dot_general(left, right, (((1,), (1,)), ((), ())), preferred_element_type=F32)


def dot_lt(left, right):
    return lax.dot_general(left, right, (((0,), (0,)), ((), ())), preferred_element_type=F32)


def dot_exact(left, right):
    return lax.dot_general(
        left, right, (((1,), (0,)), ((), ())), precision=lax.Precision.HIGHEST, preferred_element_type=F32
    )


def remote(source, target, send, recv, device):
    return pltpu.make_async_remote_copy(
        src_ref=source, dst_ref=target, send_sem=send, recv_sem=recv, device_id=device, device_id_type=MESH
    )


class Spot:
    def __init__(self):
        self.c = lax.axis_index("c")
        self.zl = lax.axis_index("zl")
        self.x = lax.axis_index("x")
        self.over_x = {"x": 1 - self.x}
        self.over_z = {"zl": 1 - self.zl}
        self.core = {"c": 1 - self.c}

    def greet(self):
        barrier = pltpu.get_barrier_semaphore()
        for device in (self.over_x, self.over_z, self.core):
            pl.semaphore_signal(barrier, inc=1, device_id=device, device_id_type=MESH)
        pl.semaphore_wait(barrier, 3)

    def slot(self, core, step):
        zl = lax.rem(self.zl + step // 2, 2)
        x = lax.rem(self.x + step % 2, 2)
        return core * 4 + zl * 2 + x


class Gather:
    @staticmethod
    def scratch(rows, width):
        dma = pltpu.SemaphoreType.DMA
        return [pltpu.VMEM((8, rows, width), BF), dma((6,)), dma((6,)), dma((4,)), dma((4,))]

    def __init__(self, spot, refs):
        self.spot = spot
        self.held, send, recv, self.core_send, self.core_recv = refs
        half = self.held.shape[1] // 2
        self.half = half

        def copy(step, part, number, device):
            ref = self.held.at[spot.slot(spot.c, step), pl.ds(part * half, half)]
            return remote(ref, ref, send.at[number], recv.at[number], device)

        self.x_first = copy(0, 0, 0, spot.over_x)
        self.x_later = copy(0, 1, 1, spot.over_x)
        self.z_later = copy(0, 0, 2, spot.over_z)
        self.z_first = copy(0, 1, 3, spot.over_z)
        self.z_relay = copy(1, 0, 4, spot.over_z)
        self.x_relay = copy(2, 1, 5, spot.over_x)

    def core_copy(self, step):
        ref = self.held.at[self.spot.slot(self.spot.c, step)]
        return remote(ref, ref, self.core_send.at[step], self.core_recv.at[step], self.spot.core)

    def put(self, part, values):
        self.held[self.spot.slot(self.spot.c, 0), pl.ds(part * self.half, self.half)] = values
        if part == 0:
            self.x_first.start()
            self.z_later.start()
        else:
            self.z_first.start()
            self.x_later.start()

    def arrive(self, step):
        @pl.when(step == 1)
        def _():
            self.x_first.wait_recv()
            self.z_relay.start()
            self.z_first.wait_recv()
            self.x_relay.start()
            self.x_later.wait_recv()

        @pl.when(step == 2)
        def _():
            self.z_later.wait_recv()

        @pl.when(step == 3)
        def _():
            self.z_relay.wait_recv()
            self.x_relay.wait_recv()

        self.core_copy(step).start()

    def arrive_core(self, step):
        self.core_copy(step).wait_recv()

    def finish(self):
        for copy in (self.x_first, self.x_later, self.z_first, self.z_later, self.z_relay, self.x_relay):
            copy.wait_send()
        for step in range(4):
            self.core_copy(step).wait_send()


class Scatter:
    @staticmethod
    def local(rows, width):
        half = rows // 2
        return [
            pltpu.VMEM((4, rows, width), BF),
            pltpu.VMEM((4, rows, width), BF),
            pltpu.VMEM((4, rows, width), F32),
            pltpu.VMEM((2, half, width), BF),
        ]

    @staticmethod
    def scratch(rows, width):
        dma = pltpu.SemaphoreType.DMA
        half = rows // 2
        return [
            pltpu.VMEM((4, rows, width), BF),
            pltpu.VMEM((6, half, width), BF),
            dma((4,)),
            dma((4,)),
            dma((6,)),
            dma((6,)),
        ]

    def __init__(self, spot, local, refs):
        self.spot = spot
        self.for_core, self.ready, self.sums, self.relayed = local
        self.from_core, self.landed, self.core_send, self.core_recv, send, recv = refs
        half = self.for_core.shape[1] // 2
        self.half = half
        first, later = pl.ds(0, half), pl.ds(half, half)

        def copy(source, number, device):
            return remote(source, self.landed.at[number], send.at[number], recv.at[number], device)

        self.x_near = copy(self.ready.at[1, first], 0, spot.over_x)
        self.x_far = copy(self.ready.at[3, first], 1, spot.over_x)
        self.z_near = copy(self.ready.at[2, later], 2, spot.over_z)
        self.z_far = copy(self.ready.at[3, later], 3, spot.over_z)
        self.z_relay = copy(self.relayed.at[0], 4, spot.over_z)
        self.x_relay = copy(self.relayed.at[1], 5, spot.over_x)

    def core_copy(self, step):
        return remote(
            self.for_core.at[step],
            self.from_core.at[step],
            self.core_send.at[step],
            self.core_recv.at[step],
            self.spot.core,
        )

    def put_other(self, step, values):
        self.for_core[step] = values.astype(BF)
        self.core_copy(step).start()

    def put_own(self, step, values):
        self.sums[step] = values

    def flush(self, step):
        self.core_copy(step).wait_recv()
        total = self.sums[step] + self.from_core[step].astype(F32)
        self.sums[step] = total
        self.ready[step] = total.astype(BF)

        @pl.when(step == 1)
        def _():
            self.x_near.start()

        @pl.when(step == 2)
        def _():
            self.z_near.start()

        @pl.when(step == 3)
        def _():
            self.x_far.start()
            self.z_far.start()

    def relay(self):
        half = self.half
        self.x_far.wait_recv()
        self.relayed[0] = (self.sums[2, pl.ds(0, half)] + self.landed[1].astype(F32)).astype(BF)
        self.z_relay.start()
        self.z_far.wait_recv()
        self.relayed[1] = (self.sums[1, pl.ds(half, half)] + self.landed[3].astype(F32)).astype(BF)
        self.x_relay.start()

    def result(self, part):
        near, last = (self.x_near, self.z_relay) if part == 0 else (self.z_near, self.x_relay)
        near.wait_recv()
        last.wait_recv()
        near_at, last_at = (0, 4) if part == 0 else (2, 5)
        return (
            self.sums[0, pl.ds(part * self.half, self.half)]
            + self.landed[near_at].astype(F32)
            + self.landed[last_at].astype(F32)
        )

    def finish(self):
        for copy in (self.x_near, self.x_far, self.z_near, self.z_far, self.z_relay, self.x_relay):
            copy.wait_send()
        for step in range(4):
            self.core_copy(step).wait_send()

    def produce(self, term):
        def visit(index, carry):
            step = 3 - index
            self.put_other(step, term(self.spot.slot(1 - self.spot.c, step)))
            self.put_own(step, term(self.spot.slot(self.spot.c, step)))
            self.flush(step)
            return carry

        lax.fori_loop(0, 4, visit, 0)


def norm_parts(values):
    average = jnp.mean(values, axis=-1, keepdims=True)
    centered = values - average
    scale = lax.rsqrt(jnp.mean(centered * centered, axis=-1, keepdims=True) + EPSILON)
    return centered * scale, scale


def norm_back(grad, gain, normed, scale):
    scaled = grad * gain
    back = scale * (
        scaled
        - jnp.mean(scaled, axis=-1, keepdims=True)
        - normed * jnp.mean(scaled * normed, axis=-1, keepdims=True)
    )
    return back, jnp.sum(grad * normed, axis=0, keepdims=True), jnp.sum(grad, axis=0, keepdims=True)


def gelu_both(values):
    size = jnp.abs(values) * 0.7071067811865476
    bell = jnp.exp(-size * size)
    t = 1.0 / (1.0 + 0.3275911 * size)
    poly = t * (
        0.254829592 + t * (-0.284496736 + t * (1.421413741 + t * (-1.453152027 + t * 1.061405429)))
    )
    tail = 0.5 * poly * bell
    below = jnp.where(values < 0, tail, 1.0 - tail)
    return values * below, below + values * bell * 0.3989422804014327


def lanes_of_head(shape, head):
    lane = lax.broadcasted_iota(jnp.int32, shape, 1)
    return (lane < HD) if head == 0 else (lane >= HD)


def averager(width):
    row = lax.broadcasted_iota(jnp.int32, (width, width), 0) // HD
    column = lax.broadcasted_iota(jnp.int32, (width, width), 1) // HD
    return jnp.where(row == column, 1.0 / HD, 0.0).astype(F32)


def project(rows, weight, bias, head_gain, head_offset, raw_ref, qk_ref, v_ref, slot):
    projected = dot(rows, weight[...]) + bias[...]
    raw = projected[:, : 4 * HD]
    raw_ref[slot] = raw
    average = averager(4 * HD)
    centered = raw - dot_exact(raw, average)
    scale = lax.rsqrt(dot_exact(centered * centered, average) + EPSILON)
    qk_ref[slot] = (centered * scale * head_gain[...] + head_offset[...]).astype(BF)
    v_ref[slot] = projected[:, 4 * HD :].astype(BF)


def first_kernel(
    frames, gains, offsets, weight, bias, head_gain, head_offset, gathered_out, raw_out, qk_out, v_out, *scratch
):
    spot = Spot()
    spot.greet()
    gather = Gather(spot, scratch[:5])
    saved = scratch[5]
    half = gather.half
    for part in range(2):
        rows = frames[pl.ds(part * half, half)].astype(F32)
        gather.put(part, (norm_parts(rows)[0] * gains[0:1] + offsets[0:1]).astype(BF))

    def use(slot):
        project(gather.held[slot], weight, bias, head_gain, head_offset, raw_out, qk_out, v_out, slot)

    def visit(step, carry):
        gather.arrive(step)
        use(spot.slot(spot.c, step))
        gather.arrive_core(step)
        use(spot.slot(1 - spot.c, step))
        return carry

    lax.fori_loop(0, 4, visit, 0)
    copy = pltpu.make_async_copy(gather.held, gathered_out, saved)
    copy.start()
    gather.finish()
    copy.wait()


def forward_kernel(is_last, *refs):
    (mixed, hidden, out_weight, up_weight, up_bias, down_weight, gains, offsets) = refs[:8]
    refs = refs[8:]
    if not is_last:
        (next_gains, next_offsets, weight, bias, head_gain, head_offset) = refs[:6]
        refs = refs[6:]
    (branch_out, middle_out, second_out, activated_out, slope_out, branch_two_out, state_out) = refs[:7]
    refs = refs[7:]
    if not is_last:
        (gathered_out, raw_out, qk_out, v_out) = refs[:4]
        refs = refs[4:]
    local, one, two, held, saved = refs[:4], refs[4:10], refs[10:16], refs[16:21], refs[21]
    spot = Spot()
    spot.greet()
    first, gather, later = Scatter(spot, local, one), Gather(spot, held), Scatter(spot, local, two)
    half = gather.half
    first.produce(lambda slot: dot(mixed[slot], out_weight[...]))
    first.relay()
    for part in range(2):
        rows = pl.ds(part * half, half)
        branch = first.result(part) + offsets[2:3]
        middle = hidden[rows].astype(F32) + gains[2:3] * branch
        branch_out[rows] = branch
        middle_out[rows] = middle
        gather.put(part, (norm_parts(middle)[0] * gains[1:2] + offsets[1:2]).astype(BF))
    first.finish()

    def term(slot):
        activated, slope = gelu_both(dot(gather.held[slot], up_weight[...]) + up_bias[...])
        activated = activated.astype(BF)
        activated_out[slot] = activated
        slope_out[slot] = slope.astype(BF)
        return dot(activated, down_weight[...])

    def visit(step, carry):
        gather.arrive(step)
        later.put_own(step, term(spot.slot(spot.c, step)))
        gather.arrive_core(step)
        later.put_other(step, term(spot.slot(1 - spot.c, step)))

        @pl.when(step > 0)
        def _():
            later.flush(step - 1)

        return carry

    lax.fori_loop(0, 4, visit, 0)
    later.flush(3)
    copy = pltpu.make_async_copy(gather.held, second_out, saved.at[0])
    copy.start()
    gather.finish()
    later.relay()
    if not is_last:
        onward = Gather(spot, refs[22:27])
    for part in range(2):
        rows = pl.ds(part * half, half)
        branch_two = later.result(part) + offsets[3:4]
        state = middle_out[rows] + gains[3:4] * branch_two
        branch_two_out[rows] = branch_two
        state_out[rows] = state.astype(state_out.dtype)
        if not is_last:
            onward.put(part, (norm_parts(state)[0] * next_gains[0:1] + next_offsets[0:1]).astype(BF))
    if not is_last:

        def use(slot):
            project(onward.held[slot], weight, bias, head_gain, head_offset, raw_out, qk_out, v_out, slot)

        def visit_next(step, carry):
            onward.arrive(step)
            use(spot.slot(spot.c, step))
            onward.arrive_core(step)
            use(spot.slot(1 - spot.c, step))
            return carry

        lax.fori_loop(0, 4, visit_next, 0)
        copy_next = pltpu.make_async_copy(onward.held, gathered_out, saved.at[1])
        copy_next.start()
        onward.finish()
        copy_next.wait()
    later.finish()
    copy.wait()


def backward_kernel(is_first, *refs):
    if is_first:
        (grad_ref,) = refs[:1]
        refs = refs[1:]
    else:
        (grad_qkv, above_weight, above_hidden, above_middle_grad, above_gains) = refs[:5]
        refs = refs[5:]
    (branch_two, activated, slope, second, middle, branch, mixed) = refs[:7]
    (down_weight, up_weight, out_weight, gains) = refs[7:11]
    refs = refs[11:]
    (middle_grad_out, mixed_grad_out, down_grad, up_grad, out_grad, up_bias_grad, small) = refs[:7]
    refs = refs[7:]
    local, one, held, held_two, up_rows, grad_rows, = refs[:4], refs[4:10], refs[10:15], refs[15:20], refs[20], refs[21]
    spot = Spot()
    spot.greet()
    gather, scatter, onward = Gather(spot, held), Scatter(spot, local, one), Gather(spot, held_two)
    half = gather.half
    small[...] = jnp.zeros_like(small)
    if not is_first:
        above = Scatter(spot, local, refs[22:28])
        above.produce(lambda slot: dot_rt(grad_qkv[slot], above_weight[...]))
        above.relay()
    for part in range(2):
        rows = pl.ds(part * half, half)
        if is_first:
            grad = grad_ref[rows]
        else:
            normed, scale = norm_parts(above_hidden[rows].astype(F32))
            grad, gain_term, offset_term = norm_back(above.result(part), above_gains[0:1], normed, scale)
            small[6:7] += gain_term
            small[7:8] += offset_term
            grad = grad + above_middle_grad[rows]
        grad_rows[rows] = grad
        scaled = gains[3:4] * grad
        gather.put(part, scaled.astype(BF))
        small[0:1] += jnp.sum(grad * branch_two[rows], axis=0, keepdims=True)
        small[1:2] += jnp.sum(scaled, axis=0, keepdims=True)
    if not is_first:
        above.finish()

    def term(slot):
        up = (dot_rt(gather.held[slot], down_weight[...]) * slope[slot].astype(F32)).astype(BF)
        up_rows[slot] = up
        return dot_rt(up, up_weight[...])

    def visit(step, carry):
        gather.arrive(step)
        scatter.put_own(step, term(spot.slot(spot.c, step)))
        gather.arrive_core(step)
        scatter.put_other(step, term(spot.slot(1 - spot.c, step)))

        @pl.when(step > 0)
        def _():
            scatter.flush(step - 1)

        return carry

    lax.fori_loop(0, 4, visit, 0)
    scatter.flush(3)
    gather.finish()
    wide = lambda ref: ref[...].reshape(ref.shape[0] * ref.shape[1], ref.shape[2])
    down_grad[...] = dot_lt(wide(activated), wide(gather.held)).astype(BF)
    scatter.relay()
    up_grad[...] = dot_lt(wide(second), wide(up_rows)).astype(BF)
    up_bias_grad[...] = jnp.sum(wide(up_rows).astype(F32), axis=0, keepdims=True)
    for part in range(2):
        rows = pl.ds(part * half, half)
        normed, scale = norm_parts(middle[rows])
        grad, gain_term, offset_term = norm_back(scatter.result(part), gains[1:2], normed, scale)
        grad = grad + grad_rows[rows]
        middle_grad_out[rows] = grad
        scaled = gains[2:3] * grad
        onward.put(part, scaled.astype(BF))
        small[2:3] += gain_term
        small[3:4] += offset_term
        small[4:5] += jnp.sum(grad * branch[rows], axis=0, keepdims=True)
        small[5:6] += jnp.sum(scaled, axis=0, keepdims=True)
    scatter.finish()

    def use(slot):
        mixed_grad_out[slot] = dot_rt(onward.held[slot], out_weight[...]).astype(BF)

    def visit_next(step, carry):
        onward.arrive(step)
        use(spot.slot(spot.c, step))
        onward.arrive_core(step)
        use(spot.slot(1 - spot.c, step))
        return carry

    lax.fori_loop(0, 4, visit_next, 0)
    onward.finish()
    out_grad[...] = dot_lt(wide(mixed), wide(onward.held)).astype(BF)


def last_kernel(grad_qkv, weight, hidden, middle_grad, gains, grad_out, small, *refs):
    spot = Spot()
    spot.greet()
    scatter = Scatter(spot, refs[:4], refs[4:10])
    half = scatter.half
    scatter.produce(lambda slot: dot_rt(grad_qkv[slot], weight[...]))
    scatter.relay()
    small[...] = jnp.zeros_like(small)
    for part in range(2):
        rows = pl.ds(part * half, half)
        normed, scale = norm_parts(hidden[rows].astype(F32))
        grad, gain_term, offset_term = norm_back(scatter.result(part), gains[0:1], normed, scale)
        small[0:1] += gain_term
        small[1:2] += offset_term
        grad_out[rows] = (grad + middle_grad[rows]).astype(BF)
    scatter.finish()


def in_three(values):
    high = values.astype(BF)
    rest = values - high.astype(F32)
    middle = rest.astype(BF)
    return high, middle, (rest - middle.astype(F32)).astype(BF)


def beside(rows, values, head):
    lane = lax.broadcasted_iota(jnp.int32, rows.shape, 1)
    start = HD if head == 0 else 0
    high, middle, low = (part.astype(F32) for part in in_three(values))
    other = jnp.where(
        lane == start, high, jnp.where(lane == start + 1, middle, jnp.where(lane == start + 2, low, 0.0))
    )
    return jnp.where(lanes_of_head(rows.shape, head), rows.astype(F32), other).astype(BF)


def attention_kernel(keys, block, qk, v, mixed, exact, query_out):
    def visit(index, carry):
        base = pl.multiple_of(index * block, block)
        rows = pl.ds(base, block)
        span = pl.ds(pl.multiple_of(base // keys * keys, keys), keys)
        queries = qk[rows, : 2 * HD] * jnp.asarray(HD**-0.5, BF)
        found = []
        for head in range(2):
            mine = jnp.where(lanes_of_head(queries.shape, head), queries, jnp.zeros_like(queries))
            scores = dot_rt(mine, qk[span, 2 * HD :])
            largest = jnp.max(scores, axis=-1, keepdims=True)
            weights = jnp.exp(scores - largest)
            total = jnp.sum(weights, axis=-1, keepdims=True)
            found.append(dot(weights.astype(BF), v[span, :]) / total)
            query_out[head, rows] = beside(mine, largest + jnp.log(total), head)
        both = jnp.where(lanes_of_head(found[0].shape, 0), found[0], found[1])
        exact[rows] = both
        mixed[rows] = both.astype(BF)
        return carry

    lax.fori_loop(0, mixed.shape[0] // block, visit, 0)


def attention_back_kernel(
    keys, block, raw, qk, v, mixed, query, grad, head_gain, grad_qkv, small, bias_grad, grads, key_in, value_in, grad_in
):
    tokens = grad.shape[0]
    width = 2 * HD
    grads[...] = jnp.zeros_like(grads)
    lane_sum = averager(width)
    row = lax.broadcasted_iota(jnp.int32, (width, width), 0) // HD
    column = lax.broadcasted_iota(jnp.int32, (width, width), 1) // HD
    swap_sum = jnp.where(row != column, 1.0, 0.0).astype(F32)
    del lane_sum

    def prepare(index, carry):
        rows = pl.ds(pl.multiple_of(index * block, block), block)
        product = grad[rows].astype(F32) * mixed[rows]
        delta = dot_exact(product, swap_sum)
        minus = jnp.full((block, width), -1.0, F32)
        lane = lax.broadcasted_iota(jnp.int32, (block, width), 1)
        high, middle, low = (part.astype(F32) for part in in_three(delta))
        for head in range(2):
            start = HD if head == 0 else 0
            own = lanes_of_head((block, width), head)
            other = jnp.where(
                lane == start, high, jnp.where(lane == start + 1, middle, jnp.where(lane == start + 2, low, 0.0))
            )
            grad_in[head, rows] = jnp.where(own, grad[rows].astype(F32), other).astype(BF)
            ones = jnp.where(own, 0.0, jnp.where(lane < start + 3, minus, 0.0))
            key_in[head, rows] = jnp.where(own, qk[rows, width:].astype(F32), ones).astype(BF)
            value_in[head, rows] = jnp.where(own, v[rows].astype(F32), ones).astype(BF)
        return carry

    lax.fori_loop(0, tokens // block, prepare, 0)
    spans = keys // block

    def visit(index, carry):
        query_at = index // spans
        key_at = query_at * block // keys * spans + lax.rem(index, spans)
        query_rows = pl.ds(pl.multiple_of(query_at * block, block), block)
        key_rows = pl.ds(pl.multiple_of(key_at * block, block), block)
        for head in range(2):
            own = lanes_of_head((block, width), head)
            zeros = jnp.zeros((block, width), BF)
            query_rows_in = query[head, query_rows]
            grad_rows_in = grad_in[head, query_rows]
            key_rows_in = key_in[head, key_rows]
            probs = jnp.exp(dot_rt(key_rows_in, query_rows_in))
            back = (probs * dot_rt(value_in[head, key_rows], grad_rows_in)).astype(BF)
            grads[key_rows, 2 * width :] += dot(probs.astype(BF), jnp.where(own, grad_rows_in, zeros))
            grads[key_rows, width : 2 * width] += dot(back, jnp.where(own, query_rows_in, zeros))
            grads[query_rows, :width] += dot_lt(back, jnp.where(own, key_rows_in, zeros))
        return carry

    lax.fori_loop(0, tokens // block * spans, visit, 0)
    small[...] = jnp.zeros_like(small)
    bias_grad[...] = jnp.zeros_like(bias_grad)
    average = averager(2 * width)

    def leave(index, carry):
        rows = pl.ds(pl.multiple_of(index * block, block), block)
        values = raw[rows]
        centered = values - dot_exact(values, average)
        scale = lax.rsqrt(dot_exact(centered * centered, average) + EPSILON)
        normed = centered * scale
        lane = lax.broadcasted_iota(jnp.int32, normed.shape, 1)
        found = grads[rows, : 2 * width] * jnp.where(lane < width, HD**-0.5, 1.0)
        small[0:1] += jnp.sum(found * normed, axis=0, keepdims=True)
        small[1:2] += jnp.sum(found, axis=0, keepdims=True)
        scaled = found * head_gain[...]
        back = scale * (scaled - dot_exact(scaled, average) - normed * dot_exact(scaled * normed, average))
        back = back.astype(BF)
        values_back = grads[rows, 2 * width :].astype(BF)
        grad_qkv[rows, : 2 * width] = back
        grad_qkv[rows, 2 * width :] = values_back
        bias_grad[:, : 2 * width] += jnp.sum(back.astype(F32), axis=0, keepdims=True)
        bias_grad[:, 2 * width :] += jnp.sum(values_back.astype(F32), axis=0, keepdims=True)
        return carry

    lax.fori_loop(0, tokens // block, leave, 0)


def over_square(kernel, name, outs, operands, scratch, number, outside=()):
    return pl.pallas_call(
        kernel,
        name=name,
        out_shape=outs,
        in_specs=[pl.BlockSpec(memory_space=pltpu.VMEM)] * len(operands),
        out_specs=[
            pl.BlockSpec(memory_space=pl.ANY if place in outside else pltpu.VMEM) for place in range(len(outs))
        ],
        scratch_shapes=scratch,
        compiler_params=pltpu.CompilerParams(
            collective_id=number, has_side_effects=True, vmem_limit_bytes=VMEM_LIMIT
        ),
    )(*operands)


def alone(kernel, name, outs, operands, scratch=()):
    return pl.pallas_call(
        kernel,
        name=name,
        out_shape=outs,
        in_specs=[pl.BlockSpec(memory_space=pltpu.VMEM)] * len(operands),
        out_specs=[pl.BlockSpec(memory_space=pltpu.VMEM)] * len(outs),
        scratch_shapes=list(scratch),
        compiler_params=pltpu.CompilerParams(vmem_limit_bytes=VMEM_LIMIT),
    )(*operands)


def shape(*sizes):
    return jax.ShapeDtypeStruct(sizes[:-1], sizes[-1])


def exchange(values):
    return lax.ppermute(values, ("c", "h"), [(0, 0), (1, 2), (2, 1), (3, 3)])


def by_kind(values):
    split = values.reshape(values.shape[:-1] + (2, 3, HD))
    return jnp.swapaxes(split, -3, -2).reshape(values.shape)


def by_head(values):
    split = values.reshape(values.shape[:-1] + (3, 2, HD))
    return jnp.swapaxes(split, -3, -2).reshape(values.shape)


def over_scenes(grad):
    sy, c, h = (lax.axis_index(name) for name in ("sy", "c", "h"))
    halves = grad.reshape(2, grad.shape[0] // 2, grad.shape[1])
    keep = lax.dynamic_index_in_dim(halves, sy, 0, keepdims=False)
    give = lax.dynamic_index_in_dim(halves, 1 - sy, 0, keepdims=False)
    got = lax.ppermute(give, "sy", [(0, 1), (1, 0)])
    share = (keep.astype(F32) + got.astype(F32)).astype(BF)
    got = lax.ppermute(share, ("c", "h"), [(1, 0), (2, 3)])
    share = (share.astype(F32) + got.astype(F32)).astype(BF)
    other = lax.ppermute(share, ("sy", "c", "h"), [(0, 4), (4, 0), (3, 7), (7, 3)])
    home = c == h
    core = [(0, 2), (3, 1)]
    share = jnp.where(home, share, lax.ppermute(share, ("c", "h"), core))
    other = jnp.where(home, other, lax.ppermute(other, ("c", "h"), core))
    first, later = jnp.where(sy == 0, share, other), jnp.where(sy == 0, other, share)
    return jnp.concatenate([first, later], axis=0)


def square_body(
    frames_in,
    qkv_weight,
    qkv_bias,
    out_weight,
    up_weight,
    up_bias,
    down_weight,
    norm_gain,
    norm_offset,
    head_gain,
    head_offset,
    cotangent,
    visible,
    query_count,
):
    rows, width = frames_in.shape[1:]
    tokens = 8 * rows
    inner = mid = 2 * HD
    hidden_units = up_weight.shape[2]
    frames = exchange(frames_in[0])
    qkv_weights, out_weights, up_weights, down_weights, qkv_biases, up_biases = (
        [exchange(stacked[block]) for block in range(2)]
        for stacked in (by_kind(qkv_weight), out_weight, up_weight, down_weight, by_kind(qkv_bias), up_bias)
    )
    qkv_biases = [bias.astype(F32)[None] for bias in qkv_biases]
    up_biases = [bias.astype(F32)[None] for bias in up_biases]
    weighting = visible[0].astype(F32) * (query_count[0].astype(F32) / QMAX)
    grad = exchange(cotangent[0]).astype(F32) * exchange(weighting)[:, None]
    head_gains, head_offsets = (
        [jnp.concatenate([pair[block, 0]] * 2 + [pair[block, 1]] * 2)[None] for block in range(2)]
        for pair in (head_gain, head_offset)
    )
    gather = Gather.scratch(rows, width)
    local, scatter = Scatter.local(rows, width), Scatter.scratch(rows, width)
    dma = pltpu.SemaphoreType.DMA
    qkv_outs = [
        shape(8, rows, width, BF),
        shape(8, rows, 2 * inner, F32),
        shape(8, rows, 2 * inner, BF),
        shape(8, rows, inner, BF),
    ]

    def attend(block, raw, qk, v):
        keys = FRAME_TOK if block == 0 else tokens
        flat = [part.reshape(tokens, part.shape[2]) for part in (qk, v)]
        return alone(
            functools.partial(attention_kernel, keys, 256),
            f"attention_{block}",
            [shape(tokens, inner, BF), shape(tokens, inner, F32), shape(2, tokens, inner, BF)],
            flat,
        )

    def attend_back(block, saved, grad_mixed):
        keys = FRAME_TOK if block == 0 else tokens
        flat = [part.reshape(tokens, part.shape[2]) for part in (saved["raw"], saved["qk"], saved["v"])]
        return alone(
            functools.partial(attention_back_kernel, keys, 512),
            f"attention_back_{block}",
            [shape(tokens, 3 * inner, BF), shape(2, 2 * inner, F32), shape(1, 3 * inner, F32)],
            flat + [saved["exact"], saved["query"], grad_mixed.reshape(tokens, inner), head_gains[block]],
            [pltpu.VMEM((tokens, 3 * inner), F32)] + [pltpu.VMEM((2, tokens, inner), BF)] * 3,
        )

    saved = [{}, {}]
    gathered, raw, qk, v = over_square(
        first_kernel,
        "gather_project",
        qkv_outs,
        [frames, norm_gain[0], norm_offset[0], qkv_weights[0], qkv_biases[0], head_gains[0], head_offsets[0]],
        gather + [dma],
        0,
        (0,),
    )
    hidden = frames
    for block in range(2):
        is_last = block == 1
        mixed, exact, query = attend(block, raw, qk, v)
        saved[block].update(hidden=hidden, gathered=gathered, raw=raw, qk=qk, v=v, mixed=mixed, exact=exact, query=query)
        operands = [
            mixed.reshape(8, rows, inner),
            hidden,
            out_weights[block],
            up_weights[block],
            up_biases[block],
            down_weights[block],
            norm_gain[block],
            norm_offset[block],
        ]
        outs = [
            shape(rows, width, F32),
            shape(rows, width, F32),
            shape(8, rows, width, BF),
            shape(8, rows, hidden_units, BF),
            shape(8, rows, hidden_units, BF),
            shape(rows, width, F32),
            shape(rows, width, BF if is_last else F32),
        ]
        scratch = local + scatter + scatter + gather + [dma((2,))]
        if not is_last:
            operands += [
                norm_gain[1], norm_offset[1], qkv_weights[1], qkv_biases[1], head_gains[1], head_offsets[1],
            ]
            outs += qkv_outs
            scratch += gather
        found = over_square(
            functools.partial(forward_kernel, is_last),
            f"feed_forward_{block}",
            outs,
            operands,
            scratch,
            1 + block,
            (2,) if is_last else (2, 7),
        )
        names = ("branch", "middle", "second", "activated", "slope", "branch_two")
        saved[block].update(zip(names, found))
        hidden = found[6]
        if not is_last:
            gathered, raw, qk, v = found[7:]
    layer_out = exchange(hidden)[None]

    large = [None, None]
    gain_rows, offset_rows = [[None] * 4, [None] * 4], [[None] * 4, [None] * 4]
    up_bias_grads, qkv_bias_grads, head_grads = [None, None], [None, None], [None, None]
    back = None
    for block in (1, 0):
        is_first = block == 1
        kept = saved[block]
        if is_first:
            operands = [grad]
        else:
            above = saved[1]
            operands = [
                back.reshape(8, rows, 3 * inner), qkv_weights[1], above["hidden"], middle_grad, norm_gain[1],
            ]
        operands += [kept[name] for name in ("branch_two", "activated", "slope", "second", "middle", "branch")]
        operands += [kept["mixed"].reshape(8, rows, inner)]
        operands += [down_weights[block], up_weights[block], out_weights[block], norm_gain[block]]
        middle_grad, mixed_grad, down_grad, up_grad, out_grad, up_bias_grads[block], small = over_square(
            functools.partial(backward_kernel, is_first),
            f"feed_back_{block}",
            [
                shape(rows, width, F32),
                shape(8, rows, inner, BF),
                shape(hidden_units, width, BF),
                shape(width, hidden_units, BF),
                shape(inner, width, BF),
                shape(1, hidden_units, F32),
                shape(8, width, F32),
            ],
            operands,
            local
            + scatter
            + gather
            + gather
            + [pltpu.VMEM((8, rows, hidden_units), BF), pltpu.VMEM((rows, width), F32)]
            + ([] if is_first else scatter),
            3 + block,
        )
        gain_rows[block][3], offset_rows[block][3] = small[0], small[1]
        gain_rows[block][1], offset_rows[block][1] = small[2], small[3]
        gain_rows[block][2], offset_rows[block][2] = small[4], small[5]
        if not is_first:
            gain_rows[1][0], offset_rows[1][0] = small[6], small[7]
        back, head_grads[block], qkv_bias_grads[block] = attend_back(block, kept, mixed_grad)
        qkv_grad = jnp.einsum(
            "td,tc->dc", kept["gathered"].reshape(tokens, width), back, preferred_element_type=F32
        ).astype(BF)
        large[block] = [over_scenes(part) for part in (qkv_grad, out_grad, up_grad, down_grad)]
    grad_in, small = over_square(
        last_kernel,
        "project_back",
        [shape(rows, width, BF), shape(8, width, F32)],
        [back.reshape(8, rows, 3 * inner), qkv_weights[0], saved[0]["hidden"], middle_grad, norm_gain[0]],
        local + scatter,
        5,
    )
    gain_rows[0][0], offset_rows[0][0] = small[0], small[1]
    input_grad = exchange(grad_in)[None]

    c, h, zl, x = (lax.axis_index(name) for name in ("c", "h", "zl", "x"))
    place = zl * 2 + x
    biases = jnp.stack(
        [jnp.concatenate([by_head(qkv_bias_grads[block][0]), up_bias_grads[block][0]]) for block in range(2)]
    )
    biases = jnp.where(jnp.arange(8)[:, None, None] == c * 4 + place, biases[None], 0.0)
    heads = jnp.stack(head_grads).reshape(2, 2, 2, 2, HD).sum(axis=3)
    small = (
        jnp.stack([jnp.stack(part) for part in gain_rows]),
        jnp.stack([jnp.stack(part) for part in offset_rows]),
        heads,
        biases,
    )
    gain_grad, offset_grad, heads, biases = lax.psum(small, AXES)
    biases = lax.dynamic_index_in_dim(biases, h * 4 + place, 0, keepdims=False)
    qkv_grad, out_grad, up_grad, down_grad = (
        jnp.stack([first, later]).astype(F32) for first, later in zip(large[0], large[1])
    )
    return (
        layer_out,
        input_grad,
        by_head(qkv_grad),
        biases[:, : 3 * inner],
        out_grad,
        up_grad,
        biases[:, 3 * inner :],
        down_grad,
        gain_grad,
        offset_grad,
        heads[:, 0],
        heads[:, 1],
    )


TP = ("c", "r")


def layer_norm(values, norm_scale, norm_bias):
    average = jnp.mean(values, axis=-1, keepdims=True)
    centered = values - average
    variance = jnp.mean(centered * centered, axis=-1, keepdims=True)
    return centered * lax.rsqrt(variance + EPSILON) * norm_scale + norm_bias


def exact_gelu(values):
    return jax.nn.gelu(values, approximate=False)


def attend_rows(query_rows, key_rows, value_rows, score_scale):
    scores = (
        jnp.einsum("qhe,khe->hqk", query_rows, key_rows, preferred_element_type=jnp.float32)
        * score_scale
    )
    largest = jnp.max(scores, axis=-1, keepdims=True)
    unnormed = jnp.exp(scores - largest)
    denominator = jnp.sum(unnormed, axis=-1, keepdims=True)
    weights = (unnormed / denominator).astype(jnp.bfloat16)
    mixed = jnp.einsum("hqk,khe->qhe", weights, value_rows, preferred_element_type=jnp.float32)
    return (mixed, (largest + jnp.log(denominator))[:, :, 0])


def attend_back(query_rows, key_rows, value_rows, log_total, grad_rows, score_scale):
    scores = (
        jnp.einsum("qhe,khe->hqk", query_rows, key_rows, preferred_element_type=jnp.float32)
        * score_scale
    )
    probs = jnp.exp(scores - log_total[:, :, None])
    grad_probs = jnp.einsum(
        "qhe,khe->hqk", grad_rows, value_rows, preferred_element_type=jnp.float32
    )
    grad_scores = probs * (grad_probs - jnp.sum(probs * grad_probs, axis=-1, keepdims=True))
    grad_scores = grad_scores.astype(jnp.bfloat16)
    grad_query = (
        jnp.einsum("hqk,khe->qhe", grad_scores, key_rows, preferred_element_type=jnp.float32)
        * score_scale
    )
    grad_key = (
        jnp.einsum("hqk,qhe->khe", grad_scores, query_rows, preferred_element_type=jnp.float32)
        * score_scale
    )
    grad_value = jnp.einsum(
        "hqk,qhe->khe", probs.astype(jnp.bfloat16), grad_rows, preferred_element_type=jnp.float32
    )
    return (grad_query, grad_key, grad_value)


def attention_forward(queries, key_all, value_all, frame_only, score_scale):
    frame_shape = (queries.shape[0] // FRAME_TOK, FRAME_TOK) + queries.shape[1:]
    query_frames = queries.reshape(frame_shape)
    if frame_only:
        mixed, log_total = lax.map(
            lambda triple: attend_rows(triple[0], triple[1], triple[2], score_scale),
            (query_frames, key_all.reshape(frame_shape), value_all.reshape(frame_shape)),
        )
    else:
        mixed, log_total = lax.map(
            lambda query_block: attend_rows(query_block, key_all, value_all, score_scale),
            query_frames,
        )
    return (mixed.reshape(queries.shape), log_total)


def attention_backward(queries, key_all, value_all, log_total, grad_mixed, frame_only, score_scale):
    frame_shape = (queries.shape[0] // FRAME_TOK, FRAME_TOK) + queries.shape[1:]
    query_frames = queries.reshape(frame_shape)
    grad_frames = grad_mixed.reshape(frame_shape)
    if frame_only:
        grad_query, grad_key, grad_value = lax.map(
            lambda group_in: attend_back(
                group_in[0], group_in[1], group_in[2], group_in[3], group_in[4], score_scale
            ),
            (
                query_frames,
                key_all.reshape(frame_shape),
                value_all.reshape(frame_shape),
                log_total,
                grad_frames,
            ),
        )
        return (
            grad_query.reshape(queries.shape),
            grad_key.reshape(queries.shape),
            grad_value.reshape(queries.shape),
        )

    def visit_frame(running, group_in):
        grad_query, grad_key, grad_value = attend_back(
            group_in[0], key_all, value_all, group_in[1], group_in[2], score_scale
        )
        return ((running[0] + grad_key, running[1] + grad_value), grad_query)

    zero_keys = jnp.zeros(key_all.shape, jnp.float32)
    (grad_key, grad_value), grad_query = lax.scan(
        visit_frame, (zero_keys, zero_keys), (query_frames, log_total, grad_frames)
    )
    return (grad_query.reshape(queries.shape), grad_key, grad_value)


def any_body(
    frames_in,
    qkv_weight,
    qkv_bias,
    out_weight,
    up_weight,
    up_bias,
    down_weight,
    norm_gain,
    norm_offset,
    head_gain,
    head_offset,
    cotangent,
    visible,
    query_count,
):
    score_scale = HD ** (-0.5)
    frames = exchange(frames_in[0])
    qkv_weight, out_weight, up_weight, down_weight, qkv_bias, up_bias = (
        [exchange(stacked[block_index]) for block_index in range(2)]
        for stacked in (qkv_weight, out_weight, up_weight, down_weight, qkv_bias, up_bias)
    )
    weighting = visible[0].astype(jnp.float32) * (query_count[0].astype(jnp.float32) / QMAX)
    weighting = exchange(weighting)
    cotangent = exchange(cotangent[0])

    def backward_block(grad_out, block_index, frame_only, saved):
        (
            hidden,
            gathered,
            split,
            queries,
            key_all,
            value_all,
            log_total,
            mixed_flat,
            branch,
            middle,
            gathered_two,
            hidden_up,
            activated,
            branch_two,
        ) = saved
        gains = norm_gain[block_index]
        offsets = norm_offset[block_index]
        total_rows = split.shape[0]
        grad_branch_two = gains[3] * grad_out
        offset_grad_three = jnp.sum(grad_branch_two, axis=0)
        gain_grad_three = jnp.sum(grad_out * branch_two, axis=0)
        shard_rows = lax.all_gather(grad_branch_two.astype(jnp.bfloat16), TP, axis=0, tiled=True)
        down_grad = jnp.einsum(
            "tf,td->fd", activated, shard_rows, preferred_element_type=jnp.float32
        )
        act_grad = jnp.einsum(
            "td,fd->tf", shard_rows, down_weight[block_index], preferred_element_type=jnp.float32
        )
        up_grad = jax.vjp(exact_gelu, hidden_up)[1](act_grad)[0].astype(jnp.bfloat16)
        down_grad, up_grads = (down_grad, up_grad)
        up_weight_grad = jnp.einsum(
            "td,tf->df", gathered_two, up_grads, preferred_element_type=jnp.float32
        )
        up_bias_grad = jnp.sum(up_grads.astype(jnp.float32), axis=0)
        second_grad = lax.psum_scatter(
            jnp.einsum(
                "tf,df->td", up_grads, up_weight[block_index], preferred_element_type=jnp.float32
            ).astype(jnp.bfloat16),
            TP,
            scatter_dimension=0,
            tiled=True,
        ).astype(jnp.float32)
        middle_grad, gain_grad_one, offset_grad_one = jax.vjp(
            layer_norm, middle, gains[1], offsets[1]
        )[1](second_grad)
        middle_grad = middle_grad + grad_out
        grad_branch = gains[2] * middle_grad
        offset_grad_two = jnp.sum(grad_branch, axis=0)
        gain_grad_two = jnp.sum(middle_grad * branch, axis=0)
        shard_rows = lax.all_gather(grad_branch.astype(jnp.bfloat16), TP, axis=0, tiled=True)
        out_grad = jnp.einsum(
            "tc,td->cd", mixed_flat, shard_rows, preferred_element_type=jnp.float32
        )
        mixed_grad = jnp.einsum(
            "td,cd->tc", shard_rows, out_weight[block_index], preferred_element_type=jnp.float32
        ).astype(jnp.bfloat16)
        out_grad, mixed_grads = (out_grad, mixed_grad)
        grad_query, grad_key, grad_value = attention_backward(
            queries,
            key_all,
            value_all,
            log_total,
            mixed_grads.reshape(queries.shape),
            frame_only,
            score_scale,
        )
        raw_query_grad, query_gain_grad, query_offset_grad = jax.vjp(
            layer_norm, split[:, :, 0], head_gain[block_index, 0], head_offset[block_index, 0]
        )[1](grad_query)
        raw_key_grad, key_gain_grad, key_offset_grad = jax.vjp(
            layer_norm, split[:, :, 1], head_gain[block_index, 1], head_offset[block_index, 1]
        )[1](grad_key)
        projected_grad = (
            jnp.stack([raw_query_grad, raw_key_grad, grad_value], axis=2)
            .reshape(total_rows, -1)
            .astype(jnp.bfloat16)
        )
        qkv_weight_grad = jnp.einsum(
            "td,tc->dc", gathered, projected_grad, preferred_element_type=jnp.float32
        )
        qkv_bias_grad = jnp.sum(projected_grad.astype(jnp.float32), axis=0)
        normed_grad = lax.psum_scatter(
            jnp.einsum(
                "tc,dc->td",
                projected_grad,
                qkv_weight[block_index],
                preferred_element_type=jnp.float32,
            ).astype(jnp.bfloat16),
            TP,
            scatter_dimension=0,
            tiled=True,
        ).astype(jnp.float32)
        hidden_grad, gain_grad_zero, offset_grad_zero = jax.vjp(
            layer_norm, hidden, gains[0], offsets[0]
        )[1](normed_grad)
        hidden_grad = hidden_grad + middle_grad
        large_grads = (
            qkv_weight_grad,
            qkv_bias_grad,
            out_grad,
            up_weight_grad,
            up_bias_grad,
            down_grad,
        )
        small_grads = (
            jnp.stack([gain_grad_zero, gain_grad_one, gain_grad_two, gain_grad_three]),
            jnp.stack([offset_grad_zero, offset_grad_one, offset_grad_two, offset_grad_three]),
            jnp.stack([query_gain_grad, key_gain_grad]),
            jnp.stack([query_offset_grad, key_offset_grad]),
        )
        return (hidden_grad, large_grads, small_grads)

    hidden = frames.astype(jnp.float32)
    kept_states = []
    for block_index in range(2):
        forward_frame_only = block_index == 0
        forward_gains = norm_gain[block_index]
        forward_offsets = norm_offset[block_index]
        normed = layer_norm(hidden, forward_gains[0], forward_offsets[0]).astype(jnp.bfloat16)
        forward_gathered = lax.all_gather(normed, TP, axis=0, tiled=True)
        projected = jnp.dot(
            forward_gathered, qkv_weight[block_index], preferred_element_type=jnp.float32
        )
        projected = projected + qkv_bias[block_index].astype(jnp.float32)
        forward_total_rows = projected.shape[0]
        forward_split = projected.reshape(forward_total_rows, -1, 3, HD)
        forward_queries = layer_norm(
            forward_split[:, :, 0], head_gain[block_index, 0], head_offset[block_index, 0]
        ).astype(jnp.bfloat16)
        forward_key_all = layer_norm(
            forward_split[:, :, 1], head_gain[block_index, 1], head_offset[block_index, 1]
        ).astype(jnp.bfloat16)
        forward_value_all = forward_split[:, :, 2].astype(jnp.bfloat16)
        mixed, forward_log_total = attention_forward(
            forward_queries, forward_key_all, forward_value_all, forward_frame_only, score_scale
        )
        forward_mixed_flat = mixed.reshape(forward_total_rows, -1).astype(jnp.bfloat16)
        forward_branch = (
            lax.psum_scatter(
                jnp.dot(
                    forward_mixed_flat, out_weight[block_index], preferred_element_type=jnp.float32
                ).astype(jnp.bfloat16),
                TP,
                scatter_dimension=0,
                tiled=True,
            ).astype(jnp.float32)
            + forward_offsets[2]
        )
        forward_middle = hidden + forward_gains[2] * forward_branch
        second = layer_norm(forward_middle, forward_gains[1], forward_offsets[1]).astype(
            jnp.bfloat16
        )
        forward_gathered_two = lax.all_gather(second, TP, axis=0, tiled=True)
        forward_hidden_up = jnp.dot(
            forward_gathered_two, up_weight[block_index], preferred_element_type=jnp.float32
        )
        forward_hidden_up = forward_hidden_up + up_bias[block_index].astype(jnp.float32)
        forward_activated = exact_gelu(forward_hidden_up).astype(jnp.bfloat16)
        forward_branch_two = (
            lax.psum_scatter(
                jnp.dot(
                    forward_activated, down_weight[block_index], preferred_element_type=jnp.float32
                ).astype(jnp.bfloat16),
                TP,
                scatter_dimension=0,
                tiled=True,
            ).astype(jnp.float32)
            + forward_offsets[3]
        )
        result = forward_middle + forward_gains[3] * forward_branch_two
        forward_saved = (
            hidden,
            forward_gathered,
            forward_split,
            forward_queries,
            forward_key_all,
            forward_value_all,
            forward_log_total,
            forward_mixed_flat,
            forward_branch,
            forward_middle,
            forward_gathered_two,
            forward_hidden_up,
            forward_activated,
            forward_branch_two,
        )
        hidden = result
        saved = forward_saved
        kept_states.append(saved)
    layer_out = exchange(hidden.astype(jnp.bfloat16))[None]
    grad_hidden = cotangent.astype(jnp.float32) * weighting[:, None]
    grad_hidden, large_one, small_one = backward_block(grad_hidden, 1, False, kept_states[1])
    grad_hidden, large_zero, small_zero = backward_block(grad_hidden, 0, True, kept_states[0])
    input_grad = exchange(grad_hidden.astype(jnp.bfloat16))[None]

    def over_scenes(grads):
        shapes = [grad.shape for grad in grads]
        parts = lax.axis_size("sy")
        flat = [grad.astype(jnp.bfloat16).reshape(parts, -1) for grad in grads]
        sizes = [part.shape[1] for part in flat]
        joined = jnp.concatenate(flat, axis=1)
        share = lax.psum_scatter(joined, "sy", scatter_dimension=0, tiled=True)
        share = lax.psum(share, "h")
        whole = exchange(lax.all_gather(share, "sy", axis=0, tiled=True))
        found = []
        start = 0
        for shape, size in zip(shapes, sizes):
            found.append(whole[:, start : start + size].reshape(shape).astype(jnp.float32))
            start += size
        return found

    summed_one = over_scenes(large_one)
    summed_zero = over_scenes(large_zero)
    summed = [jnp.stack(pair) for pair in zip(summed_zero, summed_one)]
    small = jax.tree.map(lambda first, later: jnp.stack([first, later]), small_zero, small_one)
    summed = tuple(summed) + tuple(lax.psum(small, ("sy", "c", "h", "r")))
    return (
        layer_out,
        input_grad,
        summed[0],
        summed[1],
        summed[2],
        summed[3],
        summed[4],
        summed[5],
        summed[6],
        summed[7],
        summed[8],
        summed[9],
    )


def solution(mesh):
    scenes, shards = mesh.shape["scene"], mesh.shape["tp"]
    if (scenes, shards) == (4, 8):
        body, sizes, axes, tp = square_body, (2, 2, 2, 2, 2), AXES, ("h", "zl", "x")
    else:
        body, sizes, axes, tp = any_body, (scenes // 2, 2, 2, shards // 2), ("sy", "c", "h", "r"), ("h", "r")
    scene = ("sy", "c")
    return jax.shard_map(
        body,
        mesh=jax.sharding.Mesh(mesh.devices.reshape(sizes), axes),
        in_specs=(
            P(scene, tp, None),
            P(None, None, tp),
            P(None, tp),
            P(None, tp, None),
            P(None, None, tp),
            P(None, tp),
            P(None, tp, None),
            P(),
            P(),
            P(),
            P(),
            P(scene, tp, None),
            P(scene, tp),
            P(scene),
        ),
        out_specs=(
            P(scene, tp, None),
            P(scene, tp, None),
            P(None, None, tp),
            P(None, tp),
            P(None, tp, None),
            P(None, None, tp),
            P(None, tp),
            P(None, tp, None),
            P(),
            P(),
            P(),
            P(),
        ),
        check_vma=False,
    )
```

```python
import functools
import types

import jax
import jax.numpy as jnp
from jax import lax
from jax.experimental import pallas as pl
from jax.experimental.pallas import tpu as pltpu
from jax.sharding import PartitionSpec as P

HD = 64
QMAX = 512
FRAME_TOK = 1024
EPSILON = 1e-06
BF = jnp.bfloat16
F32 = jnp.float32
MESH = pl.DeviceIdType.MESH
DMA = pltpu.SemaphoreType.DMA
VMEM_LIMIT = 63 * 1024 * 1024

AXES = ("sy", "c", "h", "zl", "x")


def dot(left, right):
    return lax.dot_general(left, right, (((1,), (0,)), ((), ())), preferred_element_type=F32)


def dot_rt(left, right):
    return lax.dot_general(left, right, (((1,), (1,)), ((), ())), preferred_element_type=F32)


def dot_lt(left, right):
    return lax.dot_general(left, right, (((0,), (0,)), ((), ())), preferred_element_type=F32)


def dot_fine(left, right):
    high = left.astype(BF)
    return dot(high, right) + dot((left - high.astype(F32)).astype(BF), right)


def remote(source, target, send, recv, device):
    return pltpu.make_async_remote_copy(
        src_ref=source, dst_ref=target, send_sem=send, recv_sem=recv, device_id=device, device_id_type=MESH
    )


class Spot:
    def __init__(self):
        self.sy, self.c, self.h, self.zl, self.x = (lax.axis_index(name) for name in AXES)
        self.over_x = dict(x=1 - self.x)
        self.over_z = dict(zl=1 - self.zl)
        self.core = dict(c=1 - self.c)
        self.over_y = dict(sy=1 - self.sy)
        self.over_h = dict(h=1 - self.h)
        self.partner = dict(c=1 - self.c, h=1 - self.h)
        self.home = self.c == self.h
        self.away = self.c != self.h

    def greet(self, *devices):
        barrier = pltpu.get_barrier_semaphore()
        for device in devices:
            pl.semaphore_signal(barrier, inc=1, device_id=device, device_id_type=MESH)
        pl.semaphore_wait(barrier, len(devices))

    def slot(self, core, step):
        zl = lax.rem(self.zl + step // 2, 2)
        x = lax.rem(self.x + step % 2, 2)
        return core * 4 + zl * 2 + x

    def part(self, size, own=True, piece=0, pieces=1):
        half = size // 2
        rows = half // pieces
        return pl.ds(pl.multiple_of((self.sy if own else 1 - self.sy) * half + piece * rows, rows), rows)


class Gather:
    @staticmethod
    def scratch(rows, width):
        return [pltpu.VMEM((8, rows, width), BF), DMA((2, 6)), DMA((2, 6)), DMA((2, 4)), DMA((2, 4))]

    def __init__(self, spot, refs):
        self.spot = spot
        self.held, self.send, self.recv, self.core_send, self.core_recv = refs
        self.rows = self.held.shape[1] // 2

    def link(self, stream, step, part, number, device):
        half = self.rows // 2
        start = pl.multiple_of(stream * self.rows + part * half, half)
        ref = self.held.at[self.spot.slot(self.spot.c, step), pl.ds(start, half)]
        return remote(ref, ref, self.send.at[stream, number], self.recv.at[stream, number], device)

    def x_first(self, stream):
        return self.link(stream, 0, 0, 0, self.spot.over_x)

    def x_later(self, stream):
        return self.link(stream, 0, 1, 1, self.spot.over_x)

    def z_later(self, stream):
        return self.link(stream, 0, 0, 2, self.spot.over_z)

    def z_first(self, stream):
        return self.link(stream, 0, 1, 3, self.spot.over_z)

    def z_relay(self, stream):
        return self.link(stream, 1, 0, 4, self.spot.over_z)

    def x_relay(self, stream):
        return self.link(stream, 2, 1, 5, self.spot.over_x)

    def core_copy(self, stream, step):
        ref = self.held.at[self.spot.slot(self.spot.c, step), self.span(stream)]
        return remote(
            ref, ref, self.core_send.at[stream, step], self.core_recv.at[stream, step], self.spot.core
        )

    def span(self, stream):
        return pl.ds(pl.multiple_of(stream * self.rows, self.rows), self.rows)

    def part(self, slot, stream):
        return self.held[slot, self.span(stream)]

    def put(self, stream, values):
        self.held[self.spot.slot(self.spot.c, 0), self.span(stream)] = values
        self.x_first(stream).start()
        self.z_first(stream).start()
        self.core_copy(stream, 0).start()
        self.z_later(stream).start()
        self.x_later(stream).start()

    def pass_on(self, stream):
        self.x_first(stream).wait_recv()
        self.z_relay(stream).start()
        self.z_first(stream).wait_recv()
        self.x_relay(stream).start()

    def arrive(self, stream, step):
        pl.when(step == 1)(lambda: self.x_later(stream).wait_recv())
        pl.when(step == 2)(lambda: self.z_later(stream).wait_recv())

        @pl.when(step == 3)
        def _():
            self.z_relay(stream).wait_recv()
            self.x_relay(stream).wait_recv()

        pl.when(step > 0)(lambda: self.core_copy(stream, step).start())

    def arrive_core(self, stream, step):
        self.core_copy(stream, step).wait_recv()

    def finish(self):
        for stream in range(2):
            for copy in (self.x_first, self.x_later, self.z_first, self.z_later, self.z_relay, self.x_relay):
                copy(stream).wait_send()
            for step in range(4):
                self.core_copy(stream, step).wait_send()

    def consume(self, use, passed=0, before=None):
        def visit(index, carry):
            stream, step = index // 4, lax.rem(index, 4)
            if before is not None:
                before(index)
            self.arrive(stream, step)
            use(self.spot.slot(self.spot.c, step), stream)
            pl.when((index >= passed) & (index < 2))(lambda: self.pass_on(index))
            self.arrive_core(stream, step)
            use(self.spot.slot(1 - self.spot.c, step), stream)
            return carry

        lax.fori_loop(0, 8, visit, 0)


class Scatter:
    @staticmethod
    def local(rows, width):
        return [
            pltpu.VMEM((4, rows, width), BF),
            pltpu.VMEM((4, rows, width), BF),
            pltpu.VMEM((2, 2, rows // 4, width), BF),
        ]

    @staticmethod
    def scratch(rows, width):
        return [
            pltpu.VMEM((4, rows, width), BF),
            pltpu.VMEM((2, 6, rows // 4, width), BF),
            DMA((2, 4)),
            DMA((2, 4)),
            DMA((2, 6)),
            DMA((2, 6)),
        ]

    def __init__(self, spot, local, refs):
        self.spot = spot
        self.for_core, self.ready, self.relayed = local
        self.from_core, self.landed, self.core_send, self.core_recv, self.send, self.recv = refs
        self.rows = self.for_core.shape[1] // 2

    def span(self, stream):
        return pl.ds(pl.multiple_of(stream * self.rows, self.rows), self.rows)

    def half(self, stream, part):
        half = self.rows // 2
        return pl.ds(pl.multiple_of(stream * self.rows + part * half, half), half)

    def link(self, source, stream, number, device):
        return remote(
            source, self.landed.at[stream, number], self.send.at[stream, number], self.recv.at[stream, number], device
        )

    def x_near(self, stream):
        return self.link(self.ready.at[1, self.half(stream, 0)], stream, 0, self.spot.over_x)

    def x_far(self, stream):
        return self.link(self.ready.at[3, self.half(stream, 0)], stream, 1, self.spot.over_x)

    def z_near(self, stream):
        return self.link(self.ready.at[2, self.half(stream, 1)], stream, 2, self.spot.over_z)

    def z_far(self, stream):
        return self.link(self.ready.at[3, self.half(stream, 1)], stream, 3, self.spot.over_z)

    def z_relay(self, stream):
        return self.link(self.relayed.at[stream, 0], stream, 4, self.spot.over_z)

    def x_relay(self, stream):
        return self.link(self.relayed.at[stream, 1], stream, 5, self.spot.over_x)

    def core_copy(self, stream, step):
        span = self.span(stream)
        return remote(
            self.for_core.at[step, span],
            self.from_core.at[step, span],
            self.core_send.at[stream, step],
            self.core_recv.at[stream, step],
            self.spot.core,
        )

    def put_other(self, stream, step, values):
        self.for_core[step, self.span(stream)] = values.astype(BF)
        self.core_copy(stream, step).start()

    def put_own(self, stream, step, values):
        self.ready[step, self.span(stream)] = values.astype(BF)

    def flush(self, stream, step):
        self.core_copy(stream, step).wait_recv()
        span = self.span(stream)
        total = self.ready[step, span].astype(F32) + self.from_core[step, span].astype(F32)
        self.ready[step, span] = total.astype(BF)

        pl.when(step == 1)(lambda: self.x_near(stream).start())
        pl.when(step == 2)(lambda: self.z_near(stream).start())

        @pl.when(step == 3)
        def _():
            self.x_far(stream).start()
            self.z_far(stream).start()

    def relay(self, stream):
        self.x_far(stream).wait_recv()
        mine = self.ready[2, self.half(stream, 0)].astype(F32)
        self.relayed[stream, 0] = (mine + self.landed[stream, 1].astype(F32)).astype(BF)
        self.z_relay(stream).start()
        self.z_far(stream).wait_recv()
        mine = self.ready[1, self.half(stream, 1)].astype(F32)
        self.relayed[stream, 1] = (mine + self.landed[stream, 3].astype(F32)).astype(BF)
        self.x_relay(stream).start()

    def result(self, stream):
        self.x_near(stream).wait_recv()
        self.z_near(stream).wait_recv()
        self.z_relay(stream).wait_recv()
        self.x_relay(stream).wait_recv()
        landed = lambda number: self.landed[stream, number].astype(F32)
        return self.ready[0, self.span(stream)].astype(F32) + jnp.concatenate(
            [landed(0) + landed(4), landed(2) + landed(5)], axis=0
        )

    def finish(self):
        for stream in range(2):
            for copy in (self.x_near, self.x_far, self.z_near, self.z_far, self.z_relay, self.x_relay):
                copy(stream).wait_send()
            for step in range(4):
                self.core_copy(stream, step).wait_send()

    def produce(self, term, before=None):
        spot = self.spot

        def visit(index, carry):
            stream, step = index // 4, 3 - lax.rem(index, 4)
            if before is not None:
                before(index)
            self.put_other(stream, step, term(spot.slot(1 - spot.c, step), stream))

            @pl.when(index > 0)
            def _():
                pl.when(index == 5)(lambda: self.relay(0))
                self.flush((index - 1) // 4, 3 - lax.rem(index - 1, 4))

            self.put_own(stream, step, term(spot.slot(spot.c, step), stream))
            return carry

        lax.fori_loop(0, 8, visit, 0)
        self.flush(1, 0)

    def produce_from(self, gather, term, passed=1):
        spot = self.spot

        def visit(index, carry):
            stream, step = index // 4, lax.rem(index, 4)
            gather.arrive(stream, step)
            self.put_own(stream, step, term(spot.slot(spot.c, step), stream))
            pl.when((index >= passed) & (index < 2))(lambda: gather.pass_on(index))
            gather.arrive_core(stream, step)
            self.put_other(stream, step, term(spot.slot(1 - spot.c, step), stream))

            @pl.when(index > 0)
            def _():
                pl.when(index == 6)(lambda: self.relay(0))
                self.flush((index - 1) // 4, lax.rem(index - 1, 4))

            return carry

        lax.fori_loop(0, 8, visit, 0)
        self.flush(1, 3)


class Swap:
    scratch = [DMA((2,))]

    def __init__(self, spot, source, target, refs):
        (sems,) = refs
        self.spot = spot
        self.local = pltpu.make_async_copy(source, target, sems.at[0])
        self.copy = remote(source, target, sems.at[0], sems.at[1], spot.partner)

    def start(self):
        pl.when(self.spot.home)(self.local.start)
        pl.when(self.spot.away)(self.copy.start)

    def arrive(self):
        pl.when(self.spot.home)(self.local.wait)
        pl.when(self.spot.away)(self.copy.wait_recv)

    def finish(self):
        pl.when(self.spot.away)(self.copy.wait_send)


class Move:
    scratch = [DMA((2, 4))]

    def __init__(self, spot, own, got, refs):
        (sems,) = refs
        self.spot, self.own, self.got = spot, own, got
        self.over, self.along = [], []
        for piece in range(2):
            rows = spot.part(got.shape[0], True, piece, 2)
            at = sems.at[piece]
            self.over.append(remote(own.at[rows], got.at[rows], at.at[0], at.at[1], spot.over_h))
            self.along.append(remote(got.at[rows], got.at[rows], at.at[2], at.at[3], spot.over_y))

    def start(self):
        @pl.when(self.spot.home)
        def _():
            for copy in self.over:
                copy.start()

    def relay(self, piece):
        @pl.when(self.spot.away)
        def _():
            self.over[piece].wait_recv()
            self.along[piece].start()

    def finish(self):
        @pl.when(self.spot.away)
        def _():
            for copy in self.along:
                copy.wait_recv()
                copy.wait_send()

        @pl.when(self.spot.home)
        def _():
            for copy in self.over:
                copy.wait_send()

    def pick(self, target, sem):
        copy = pltpu.make_async_copy(self.got, target, sem)
        pl.when(self.spot.home)(pltpu.make_async_copy(self.own, target, sem).start)
        pl.when(self.spot.away)(copy.start)
        return copy


class Total:
    @staticmethod
    def scratch(rows, width):
        half = pltpu.VMEM((rows // 2, width), BF)
        return [half, half, half, DMA((11,))]

    def __init__(self, spot, grad, whole, refs):
        self.landed, self.share, self.later_landed, sems = refs
        self.grad, self.spot = grad, spot
        size = grad.shape[0]
        mine, other = whole.at[spot.part(size)], whole.at[spot.part(size, False)]
        share = self.share
        self.first = remote(grad.at[spot.part(size, False)], self.landed, sems.at[0], sems.at[1], spot.over_y)
        self.over = remote(share, self.later_landed, sems.at[2], sems.at[3], spot.over_h)
        self.along = remote(share, mine, sems.at[4], sems.at[5], spot.over_y)
        self.near = remote(share, mine, sems.at[6], sems.at[7], spot.core)
        self.later = remote(other, other, sems.at[8], sems.at[9], spot.core)
        self.local = pltpu.make_async_copy(share, mine, sems.at[10])

    def start(self):
        self.first.start()

    def add(self):
        self.first.wait_recv()
        mine = self.grad[self.spot.part(self.grad.shape[0])]
        self.share[...] = (mine.astype(F32) + self.landed[...].astype(F32)).astype(BF)
        pl.when(self.spot.away)(self.over.start)

    def add_over(self):
        @pl.when(self.spot.home)
        def _():
            self.over.wait_recv()
            self.share[...] = (self.share[...].astype(F32) + self.later_landed[...].astype(F32)).astype(BF)
            self.along.start()
            self.near.start()
            self.local.start()

    def relay(self):
        @pl.when(self.spot.home)
        def _():
            self.along.wait_recv()
            self.later.start()

    def finish(self):
        self.first.wait_send()

        @pl.when(self.spot.home)
        def _():
            self.along.wait_send()
            self.near.wait_send()
            self.later.wait_send()
            self.local.wait()

        @pl.when(self.spot.away)
        def _():
            self.over.wait_send()
            self.near.wait_recv()
            self.later.wait_recv()


class SmallSum:
    @staticmethod
    def scratch(rows, width):
        return [pltpu.VMEM((5, rows, width), F32), DMA((5,)), DMA((5,))]

    def __init__(self, spot, total, refs):
        landed, send, recv = refs
        self.total, self.landed = total, landed
        self.copies = [
            remote(total, landed.at[number], send.at[number], recv.at[number], device)
            for number, device in enumerate((spot.core, spot.over_x, spot.over_z, spot.over_h, spot.over_y))
        ]

    def step(self, number):
        if number > 0:
            self.copies[number - 1].wait()
            self.total[...] += self.landed[number - 1]
        if number < 5:
            self.copies[number].start()


class QuickSum:
    @staticmethod
    def scratch(rows, width):
        return [pltpu.VMEM((8, rows, width), F32), pltpu.VMEM((4, rows, width), F32), DMA((10,)), DMA((10,))]

    def __init__(self, spot, total, refs):
        self.total = total
        self.near, self.far, send, recv = refs
        self.near_place = spot.c * 4 + spot.zl * 2 + spot.x
        self.far_place = spot.sy * 2 + spot.h
        self.near_copies, self.far_copies = [], []
        for number in range(1, 8):
            device = dict(c=spot.c, zl=spot.zl, x=spot.x)
            for bit, name in ((4, "c"), (2, "zl"), (1, "x")):
                if number & bit:
                    device[name] = 1 - device[name]
            target = self.near.at[self.near_place]
            self.near_copies.append(remote(total, target, send.at[number - 1], recv.at[number - 1], device))
        for number in range(1, 4):
            device = dict(sy=spot.sy, h=spot.h)
            for bit, name in ((2, "sy"), (1, "h")):
                if number & bit:
                    device[name] = 1 - device[name]
            target = self.far.at[self.far_place]
            self.far_copies.append(remote(total, target, send.at[number + 6], recv.at[number + 6], device))

    @staticmethod
    def partners(spot):
        flip = lambda **names: {name: 1 - getattr(spot, name) for name in names}
        return [
            flip(c=0, x=0), flip(c=0, zl=0), flip(zl=0, x=0), flip(c=0, zl=0, x=0), flip(sy=0, h=0),
        ]

    def start(self):
        self.near[self.near_place] = self.total[...]
        for copy in self.near_copies:
            copy.start()

    def step(self):
        for copy in self.near_copies:
            copy.wait()
        total = self.near[0]
        for place in range(1, 8):
            total += self.near[place]
        self.total[...] = total
        self.far[self.far_place] = total
        for copy in self.far_copies:
            copy.start()

    def end(self):
        for copy in self.far_copies:
            copy.wait()
        total = self.far[0]
        for place in range(1, 4):
            total += self.far[place]
        self.total[...] = total


def norm_parts(values):
    average = jnp.mean(values, axis=-1, keepdims=True)
    centered = values - average
    scale = lax.rsqrt(jnp.mean(centered * centered, axis=-1, keepdims=True) + EPSILON)
    return centered * scale, scale


def norm_back(grad, gain, normed, scale):
    scaled = grad * gain
    back = scale * (
        scaled
        - jnp.mean(scaled, axis=-1, keepdims=True)
        - normed * jnp.mean(scaled * normed, axis=-1, keepdims=True)
    )
    return back, jnp.sum(grad * normed, axis=0, keepdims=True), jnp.sum(grad, axis=0, keepdims=True)


def gelu_both(values):
    size = jnp.abs(values) * 0.7071067811865476
    bell = jnp.exp(-size * size)
    t = 1.0 / (1.0 + 0.3275911 * size)
    poly = t * (
        0.254829592 + t * (-0.284496736 + t * (1.421413741 + t * (-1.453152027 + t * 1.061405429)))
    )
    tail = 0.5 * poly * bell
    below = jnp.where(values < 0, tail, 1.0 - tail)
    return values * below, below + values * bell * 0.3989422804014327


def lanes_of_head(shape, head):
    lane = lax.broadcasted_iota(jnp.int32, shape, 1)
    return (lane < HD) if head == 0 else (lane >= HD)


def pack_queries_keys(projected):
    one, two, three = (projected[:, part * 2 * HD : (part + 1) * 2 * HD] for part in range(3))
    low = lanes_of_head(one.shape, 0)
    keys = pltpu.roll(jnp.where(low, three, one), HD, 1)
    return jnp.concatenate([jnp.where(low, one, two), keys], axis=1), jnp.where(low, two, three)


def unpack_queries_keys(queries, keys, values):
    low = lanes_of_head(queries.shape, 0)
    keys = pltpu.roll(keys, HD, 1)
    return jnp.where(low, queries, keys), jnp.where(low, values, queries), jnp.where(low, keys, values)


def averager(width):
    row = lax.broadcasted_iota(jnp.int32, (width, width), 0) // HD
    column = lax.broadcasted_iota(jnp.int32, (width, width), 1) // HD
    return jnp.where(row == column, 1.0 / HD, 0.0).astype(BF)


def project(k, block, gather, slot, stream):
    span = gather.span(stream)
    projected = dot(gather.part(slot, stream), k.qkv_weight[...]) + k.biases[block : block + 1, : 6 * HD]
    raw, values = pack_queries_keys(projected)
    k.raw[slot, span] = raw
    average = averager(4 * HD)
    centered = raw - dot_fine(raw, average)
    scale = lax.rsqrt(dot_fine(centered * centered, average) + EPSILON)
    gain, offset = k.head_gains[block : block + 1], k.head_offsets[block : block + 1]
    k.qk[slot, span] = (centered * scale * gain + offset).astype(BF)
    k.v[slot, span] = values.astype(BF)


def in_three(values):
    high = values.astype(BF)
    rest = values - high.astype(F32)
    middle = rest.astype(BF)
    return high.astype(F32), middle.astype(F32), (rest - middle.astype(F32)).astype(BF).astype(F32)


def beside(rows, values, head):
    lane = lax.broadcasted_iota(jnp.int32, rows.shape, 1)
    start = HD if head == 0 else 0
    high, middle, low = in_three(values)
    other = jnp.where(
        lane == start, high, jnp.where(lane == start + 1, middle, jnp.where(lane == start + 2, low, 0.0))
    )
    return jnp.where(lanes_of_head(rows.shape, head), rows.astype(F32), other).astype(BF)


def slice_attend(k, keys, start, size):
    rows = pl.ds(pl.multiple_of(start, size), size)
    span = pl.ds(pl.multiple_of(start // keys * keys, keys), keys)
    queries = k.qk_in[rows, : 2 * HD] * jnp.asarray(HD**-0.5, BF)
    low = lanes_of_head(queries.shape, 0)
    zeros = jnp.zeros_like(queries)
    mine = [jnp.where(low, queries, zeros), jnp.where(low, zeros, queries)]
    scores = dot_rt(jnp.concatenate(mine, axis=0), k.qk_in[span, 2 * HD :])
    largest = jnp.max(scores, axis=-1, keepdims=True)
    weights = jnp.exp(scores - largest)
    total = jnp.sum(weights, axis=-1, keepdims=True)
    found = dot(weights.astype(BF), k.v_in[span, :]) / total
    logs = largest + jnp.log(total)
    for head in range(2):
        k.query[head, rows] = beside(mine[head], logs[head * size : (head + 1) * size], head)
    both = jnp.where(low, found[:size], found[size:])
    k.exact[rows] = both
    k.mixed[rows] = both.astype(BF)


def first_kernel(k):
    spot = k.spot
    spot.greet(spot.over_x, spot.over_z, spot.core, spot.over_y, spot.over_h, spot.partner)
    gather = Gather(spot, k.gather)
    swaps = [
        Swap(spot, k.frames.at[0, gather.span(stream)], k.hidden.at[gather.span(stream)], k.swaps[stream])
        for stream in range(2)
    ]
    swaps.append(Swap(spot, k.own_biases, k.biases, k.swaps[2]))
    swaps[0].start()
    swaps[2].start()
    swaps[0].finish()
    swaps[1].start()
    for stream in range(2):
        swaps[stream].arrive()
        rows = k.hidden[gather.span(stream)].astype(F32)
        values = (norm_parts(rows)[0] * k.gains[0, 0:1] + k.offsets[0, 0:1]).astype(BF)
        if stream == 1:
            gather.pass_on(0)
        gather.put(stream, values)
    qkv, out, up = (
        Move(spot, own.at[0], got, refs)
        for own, got, refs in zip((k.qkv_own, k.out_own, k.up_own), (k.qkv_got, k.out_got, k.up_got), k.moves)
    )
    for move in (qkv, out, up):
        move.start()
    k.saves.hidden()
    gather.pass_on(1)
    qkv.relay(0)
    qkv.relay(1)
    gather.arrive(0, 1)
    qkv.finish()
    swaps[2].arrive()
    qkv.pick(k.qkv_weight, k.pick).wait()

    def visit(index, carry):
        stream, step = index // 4, lax.rem(index, 4)
        pl.when(index > 1)(lambda: gather.arrive(stream, step))
        project(k, 0, gather, spot.slot(spot.c, step), stream)
        gather.arrive_core(stream, step)
        project(k, 0, gather, spot.slot(1 - spot.c, step), stream)

        @pl.when(index == 6)
        def _():
            out.relay(0)
            out.relay(1)
            up.relay(0)

        return carry

    lax.fori_loop(0, 8, visit, 0)
    k.saves.gathered(gather.held)
    k.saves.raw()
    k.saves.qk()
    k.saves.v()
    up.relay(1)
    for swap in swaps[1:]:
        swap.finish()
    gather.finish()
    out.finish()
    up.finish()


def forward_kernel(is_last, k):
    spot = k.spot
    block = 1 if is_last else 0
    spot.greet(spot.over_x, spot.over_z, spot.core, spot.over_y, spot.over_h, spot.partner)
    down = Move(spot, k.down_own.at[block], k.down_got, k.moves[0])
    if is_last:
        up = Move(spot, k.up_own.at[1], k.up_got, k.moves[1])
        up.start()
        others = []
    else:
        down.start()
        others = [Move(spot, k.qkv_own.at[1], k.qkv_got, k.moves[1]), Move(spot, k.out_own.at[1], k.out_got, k.moves[2])]
    first, gather, later = Scatter(spot, k.local, k.one), Gather(spot, k.gather), Scatter(spot, k.local, k.two)
    rows_of = gather.span
    size = gather.held.shape[1]
    keys = k.mixed.shape[0] if is_last else FRAME_TOK
    k.loads.qk_in.wait()
    k.loads.v_in.wait()
    k.loads.out_weight.wait()

    def term_attention(slot, stream):
        start = pl.multiple_of(slot * size + stream * (size // 2), size // 2)
        slice_attend(k, keys, start, size // 2)
        return dot(k.mixed[pl.ds(start, size // 2)], k.out_weight[...])

    def before(index):
        if is_last:

            @pl.when(index == 6)
            def _():
                up.relay(0)
                up.relay(1)
                down.start()

        else:
            pl.when(index == 6)(lambda: down.relay(0))

    first.produce(term_attention, before)
    k.saves.exact()
    k.saves.query()
    k.loads.hidden.wait()
    for stream in range(2):
        rows = rows_of(stream)
        branch = first.result(stream) + k.offsets[block, 2:3]
        middle = k.hidden[rows].astype(F32) + k.gains[block, 2:3] * branch
        k.branch[rows] = branch
        k.middle[rows] = middle
        gather.put(stream, (norm_parts(middle)[0] * k.gains[block, 1:2] + k.offsets[block, 1:2]).astype(BF))
        if stream == 0:
            first.relay(1)
            if is_last:
                down.relay(0)
            else:
                down.relay(1)
            gather.pass_on(0)
    if is_last:
        down.relay(1)
        up.finish()
        up_pick = up.pick(k.up_weight, k.pick.at[0])
    if is_last:
        cotangent = Swap(spot, k.cotangent.at[0], k.cotangent_here, k.swaps[0])
        weighting = Swap(spot, k.weighting, k.weighting_here, k.swaps[1])
        cotangent.start()
        weighting.start()
    for move in others:
        move.start()
    k.saves.branch()
    k.saves.middle()
    first.finish()
    gather.pass_on(1)
    down.finish()
    down_pick = down.pick(k.down_weight, k.pick.at[1])
    if is_last:
        up_pick.wait()
    else:
        k.loads.up_weight.wait()
    down_pick.wait()

    def term(slot, stream):
        bias = k.biases[block : block + 1, 6 * HD :]
        activated, slope = gelu_both(dot(gather.part(slot, stream), k.up_weight[...]) + bias)
        activated = activated.astype(BF)
        k.activated[slot, rows_of(stream)] = activated
        k.slope[slot, rows_of(stream)] = slope.astype(BF)
        return dot(activated, k.down_weight[...])

    later.produce_from(gather, term, 2)
    k.saves.second(gather.held)
    k.saves.activated()
    k.saves.slope()
    if not is_last:
        onward = Gather(spot, k.gather_next)
    for stream in range(2):
        rows = rows_of(stream)
        branch = later.result(stream) + k.offsets[block, 3:4]
        state = k.middle[rows] + k.gains[block, 3:4] * branch
        k.branch_two[rows] = branch
        k.state[rows] = state.astype(k.state.dtype)
        if not is_last:
            onward.put(stream, (norm_parts(state)[0] * k.gains[1, 0:1] + k.offsets[1, 0:1]).astype(BF))
        if stream == 0:
            later.relay(1)
            if not is_last:
                onward.pass_on(0)
            for move in others:
                move.relay(0)
                move.relay(1)
    k.saves.branch_two()
    k.saves.state()
    gather.finish()
    later.finish()
    if is_last:
        for swap in (cotangent, weighting):
            swap.arrive()
            swap.finish()
        return
    for move in others:
        move.finish()
    others[0].pick(k.qkv_weight, k.pick.at[0]).wait()
    onward.consume(functools.partial(project, k, 1, onward), 1)
    k.saves.gathered(onward.held)
    k.saves.raw()
    k.saves.qk()
    k.saves.v()
    onward.finish()


def wide(ref):
    return ref[...].reshape(ref.shape[0] * ref.shape[1], ref.shape[2])


def with_bias_row(grad_ref, weight_grad, bias_grad):
    size = weight_grad.shape[0]
    row = lax.broadcasted_iota(jnp.int32, (grad_ref.shape[0] - size, grad_ref.shape[1]), 0)
    grad_ref[:size] = weight_grad.astype(BF)
    grad_ref[size:] = jnp.where(row == 0, bias_grad, 0.0).astype(BF)


def pieces_of(ref):
    cut = ref.shape[0] // 64 * 32
    return pl.ds(0, cut), pl.ds(cut, ref.shape[0] - cut)


def qkv_weight_grad(k, gathered):
    rows = wide(k.above_qkv)
    with_bias_row(k.qkv_grad, dot_lt(wide(gathered), rows), jnp.sum(rows.astype(F32), axis=0, keepdims=True))


def prepare_keys(k, rows):
    shape = (rows.size, 2 * HD)
    lane = lax.broadcasted_iota(jnp.int32, shape, 1)
    for head in range(2):
        own = lanes_of_head(shape, head)
        ones = jnp.where(lane < (HD if head == 0 else 0) + 3, -1.0, 0.0)
        k.key_in[head, rows] = jnp.where(own, k.qk_in[rows, 2 * HD :].astype(F32), ones).astype(BF)
        k.value_in[head, rows] = jnp.where(own, k.v_in[rows].astype(F32), ones).astype(BF)


def slice_back(k, keys, block_keys, start, size, grad):
    width = 2 * HD
    rows = pl.ds(pl.multiple_of(start, size), size)
    row = lax.broadcasted_iota(jnp.int32, (width, width), 0) // HD
    column = lax.broadcasted_iota(jnp.int32, (width, width), 1) // HD
    swap_sum = jnp.where(row != column, 1.0, 0.0).astype(BF)
    delta = dot_fine(grad * k.exact[rows], swap_sum)
    lane = lax.broadcasted_iota(jnp.int32, (size, width), 1)
    high, middle, low = in_three(delta)
    for head in range(2):
        lead = HD if head == 0 else 0
        other = jnp.where(
            lane == lead, high, jnp.where(lane == lead + 1, middle, jnp.where(lane == lead + 2, low, 0.0))
        )
        k.grad_in[head] = jnp.where(lanes_of_head((size, width), head), grad, other).astype(BF)
    k.query_grad[...] = jnp.zeros_like(k.query_grad)
    first = start // keys * keys

    def visit(index, carry):
        key_rows = pl.ds(pl.multiple_of(first + index * block_keys, block_keys), block_keys)
        for head in range(2):
            own = lanes_of_head((size, width), head)
            own_keys = lanes_of_head((block_keys, width), head)
            query = k.query[head, rows]
            grad_rows = k.grad_in[head]
            key = k.key_in[head, key_rows]
            probs = jnp.exp(dot_rt(key, query))
            back = (probs * dot_rt(k.value_in[head, key_rows], grad_rows)).astype(BF)
            zeros = jnp.zeros((size, width), BF)
            k.grads[key_rows, 2 * width :] += dot(probs.astype(BF), jnp.where(own, grad_rows, zeros))
            k.grads[key_rows, width : 2 * width] += dot(back, jnp.where(own, query, zeros))
            k.query_grad[...] += dot_lt(back, jnp.where(own_keys, key, jnp.zeros((block_keys, width), BF)))
        return carry

    lax.fori_loop(0, keys // block_keys, visit, 0)
    k.grads[rows, :width] = k.query_grad[...]


def leave_heads(k, level, rows, target):
    width = 2 * HD
    average = averager(2 * width)
    values = k.raw_in[rows]
    centered = values - dot_fine(values, average)
    scale = lax.rsqrt(dot_fine(centered * centered, average) + EPSILON)
    normed = centered * scale
    lane = lax.broadcasted_iota(jnp.int32, normed.shape, 1)
    found = k.grads[rows, : 2 * width] * jnp.where(lane < width, HD**-0.5, 1.0)
    k.head_small[0:1] += jnp.sum(found * normed, axis=0, keepdims=True)
    k.head_small[1:2] += jnp.sum(found, axis=0, keepdims=True)
    scaled = found * k.head_gains[level : level + 1]
    back = scale * (scaled - dot_fine(scaled, average) - normed * dot_fine(scaled * normed, average))
    parts = unpack_queries_keys(back[:, :width], back[:, width:], k.grads[rows, 2 * width :])
    for number, part in enumerate(parts):
        target[:, number * width : (number + 1) * width] = part.astype(BF)


def backward_kernel(is_first, k):
    spot = k.spot
    block = 1 if is_first else 0
    spot.greet(spot.over_x, spot.over_z, spot.core, spot.over_y, spot.over_h, *((spot.partner,) if is_first else ()))
    gather, scatter, onward = Gather(spot, k.gather), Scatter(spot, k.local, k.one), Gather(spot, k.gather_next)
    rows_of = gather.span
    size = gather.held.shape[1]
    tokens = 8 * size
    keys = tokens if is_first else FRAME_TOK
    sums = [
        Total(spot, grad.at[rows], whole.at[rows], refs)
        for (grad, whole), pieces in (
            ((k.down_grad, k.down_whole), zip(pieces_of(k.down_grad), k.down_total)),
            ((k.up_grad, k.up_whole), zip(pieces_of(k.up_grad), k.up_total)),
        )
        for rows, refs in pieces
    ]
    k.small[...] = jnp.zeros_like(k.small)
    if is_first:
        layer = Swap(spot, k.state, k.layer_out, k.swap)
        k.loads.cotangent.wait()
    else:
        above = Scatter(spot, k.local, k.two)
        qkv = Total(spot, k.qkv_grad, k.qkv_whole, k.qkv_total)
        out = Total(spot, k.out_grad_in, k.out_whole, k.out_total)
        out.start()
        k.loads.above_qkv.wait()
        k.loads.qkv_weight.wait()
        above.produce(lambda slot, stream: dot_rt(k.above_qkv[slot, rows_of(stream)], k.qkv_weight[...]))
        gathered = pltpu.make_async_copy(k.gathered, k.shared, k.pick.at[0])
        gathered.start()
        out.add()
        gathered.wait()
        qkv_weight_grad(k, k.shared)
        qkv.start()
        k.loads.above_hidden.wait()
        k.loads.above_middle_grad.wait()
    k.loads.branch_two.wait()
    for stream in range(2):
        rows = rows_of(stream)
        if is_first:
            grad = k.cotangent[rows].astype(F32) * k.weighting[rows, 0:1]
        else:
            normed, scale = norm_parts(k.above_hidden[rows])
            grad, gain_term, offset_term = norm_back(above.result(stream), k.gains[1, 0:1], normed, scale)
            k.small[6:7] += gain_term
            k.small[7:8] += offset_term
            grad = grad + k.above_middle_grad[rows]
        k.grad_rows[rows] = grad
        scaled = k.gains[block, 3:4] * grad
        gather.put(stream, scaled.astype(BF))
        k.small[0:1] += jnp.sum(grad * k.branch_two[rows], axis=0, keepdims=True)
        k.small[1:2] += jnp.sum(scaled, axis=0, keepdims=True)
        if stream == 0:
            if not is_first:
                above.relay(1)
            gather.pass_on(0)
    second = pltpu.make_async_copy(k.second, k.shared, k.pick.at[1])
    second.start()
    if is_first:
        middle_rows, branch_rows, fetched = k.middle, k.branch, [k.loads.middle, k.loads.branch]
    else:
        middle_rows, branch_rows = k.above_hidden, k.above_middle_grad
        fetched = [
            pltpu.make_async_copy(k.middle, middle_rows, k.pick.at[2]),
            pltpu.make_async_copy(k.branch, branch_rows, k.pick.at[3]),
        ]
        for copy in fetched:
            copy.start()
    if is_first:
        layer.start()
    else:
        above.finish()
        qkv.add()
        out.add_over()
    k.loads.down_weight.wait()
    k.loads.up_weight.wait()
    k.loads.slope.wait()

    def term(slot, stream):
        slope = k.slope[slot, rows_of(stream)].astype(F32)
        up_rows = (dot_rt(gather.part(slot, stream), k.down_weight[...]) * slope).astype(BF)
        k.up_rows[slot, rows_of(stream)] = up_rows
        return dot_rt(up_rows, k.up_weight[...])

    scatter.produce_from(gather, term)
    gather.finish()
    for copy in fetched:
        copy.wait()
    k.loads.activated.wait()

    def down_piece(piece):
        cut = k.down_grad.shape[0] // 2
        lanes = slice(piece * cut, (piece + 1) * cut)
        rows = k.activated[:, :, lanes].reshape(tokens, cut)
        k.down_grad[lanes] = dot_lt(rows, wide(gather.held)).astype(BF)
        sums[piece].start()

    def up_piece(piece):
        cut = k.shared.shape[2] // 2
        lanes = slice(piece * cut, (piece + 1) * cut)
        rows = k.shared[:, :, lanes].reshape(tokens, cut)
        k.up_grad[lanes] = dot_lt(rows, wide(k.up_rows)).astype(BF)
        if piece == 1:
            total = jnp.sum(wide(k.up_rows).astype(F32), axis=0, keepdims=True)
            row = lax.broadcasted_iota(jnp.int32, (k.up_grad.shape[0] - 2 * cut, k.up_grad.shape[1]), 0)
            k.up_grad[2 * cut :] = jnp.where(row == 0, total, 0.0).astype(BF)
        sums[2 + piece].start()

    def leave_rows(stream):
        rows = rows_of(stream)
        normed, scale = norm_parts(middle_rows[rows])
        grad, gain_term, offset_term = norm_back(scatter.result(stream), k.gains[block, 1:2], normed, scale)
        grad = grad + k.grad_rows[rows]
        k.middle_grad[rows] = grad
        scaled = k.gains[block, 2:3] * grad
        onward.put(stream, scaled.astype(BF))
        k.small[2:3] += gain_term
        k.small[3:4] += offset_term
        k.small[4:5] += jnp.sum(grad * branch_rows[rows], axis=0, keepdims=True)
        k.small[5:6] += jnp.sum(scaled, axis=0, keepdims=True)

    down_piece(0)
    scatter.relay(1)
    leave_rows(0)
    down_piece(1)
    second.wait()
    up_piece(0)
    up_piece(1)
    onward.pass_on(0)
    leave_rows(1)
    if not is_first:
        qkv.add_over()
        out.relay()
    k.saves.middle_grad()
    if not is_first:
        early = SmallSum(spot, k.early, k.early_sum)
        lanes = 4 * HD
        k.early[0:8] = k.small_first[...]
        k.early[8:16] = k.small[...]
        k.early[16:24] = jnp.zeros_like(k.early[16:24])
        k.early[16:17, :lanes] = k.head_first[0:1]
        k.early[16:17, lanes : 2 * lanes] = k.head_first[1:2]
        early.step(0)
    scatter.finish()
    k.loads.out_weight.wait()
    k.loads.qk_in.wait()
    k.loads.v_in.wait()
    k.loads.query.wait()
    k.loads.exact.wait()
    k.grads[...] = jnp.zeros_like(k.grads)

    def prepare(index, carry):
        prepare_keys(k, pl.ds(pl.multiple_of(index * size, size), size))
        return carry

    lax.fori_loop(0, 8, prepare, 0)

    def use(slot):
        grad = dot_rt(onward.held[slot], k.out_weight[...]).astype(BF).astype(F32)
        slice_back(k, keys, 512, slot * size, size, grad)

    def visit(step, carry):
        for stream in range(2):
            onward.arrive(stream, step)
        use(spot.slot(spot.c, step))

        @pl.when(step == 0)
        def _():
            onward.pass_on(1)
            sums[0].add()
            sums[1].add()

        for stream in range(2):
            onward.arrive_core(stream, step)
        use(spot.slot(1 - spot.c, step))

        @pl.when(step == 0)
        def _():
            sums[2].add()
            if not is_first:
                qkv.relay()
                early.step(1)

        @pl.when(step == 1)
        def _():
            sums[3].add()
            sums[0].add_over()
            if not is_first:
                early.step(2)

        @pl.when(step == 2)
        def _():
            sums[1].add_over()
            if not is_first:
                early.step(3)

        @pl.when(step == 3)
        def _():
            sums[2].add_over()
            sums[0].relay()
            sums[1].relay()
            if not is_first:
                early.step(4)

        return carry

    lax.fori_loop(0, 4, visit, 0)
    k.out_grad[...] = dot_lt(k.exact[...].astype(BF), wide(onward.held)).astype(BF)
    k.saves.out_grad()
    k.loads.raw_in.wait()
    k.head_small[...] = jnp.zeros_like(k.head_small)
    qkv_rows = k.qkv_rows if is_first else k.above_qkv

    def leave(index, carry):
        leave_heads(k, block, pl.ds(pl.multiple_of(index * size, size), size), qkv_rows.at[index])
        return carry

    lax.fori_loop(0, 8, leave, 0)
    k.saves.grad_qkv(qkv_rows)
    onward.finish()
    if not is_first:
        early.step(5)
    sums[3].add_over()
    sums[2].relay()
    sums[3].relay()
    if is_first:
        layer.arrive()
        layer.finish()
    else:
        sums += [qkv, out]
    for total in sums:
        total.finish()


def last_kernel(k):
    spot = k.spot
    spot.greet(
        spot.over_x, spot.over_z, spot.core, spot.over_y, spot.over_h, spot.partner, *QuickSum.partners(spot)
    )
    scatter = Scatter(spot, k.local, k.one)
    out = Total(spot, k.out_grad_in, k.out_whole, k.out_total)
    pieces = pieces_of(k.qkv_grad)
    sums = [
        Total(spot, k.qkv_grad.at[rows], k.qkv_whole.at[rows], refs) for rows, refs in zip(pieces, k.qkv_total)
    ]
    out.start()
    k.loads.qkv_weight.wait()
    k.loads.above_qkv.wait()
    scatter.produce(lambda slot, stream: dot_rt(k.above_qkv[slot, scatter.span(stream)], k.qkv_weight[...]))
    late = QuickSum(spot, k.late, k.late_sum)
    k.loads.gathered.wait()
    rows = wide(k.above_qkv)
    cut = k.gathered.shape[2] // 2
    k.qkv_grad[:cut] = dot_lt(k.gathered[:, :, :cut].reshape(rows.shape[0], cut), rows).astype(BF)
    sums[0].start()
    scatter.relay(1)
    out.add()
    k.qkv_grad[cut : 2 * cut] = dot_lt(k.gathered[:, :, cut:].reshape(rows.shape[0], cut), rows).astype(BF)
    total = jnp.sum(rows.astype(F32), axis=0, keepdims=True)
    row = lax.broadcasted_iota(jnp.int32, (k.qkv_grad.shape[0] - 2 * cut, k.qkv_grad.shape[1]), 0)
    k.qkv_grad[2 * cut :] = jnp.where(row == 0, total, 0.0).astype(BF)
    sums[1].start()
    lanes = 4 * HD
    k.late[...] = jnp.zeros_like(k.late)
    k.late[2:3, :lanes] = k.head_later[0:1]
    k.late[2:3, lanes : 2 * lanes] = k.head_later[1:2]
    k.loads.hidden.wait()
    k.loads.middle_grad.wait()
    swaps = []
    for stream in range(2):
        span = scatter.span(stream)
        normed, scale = norm_parts(k.hidden[span].astype(F32))
        grad, gain_term, offset_term = norm_back(scatter.result(stream), k.gains[0, 0:1], normed, scale)
        k.late[0:1] += gain_term
        k.late[1:2] += offset_term
        k.grad_in[span] = (grad + k.middle_grad[span]).astype(BF)
        swap = Swap(spot, k.grad_in.at[span], k.input_grad.at[span], k.swaps[stream])
        swap.start()
        swaps.append(swap)
        if stream == 0:
            sums[0].add()
    late.start()
    sums[1].add()
    out.add_over()
    late.step()
    sums[0].add_over()
    out.relay()
    late.end()
    sums[1].add_over()
    sums[0].relay()
    sums[1].relay()
    for swap in swaps:
        swap.arrive()
        swap.finish()
    for part in sums:
        part.finish()
    out.finish()
    scatter.finish()


class Own:
    def __init__(self, own, level, got):
        self.own, self.level, self.got = own, level, got


class Load:
    def __init__(self, values):
        self.values = values


class Outside(Load):
    pass


INSIDE, APART, SAVED, TARGET = range(4)


def run(kernel, number, inputs, outputs, scratch):
    operands, in_specs = [], []
    vmem, outside = pl.BlockSpec(memory_space=pltpu.VMEM), pl.BlockSpec(memory_space=pl.ANY)
    loaded, places = {}, {}

    def give(values, spec):
        operands.append(values)
        in_specs.append(spec)
        return len(operands) - 1

    for key, value in inputs.items():
        if isinstance(value, Own):
            places[key] = (give(value.own, outside), give(value.got, outside))
            loaded[key] = value.own.shape[1:], value.own.dtype
        elif isinstance(value, Load):
            places[key] = give(value.values, outside)
            if not isinstance(value, Outside):
                loaded[key] = value.values.shape, value.values.dtype
        else:
            places[key] = give(value, vmem)
    out_keys = list(outputs)
    kinds = [outputs[key][1] for key in out_keys]
    saved = [key for key, kind in zip(out_keys, kinds) if kind in (SAVED, TARGET)]
    shapes = []

    def hold(item):
        if isinstance(item, list):
            return [hold(part) for part in item]
        shapes.append(item)
        return len(shapes) - 1

    layout = {key: hold(item) for key, item in scratch.items()}
    load_layout = {key: hold(pltpu.VMEM(size, kind)) for key, (size, kind) in loaded.items()}
    for key, kind in zip(out_keys, kinds):
        if kind == SAVED:
            layout[key] = hold(pltpu.VMEM(outputs[key][0].shape, outputs[key][0].dtype))
    load_at, save_at = hold(DMA((max(len(loaded), 1),))), hold(DMA((max(len(saved), 1),)))

    def whole(*refs):
        ins, rest = refs[: len(operands)], refs[len(operands) :]
        outs, held = rest[: len(out_keys)], rest[len(out_keys) :]

        def find(item):
            return [find(part) for part in item] if isinstance(item, list) else held[item]

        k = types.SimpleNamespace(**{key: find(item) for key, item in layout.items()})
        k.spot = Spot()
        saving = []
        loads, saves = {}, {}

        def saver(ref, target, sem):
            def save(source=ref):
                copy = pltpu.make_async_copy(source, target, sem)
                copy.start()
                saving.append(copy)

            return save

        for key, kind, out in zip(out_keys, kinds, outs):
            if kind in (INSIDE, APART):
                setattr(k, key, out)
            else:
                saves[key] = saver(getattr(k, key, None), out, held[save_at].at[saved.index(key)])
        for place, key in enumerate(loaded):
            target, sem = held[load_layout[key]], held[load_at].at[place]
            setattr(k, key, target)
            if isinstance(inputs[key], Own):
                own, got = (ins[at] for at in places[key])
                copy = pltpu.make_async_copy(got, target, sem)
                pl.when(k.spot.home)(pltpu.make_async_copy(own.at[inputs[key].level], target, sem).start)
                pl.when(k.spot.away)(copy.start)
            else:
                copy = pltpu.make_async_copy(ins[places[key]], target, sem)
                copy.start()
            loads[key] = copy
        for key in inputs:
            if key not in loaded:
                setattr(k, key, ins[places[key]])
        k.loads, k.saves = types.SimpleNamespace(**loads), types.SimpleNamespace(**saves)
        kernel(k)
        for copy in saving:
            copy.wait()

    found = pl.pallas_call(
        whole,
        name=getattr(kernel, "func", kernel).__name__,
        out_shape=[outputs[key][0] for key in out_keys],
        in_specs=in_specs,
        out_specs=[vmem if kind == INSIDE else outside for kind in kinds],
        scratch_shapes=shapes,
        compiler_params=pltpu.CompilerParams(
            collective_id=number, has_side_effects=True, vmem_limit_bytes=VMEM_LIMIT
        ),
    )(*operands)
    return types.SimpleNamespace(**dict(zip(out_keys, found)))


def shape(*sizes):
    return jax.ShapeDtypeStruct(sizes[:-1], sizes[-1])


def square_body(
    frames_in,
    qkv_weight,
    qkv_bias,
    out_weight,
    up_weight,
    up_bias,
    down_weight,
    norm_gain,
    norm_offset,
    head_gain,
    head_offset,
    cotangent,
    visible,
    query_count,
):
    rows, width = frames_in.shape[1:]
    tokens = 8 * rows
    inner = 2 * HD
    units = up_weight.shape[2]
    gather = Gather.scratch(rows, width)
    local, scatter = Scatter.local(rows, width), Scatter.scratch(rows, width)
    pad = 32

    def moved(weight):
        return shape(*weight.shape[1:], BF), APART

    def flat(values):
        return values.reshape(tokens, values.shape[2])

    biases = jnp.concatenate([qkv_bias, up_bias], axis=1).astype(F32)
    biases = jnp.pad(biases, ((0, 6), (0, 0)))
    weighting = visible[0].astype(F32) * (query_count[0].astype(F32) / QMAX)
    weighting = jnp.broadcast_to(weighting[:, None], (rows, 128))
    head_gains, head_offsets = (
        jnp.concatenate([pair[:, 0], pair[:, 0], pair[:, 1], pair[:, 1]], axis=1) for pair in (head_gain, head_offset)
    )
    norms = dict(gains=norm_gain, offsets=norm_offset)
    heads = dict(head_gains=head_gains, head_offsets=head_offsets)
    qkv_outs = dict(
        gathered=(shape(8, rows, width, BF), TARGET),
        raw=(shape(8, rows, 2 * inner, F32), SAVED),
        qk=(shape(8, rows, 2 * inner, BF), SAVED),
        v=(shape(8, rows, inner, BF), SAVED),
    )
    entry = run(
        first_kernel,
        0,
        dict(
            frames=Outside(frames_in),
            own_biases=biases,
            qkv_own=Outside(qkv_weight),
            out_own=Outside(out_weight),
            up_own=Outside(up_weight),
            **norms,
            **heads,
        ),
        dict(
            hidden=(shape(rows, width, BF), SAVED),
            biases=(shape(*biases.shape, F32), INSIDE),
            qkv_got=moved(qkv_weight),
            out_got=moved(out_weight),
            up_got=moved(up_weight),
            **qkv_outs,
        ),
        dict(
            gather=gather,
            swaps=[Swap.scratch] * 3,
            moves=[Move.scratch] * 3,
            qkv_weight=pltpu.VMEM(qkv_weight.shape[1:], BF),
            pick=DMA,
        ),
    )
    biases = entry.biases
    down_buffer = pltpu.VMEM(down_weight.shape[1:], BF)

    def forward(is_last, came, **extra):
        inputs, outputs, scratch = extra.pop("inputs"), extra.pop("outputs"), extra.pop("scratch")
        block = 1 if is_last else 0
        return run(
            functools.partial(forward_kernel, is_last),
            1 + block,
            dict(
                qk_in=Load(flat(came.qk)),
                v_in=Load(flat(came.v)),
                hidden=Load(came.hidden),
                down_own=Outside(down_weight),
                biases=biases,
                **norms,
                **inputs,
            ),
            dict(
                exact=(shape(tokens, inner, F32), SAVED),
                query=(shape(2, tokens, inner, BF), SAVED),
                branch=(shape(rows, width, F32), SAVED),
                middle=(shape(rows, width, F32), SAVED),
                second=(shape(8, rows, width, BF), TARGET),
                activated=(shape(8, rows, units, BF), SAVED),
                slope=(shape(8, rows, units, BF), SAVED),
                branch_two=(shape(rows, width, F32), SAVED),
                state=(shape(rows, width, BF if is_last else F32), SAVED),
                down_got=moved(down_weight),
                **outputs,
            ),
            dict(
                local=local,
                one=scatter,
                two=scatter,
                gather=gather,
                pick=DMA((2,)),
                mixed=pltpu.VMEM((tokens, inner), BF),
                down_weight=down_buffer,
                **scratch,
            ),
        )

    lower = forward(
        False,
        entry,
        inputs=dict(
            out_weight=Own(out_weight, 0, entry.out_got),
            up_weight=Own(up_weight, 0, entry.up_got),
            qkv_own=Outside(qkv_weight),
            out_own=Outside(out_weight),
            **heads,
        ),
        outputs=dict(qkv_got=moved(qkv_weight), out_got=moved(out_weight), **qkv_outs),
        scratch=dict(gather_next=gather, qkv_weight=pltpu.VMEM(qkv_weight.shape[1:], BF), moves=[Move.scratch] * 3),
    )
    between = types.SimpleNamespace(hidden=lower.state, **{key: getattr(lower, key) for key in qkv_outs})
    upper = forward(
        True,
        between,
        inputs=dict(
            out_weight=Own(out_weight, 1, lower.out_got),
            up_own=Outside(up_weight),
            cotangent=Outside(cotangent),
            weighting=weighting,
        ),
        outputs=dict(
            up_got=moved(up_weight),
            cotangent_here=(shape(rows, width, BF), APART),
            weighting_here=(shape(rows, 128, F32), APART),
        ),
        scratch=dict(
            swaps=[Swap.scratch] * 2, up_weight=pltpu.VMEM(up_weight.shape[1:], BF), moves=[Move.scratch] * 2
        ),
    )

    qkv_grad = pltpu.VMEM((width + pad, 3 * inner), BF)

    def in_pieces(size, lanes):
        cut = size // 64 * 32
        return [Total.scratch(cut, lanes), Total.scratch(size - cut, lanes)]

    qkv_whole = dict(qkv_whole=(shape(width + pad, 3 * inner, BF), APART))
    out_whole = dict(out_whole=(shape(inner, width, BF), APART))
    out_total = dict(out_total=Total.scratch(inner, width))

    def backward(is_first, came, kept, up_got, out_got, inputs, outputs, scratch):
        block = 1 if is_first else 0
        return run(
            functools.partial(backward_kernel, is_first),
            3 + block,
            dict(
                **inputs,
                branch_two=Load(kept.branch_two),
                down_weight=Own(down_weight, block, kept.down_got),
                up_weight=Own(up_weight, block, up_got),
                slope=Load(kept.slope),
                activated=Load(kept.activated),
                second=Outside(kept.second),
                out_weight=Own(out_weight, block, out_got),
                qk_in=Load(flat(came.qk)),
                v_in=Load(flat(came.v)),
                query=Load(kept.query),
                exact=Load(kept.exact),
                raw_in=Load(flat(came.raw)),
                gains=norm_gain,
                head_gains=head_gains,
            ),
            dict(
                middle_grad=(shape(rows, width, F32), SAVED),
                grad_qkv=(shape(8, rows, 3 * inner, BF), TARGET),
                out_grad=(shape(inner, width, BF), SAVED),
                down_whole=(shape(units, width, BF), APART),
                up_whole=(shape(width + pad, units, BF), APART),
                small=(shape(8, width, F32), INSIDE),
                head_small=(shape(2, 2 * inner, F32), INSIDE),
                **outputs,
            ),
            dict(
                local=local,
                one=scatter,
                gather=gather,
                gather_next=gather,
                up_rows=pltpu.VMEM((8, rows, units), BF),
                grad_rows=pltpu.VMEM((rows, width), F32),
                shared=pltpu.VMEM((8, rows, width), BF),
                pick=DMA((4,)),
                down_grad=pltpu.VMEM((units, width), BF),
                up_grad=pltpu.VMEM((width + pad, units), BF),
                down_total=in_pieces(units, width),
                up_total=in_pieces(width + pad, units),
                key_in=pltpu.VMEM((2, tokens, inner), BF),
                value_in=pltpu.VMEM((2, tokens, inner), BF),
                grad_in=pltpu.VMEM((2, rows, inner), BF),
                query_grad=pltpu.VMEM((rows, inner), F32),
                grads=pltpu.VMEM((tokens, 3 * inner), F32),
                **scratch,
            ),
        )

    upper_back = backward(
        True,
        between,
        upper,
        upper.up_got,
        lower.out_got,
        dict(
            cotangent=Load(upper.cotangent_here),
            weighting=upper.weighting_here,
            state=Outside(upper.state),
            middle=Load(upper.middle),
            branch=Load(upper.branch),
        ),
        dict(layer_out=(shape(rows, width, BF), APART)),
        dict(swap=Swap.scratch, qkv_rows=pltpu.VMEM((8, rows, 3 * inner), BF)),
    )
    lower_back = backward(
        False,
        entry,
        lower,
        entry.up_got,
        entry.out_got,
        dict(
            above_qkv=Load(upper_back.grad_qkv),
            qkv_weight=Own(qkv_weight, 1, lower.qkv_got),
            gathered=Outside(between.gathered),
            above_hidden=Load(between.hidden),
            above_middle_grad=Load(upper_back.middle_grad),
            out_grad_in=upper_back.out_grad,
            middle=Outside(lower.middle),
            branch=Outside(lower.branch),
            small_first=upper_back.small,
            head_first=upper_back.head_small,
        ),
        dict(early=(shape(24, width, F32), INSIDE), **qkv_whole, **out_whole),
        dict(
            early_sum=SmallSum.scratch(24, width),
            two=scatter,
            qkv_grad=qkv_grad, qkv_total=Total.scratch(width + pad, 3 * inner), **out_total),
    )
    last = run(
        last_kernel,
        5,
        dict(
            above_qkv=Load(lower_back.grad_qkv),
            qkv_weight=Own(qkv_weight, 0, entry.qkv_got),
            gathered=Load(entry.gathered),
            hidden=Load(entry.hidden),
            middle_grad=Load(lower_back.middle_grad),
            out_grad_in=lower_back.out_grad,
            gains=norm_gain,
            head_later=lower_back.head_small,
        ),
        dict(
            input_grad=(shape(rows, width, BF), APART),
            late=(shape(8, width, F32), INSIDE),
            **qkv_whole,
            **out_whole,
        ),
        dict(
            local=local,
            one=scatter,
            grad_in=pltpu.VMEM((rows, width), BF),
            swaps=[Swap.scratch] * 2,
            late_sum=QuickSum.scratch(8, width),
            qkv_grad=qkv_grad,
            qkv_total=in_pieces(width + pad, 3 * inner),
            **out_total,
        ),
    )
    early, late = lower_back.early, last.late
    gains = [late[0], early[10], early[12], early[8], early[14], early[2], early[4], early[0]]
    offsets = [late[1], early[11], early[13], early[9], early[15], early[3], early[5], early[1]]
    head_sums = jnp.stack([late[2, : 8 * HD], early[16, : 8 * HD]]).reshape(2, 2, 2, 2, HD).sum(axis=3)

    def joined(first, later, part):
        return jnp.stack([first[part], later[part]]).astype(F32)

    qkv_sums, up_sums = (last.qkv_whole, lower_back.qkv_whole), (lower_back.up_whole, upper_back.up_whole)
    inside = slice(width)
    return (
        upper_back.layer_out[None],
        last.input_grad[None],
        joined(*qkv_sums, inside),
        joined(*qkv_sums, width),
        joined(last.out_whole, lower_back.out_whole, inside),
        joined(*up_sums, inside),
        joined(*up_sums, width),
        joined(lower_back.down_whole, upper_back.down_whole, inside),
        jnp.stack(gains).reshape(2, 4, width),
        jnp.stack(offsets).reshape(2, 4, width),
        head_sums[:, 0],
        head_sums[:, 1],
    )


TP = ("c", "r")


def exchange(values):
    return lax.ppermute(values, ("c", "h"), [(0, 0), (1, 2), (2, 1), (3, 3)])


def layer_norm(values, norm_scale, norm_bias):
    average = jnp.mean(values, axis=-1, keepdims=True)
    centered = values - average
    variance = jnp.mean(centered * centered, axis=-1, keepdims=True)
    return centered * lax.rsqrt(variance + EPSILON) * norm_scale + norm_bias


def exact_gelu(values):
    return jax.nn.gelu(values, approximate=False)


def attend_rows(query_rows, key_rows, value_rows, score_scale):
    scores = (
        jnp.einsum("qhe,khe->hqk", query_rows, key_rows, preferred_element_type=jnp.float32)
        * score_scale
    )
    largest = jnp.max(scores, axis=-1, keepdims=True)
    unnormed = jnp.exp(scores - largest)
    denominator = jnp.sum(unnormed, axis=-1, keepdims=True)
    weights = (unnormed / denominator).astype(jnp.bfloat16)
    mixed = jnp.einsum("hqk,khe->qhe", weights, value_rows, preferred_element_type=jnp.float32)
    return (mixed, (largest + jnp.log(denominator))[:, :, 0])


def attend_back(query_rows, key_rows, value_rows, log_total, grad_rows, score_scale):
    scores = (
        jnp.einsum("qhe,khe->hqk", query_rows, key_rows, preferred_element_type=jnp.float32)
        * score_scale
    )
    probs = jnp.exp(scores - log_total[:, :, None])
    grad_probs = jnp.einsum(
        "qhe,khe->hqk", grad_rows, value_rows, preferred_element_type=jnp.float32
    )
    grad_scores = probs * (grad_probs - jnp.sum(probs * grad_probs, axis=-1, keepdims=True))
    grad_scores = grad_scores.astype(jnp.bfloat16)
    grad_query = (
        jnp.einsum("hqk,khe->qhe", grad_scores, key_rows, preferred_element_type=jnp.float32)
        * score_scale
    )
    grad_key = (
        jnp.einsum("hqk,qhe->khe", grad_scores, query_rows, preferred_element_type=jnp.float32)
        * score_scale
    )
    grad_value = jnp.einsum(
        "hqk,qhe->khe", probs.astype(jnp.bfloat16), grad_rows, preferred_element_type=jnp.float32
    )
    return (grad_query, grad_key, grad_value)


def attention_forward(queries, key_all, value_all, frame_only, score_scale):
    frame_shape = (queries.shape[0] // FRAME_TOK, FRAME_TOK) + queries.shape[1:]
    query_frames = queries.reshape(frame_shape)
    if frame_only:
        mixed, log_total = lax.map(
            lambda triple: attend_rows(triple[0], triple[1], triple[2], score_scale),
            (query_frames, key_all.reshape(frame_shape), value_all.reshape(frame_shape)),
        )
    else:
        mixed, log_total = lax.map(
            lambda query_block: attend_rows(query_block, key_all, value_all, score_scale),
            query_frames,
        )
    return (mixed.reshape(queries.shape), log_total)


def attention_backward(queries, key_all, value_all, log_total, grad_mixed, frame_only, score_scale):
    frame_shape = (queries.shape[0] // FRAME_TOK, FRAME_TOK) + queries.shape[1:]
    query_frames = queries.reshape(frame_shape)
    grad_frames = grad_mixed.reshape(frame_shape)
    if frame_only:
        grad_query, grad_key, grad_value = lax.map(
            lambda group_in: attend_back(
                group_in[0], group_in[1], group_in[2], group_in[3], group_in[4], score_scale
            ),
            (
                query_frames,
                key_all.reshape(frame_shape),
                value_all.reshape(frame_shape),
                log_total,
                grad_frames,
            ),
        )
        return (
            grad_query.reshape(queries.shape),
            grad_key.reshape(queries.shape),
            grad_value.reshape(queries.shape),
        )

    def visit_frame(running, group_in):
        grad_query, grad_key, grad_value = attend_back(
            group_in[0], key_all, value_all, group_in[1], group_in[2], score_scale
        )
        return ((running[0] + grad_key, running[1] + grad_value), grad_query)

    zero_keys = jnp.zeros(key_all.shape, jnp.float32)
    (grad_key, grad_value), grad_query = lax.scan(
        visit_frame, (zero_keys, zero_keys), (query_frames, log_total, grad_frames)
    )
    return (grad_query.reshape(queries.shape), grad_key, grad_value)


def any_body(
    frames_in,
    qkv_weight,
    qkv_bias,
    out_weight,
    up_weight,
    up_bias,
    down_weight,
    norm_gain,
    norm_offset,
    head_gain,
    head_offset,
    cotangent,
    visible,
    query_count,
):
    score_scale = HD ** (-0.5)
    frames = exchange(frames_in[0])
    qkv_weight, out_weight, up_weight, down_weight, qkv_bias, up_bias = (
        [exchange(stacked[block_index]) for block_index in range(2)]
        for stacked in (qkv_weight, out_weight, up_weight, down_weight, qkv_bias, up_bias)
    )
    weighting = visible[0].astype(jnp.float32) * (query_count[0].astype(jnp.float32) / QMAX)
    weighting = exchange(weighting)
    cotangent = exchange(cotangent[0])

    def backward_block(grad_out, block_index, frame_only, saved):
        (
            hidden,
            gathered,
            split,
            queries,
            key_all,
            value_all,
            log_total,
            mixed_flat,
            branch,
            middle,
            gathered_two,
            hidden_up,
            activated,
            branch_two,
        ) = saved
        gains = norm_gain[block_index]
        offsets = norm_offset[block_index]
        total_rows = split.shape[0]
        grad_branch_two = gains[3] * grad_out
        offset_grad_three = jnp.sum(grad_branch_two, axis=0)
        gain_grad_three = jnp.sum(grad_out * branch_two, axis=0)
        shard_rows = lax.all_gather(grad_branch_two.astype(jnp.bfloat16), TP, axis=0, tiled=True)
        down_grad = jnp.einsum(
            "tf,td->fd", activated, shard_rows, preferred_element_type=jnp.float32
        )
        act_grad = jnp.einsum(
            "td,fd->tf", shard_rows, down_weight[block_index], preferred_element_type=jnp.float32
        )
        up_grad = jax.vjp(exact_gelu, hidden_up)[1](act_grad)[0].astype(jnp.bfloat16)
        down_grad, up_grads = (down_grad, up_grad)
        up_weight_grad = jnp.einsum(
            "td,tf->df", gathered_two, up_grads, preferred_element_type=jnp.float32
        )
        up_bias_grad = jnp.sum(up_grads.astype(jnp.float32), axis=0)
        second_grad = lax.psum_scatter(
            jnp.einsum(
                "tf,df->td", up_grads, up_weight[block_index], preferred_element_type=jnp.float32
            ).astype(jnp.bfloat16),
            TP,
            scatter_dimension=0,
            tiled=True,
        ).astype(jnp.float32)
        middle_grad, gain_grad_one, offset_grad_one = jax.vjp(
            layer_norm, middle, gains[1], offsets[1]
        )[1](second_grad)
        middle_grad = middle_grad + grad_out
        grad_branch = gains[2] * middle_grad
        offset_grad_two = jnp.sum(grad_branch, axis=0)
        gain_grad_two = jnp.sum(middle_grad * branch, axis=0)
        shard_rows = lax.all_gather(grad_branch.astype(jnp.bfloat16), TP, axis=0, tiled=True)
        out_grad = jnp.einsum(
            "tc,td->cd", mixed_flat, shard_rows, preferred_element_type=jnp.float32
        )
        mixed_grad = jnp.einsum(
            "td,cd->tc", shard_rows, out_weight[block_index], preferred_element_type=jnp.float32
        ).astype(jnp.bfloat16)
        out_grad, mixed_grads = (out_grad, mixed_grad)
        grad_query, grad_key, grad_value = attention_backward(
            queries,
            key_all,
            value_all,
            log_total,
            mixed_grads.reshape(queries.shape),
            frame_only,
            score_scale,
        )
        raw_query_grad, query_gain_grad, query_offset_grad = jax.vjp(
            layer_norm, split[:, :, 0], head_gain[block_index, 0], head_offset[block_index, 0]
        )[1](grad_query)
        raw_key_grad, key_gain_grad, key_offset_grad = jax.vjp(
            layer_norm, split[:, :, 1], head_gain[block_index, 1], head_offset[block_index, 1]
        )[1](grad_key)
        projected_grad = (
            jnp.stack([raw_query_grad, raw_key_grad, grad_value], axis=2)
            .reshape(total_rows, -1)
            .astype(jnp.bfloat16)
        )
        qkv_weight_grad = jnp.einsum(
            "td,tc->dc", gathered, projected_grad, preferred_element_type=jnp.float32
        )
        qkv_bias_grad = jnp.sum(projected_grad.astype(jnp.float32), axis=0)
        normed_grad = lax.psum_scatter(
            jnp.einsum(
                "tc,dc->td",
                projected_grad,
                qkv_weight[block_index],
                preferred_element_type=jnp.float32,
            ).astype(jnp.bfloat16),
            TP,
            scatter_dimension=0,
            tiled=True,
        ).astype(jnp.float32)
        hidden_grad, gain_grad_zero, offset_grad_zero = jax.vjp(
            layer_norm, hidden, gains[0], offsets[0]
        )[1](normed_grad)
        hidden_grad = hidden_grad + middle_grad
        large_grads = (
            qkv_weight_grad,
            qkv_bias_grad,
            out_grad,
            up_weight_grad,
            up_bias_grad,
            down_grad,
        )
        small_grads = (
            jnp.stack([gain_grad_zero, gain_grad_one, gain_grad_two, gain_grad_three]),
            jnp.stack([offset_grad_zero, offset_grad_one, offset_grad_two, offset_grad_three]),
            jnp.stack([query_gain_grad, key_gain_grad]),
            jnp.stack([query_offset_grad, key_offset_grad]),
        )
        return (hidden_grad, large_grads, small_grads)

    hidden = frames.astype(jnp.float32)
    kept_states = []
    for block_index in range(2):
        forward_frame_only = block_index == 0
        forward_gains = norm_gain[block_index]
        forward_offsets = norm_offset[block_index]
        normed = layer_norm(hidden, forward_gains[0], forward_offsets[0]).astype(jnp.bfloat16)
        forward_gathered = lax.all_gather(normed, TP, axis=0, tiled=True)
        projected = jnp.dot(
            forward_gathered, qkv_weight[block_index], preferred_element_type=jnp.float32
        )
        projected = projected + qkv_bias[block_index].astype(jnp.float32)
        forward_total_rows = projected.shape[0]
        forward_split = projected.reshape(forward_total_rows, -1, 3, HD)
        forward_queries = layer_norm(
            forward_split[:, :, 0], head_gain[block_index, 0], head_offset[block_index, 0]
        ).astype(jnp.bfloat16)
        forward_key_all = layer_norm(
            forward_split[:, :, 1], head_gain[block_index, 1], head_offset[block_index, 1]
        ).astype(jnp.bfloat16)
        forward_value_all = forward_split[:, :, 2].astype(jnp.bfloat16)
        mixed, forward_log_total = attention_forward(
            forward_queries, forward_key_all, forward_value_all, forward_frame_only, score_scale
        )
        forward_mixed_flat = mixed.reshape(forward_total_rows, -1).astype(jnp.bfloat16)
        forward_branch = (
            lax.psum_scatter(
                jnp.dot(
                    forward_mixed_flat, out_weight[block_index], preferred_element_type=jnp.float32
                ).astype(jnp.bfloat16),
                TP,
                scatter_dimension=0,
                tiled=True,
            ).astype(jnp.float32)
            + forward_offsets[2]
        )
        forward_middle = hidden + forward_gains[2] * forward_branch
        second = layer_norm(forward_middle, forward_gains[1], forward_offsets[1]).astype(
            jnp.bfloat16
        )
        forward_gathered_two = lax.all_gather(second, TP, axis=0, tiled=True)
        forward_hidden_up = jnp.dot(
            forward_gathered_two, up_weight[block_index], preferred_element_type=jnp.float32
        )
        forward_hidden_up = forward_hidden_up + up_bias[block_index].astype(jnp.float32)
        forward_activated = exact_gelu(forward_hidden_up).astype(jnp.bfloat16)
        forward_branch_two = (
            lax.psum_scatter(
                jnp.dot(
                    forward_activated, down_weight[block_index], preferred_element_type=jnp.float32
                ).astype(jnp.bfloat16),
                TP,
                scatter_dimension=0,
                tiled=True,
            ).astype(jnp.float32)
            + forward_offsets[3]
        )
        result = forward_middle + forward_gains[3] * forward_branch_two
        forward_saved = (
            hidden,
            forward_gathered,
            forward_split,
            forward_queries,
            forward_key_all,
            forward_value_all,
            forward_log_total,
            forward_mixed_flat,
            forward_branch,
            forward_middle,
            forward_gathered_two,
            forward_hidden_up,
            forward_activated,
            forward_branch_two,
        )
        hidden = result
        saved = forward_saved
        kept_states.append(saved)
    layer_out = exchange(hidden.astype(jnp.bfloat16))[None]
    grad_hidden = cotangent.astype(jnp.float32) * weighting[:, None]
    grad_hidden, large_one, small_one = backward_block(grad_hidden, 1, False, kept_states[1])
    grad_hidden, large_zero, small_zero = backward_block(grad_hidden, 0, True, kept_states[0])
    input_grad = exchange(grad_hidden.astype(jnp.bfloat16))[None]

    def over_scenes(grads):
        shapes = [grad.shape for grad in grads]
        parts = lax.axis_size("sy")
        flat = [grad.astype(jnp.bfloat16).reshape(parts, -1) for grad in grads]
        sizes = [part.shape[1] for part in flat]
        joined = jnp.concatenate(flat, axis=1)
        share = lax.psum_scatter(joined, "sy", scatter_dimension=0, tiled=True)
        share = lax.psum(share, "h")
        whole = exchange(lax.all_gather(share, "sy", axis=0, tiled=True))
        found = []
        start = 0
        for shape, size in zip(shapes, sizes):
            found.append(whole[:, start : start + size].reshape(shape).astype(jnp.float32))
            start += size
        return found

    summed_one = over_scenes(large_one)
    summed_zero = over_scenes(large_zero)
    summed = [jnp.stack(pair) for pair in zip(summed_zero, summed_one)]
    small = jax.tree.map(lambda first, later: jnp.stack([first, later]), small_zero, small_one)
    summed = tuple(summed) + tuple(lax.psum(small, ("sy", "c", "h", "r")))
    return (
        layer_out,
        input_grad,
        summed[0],
        summed[1],
        summed[2],
        summed[3],
        summed[4],
        summed[5],
        summed[6],
        summed[7],
        summed[8],
        summed[9],
    )


def solution(mesh):
    scenes, shards = mesh.shape["scene"], mesh.shape["tp"]
    if (scenes, shards) == (4, 8):
        body, sizes, axes, tp = square_body, (2, 2, 2, 2, 2), AXES, ("h", "zl", "x")
    else:
        body, sizes, axes, tp = any_body, (scenes // 2, 2, 2, shards // 2), ("sy", "c", "h", "r"), ("h", "r")
    scene = ("sy", "c")
    return jax.shard_map(
        body,
        mesh=jax.sharding.Mesh(mesh.devices.reshape(sizes), axes),
        in_specs=(
            P(scene, tp, None),
            P(None, None, tp),
            P(None, tp),
            P(None, tp, None),
            P(None, None, tp),
            P(None, tp),
            P(None, tp, None),
            P(),
            P(),
            P(),
            P(),
            P(scene, tp, None),
            P(scene, tp),
            P(scene),
        ),
        out_specs=(
            P(scene, tp, None),
            P(scene, tp, None),
            P(None, None, tp),
            P(None, tp),
            P(None, tp, None),
            P(None, None, tp),
            P(None, tp),
            P(None, tp, None),
            P(),
            P(),
            P(),
            P(),
        ),
        check_vma=False,
    )
```

```python
import functools
import types

import jax
import jax.numpy as jnp
from jax import lax
from jax.experimental import pallas as pl
from jax.experimental.pallas import tpu as pltpu
from jax.sharding import PartitionSpec as P

HD = 64
QMAX = 512
FRAME_TOK = 1024
EPSILON = 1e-06
BF = jnp.bfloat16
F32 = jnp.float32
MESH = pl.DeviceIdType.MESH
DMA = pltpu.SemaphoreType.DMA
VMEM_LIMIT = 63 * 1024 * 1024

AXES = ("sy", "c", "h", "zl", "x")


def dot(left, right):
    return lax.dot_general(left, right, (((1,), (0,)), ((), ())), preferred_element_type=F32)


def dot_rt(left, right):
    return lax.dot_general(left, right, (((1,), (1,)), ((), ())), preferred_element_type=F32)


def dot_lt(left, right):
    return lax.dot_general(left, right, (((0,), (0,)), ((), ())), preferred_element_type=F32)


def dot_fine(left, right):
    high = left.astype(BF)
    return dot(high, right) + dot((left - high.astype(F32)).astype(BF), right)


def remote(source, target, send, recv, device):
    return pltpu.make_async_remote_copy(
        src_ref=source, dst_ref=target, send_sem=send, recv_sem=recv, device_id=device, device_id_type=MESH
    )


class Spot:
    def __init__(self):
        self.sy, self.c, self.h, self.zl, self.x = (lax.axis_index(name) for name in AXES)
        self.over_x = dict(x=1 - self.x)
        self.over_z = dict(zl=1 - self.zl)
        self.core = dict(c=1 - self.c)
        self.over_y = dict(sy=1 - self.sy)
        self.over_h = dict(h=1 - self.h)
        self.partner = dict(c=1 - self.c, h=1 - self.h)
        self.home = self.c == self.h
        self.away = self.c != self.h

    def greet(self, *devices):
        barrier = pltpu.get_barrier_semaphore()
        for device in devices:
            pl.semaphore_signal(barrier, inc=1, device_id=device, device_id_type=MESH)
        pl.semaphore_wait(barrier, len(devices))

    def slot(self, core, step):
        zl = lax.rem(self.zl + step // 2, 2)
        x = lax.rem(self.x + step % 2, 2)
        return core * 4 + zl * 2 + x

    def part(self, size, own=True, piece=0, pieces=1):
        half = size // 2
        rows = half // pieces
        return pl.ds(pl.multiple_of((self.sy if own else 1 - self.sy) * half + piece * rows, rows), rows)


class Gather:
    @staticmethod
    def scratch(rows, width):
        return [pltpu.VMEM((8, rows, width), BF), DMA((2, 6)), DMA((2, 6)), DMA((2, 4)), DMA((2, 4))]

    def __init__(self, spot, refs):
        self.spot = spot
        self.held, self.send, self.recv, self.core_send, self.core_recv = refs
        self.rows = self.held.shape[1] // 2

    def link(self, stream, step, part, number, device):
        half = self.rows // 2
        start = pl.multiple_of(stream * self.rows + part * half, half)
        ref = self.held.at[self.spot.slot(self.spot.c, step), pl.ds(start, half)]
        return remote(ref, ref, self.send.at[stream, number], self.recv.at[stream, number], device)

    def x_first(self, stream):
        return self.link(stream, 0, 0, 0, self.spot.over_x)

    def x_later(self, stream):
        return self.link(stream, 0, 1, 1, self.spot.over_x)

    def z_later(self, stream):
        return self.link(stream, 0, 0, 2, self.spot.over_z)

    def z_first(self, stream):
        return self.link(stream, 0, 1, 3, self.spot.over_z)

    def z_relay(self, stream):
        return self.link(stream, 1, 0, 4, self.spot.over_z)

    def x_relay(self, stream):
        return self.link(stream, 2, 1, 5, self.spot.over_x)

    def core_copy(self, stream, step):
        ref = self.held.at[self.spot.slot(self.spot.c, step), self.span(stream)]
        return remote(
            ref, ref, self.core_send.at[stream, step], self.core_recv.at[stream, step], self.spot.core
        )

    def span(self, stream):
        return pl.ds(pl.multiple_of(stream * self.rows, self.rows), self.rows)

    def part(self, slot, stream):
        return self.held[slot, self.span(stream)]

    def put(self, stream, values):
        self.held[self.spot.slot(self.spot.c, 0), self.span(stream)] = values
        self.x_first(stream).start()
        self.z_first(stream).start()
        self.core_copy(stream, 0).start()
        self.z_later(stream).start()
        self.x_later(stream).start()

    def pass_on(self, stream):
        self.x_first(stream).wait_recv()
        self.z_relay(stream).start()
        self.z_first(stream).wait_recv()
        self.x_relay(stream).start()

    def arrive(self, stream, step):
        pl.when(step == 1)(lambda: self.x_later(stream).wait_recv())
        pl.when(step == 2)(lambda: self.z_later(stream).wait_recv())

        @pl.when(step == 3)
        def _():
            self.z_relay(stream).wait_recv()
            self.x_relay(stream).wait_recv()

        pl.when(step > 0)(lambda: self.core_copy(stream, step).start())

    def arrive_core(self, stream, step):
        self.core_copy(stream, step).wait_recv()

    def finish(self):
        for stream in range(2):
            for copy in (self.x_first, self.x_later, self.z_first, self.z_later, self.z_relay, self.x_relay):
                copy(stream).wait_send()
            for step in range(4):
                self.core_copy(stream, step).wait_send()

    def consume(self, use, passed=0, before=None):
        def visit(index, carry):
            stream, step = index // 4, lax.rem(index, 4)
            if before is not None:
                before(index)
            self.arrive(stream, step)
            use(self.spot.slot(self.spot.c, step), stream)
            pl.when((index >= passed) & (index < 2))(lambda: self.pass_on(index))
            self.arrive_core(stream, step)
            use(self.spot.slot(1 - self.spot.c, step), stream)
            return carry

        lax.fori_loop(0, 8, visit, 0)


class Scatter:
    @staticmethod
    def local(rows, width):
        return [
            pltpu.VMEM((4, rows, width), BF),
            pltpu.VMEM((4, rows, width), BF),
            pltpu.VMEM((2, 2, rows // 4, width), BF),
        ]

    @staticmethod
    def scratch(rows, width):
        return [
            pltpu.VMEM((4, rows, width), BF),
            pltpu.VMEM((2, 6, rows // 4, width), BF),
            DMA((2, 4)),
            DMA((2, 4)),
            DMA((2, 6)),
            DMA((2, 6)),
        ]

    def __init__(self, spot, local, refs):
        self.spot = spot
        self.for_core, self.ready, self.relayed = local
        self.from_core, self.landed, self.core_send, self.core_recv, self.send, self.recv = refs
        self.rows = self.for_core.shape[1] // 2

    def span(self, stream):
        return pl.ds(pl.multiple_of(stream * self.rows, self.rows), self.rows)

    def half(self, stream, part):
        half = self.rows // 2
        return pl.ds(pl.multiple_of(stream * self.rows + part * half, half), half)

    def link(self, source, stream, number, device):
        return remote(
            source, self.landed.at[stream, number], self.send.at[stream, number], self.recv.at[stream, number], device
        )

    def x_near(self, stream):
        return self.link(self.ready.at[1, self.half(stream, 0)], stream, 0, self.spot.over_x)

    def x_far(self, stream):
        return self.link(self.ready.at[3, self.half(stream, 0)], stream, 1, self.spot.over_x)

    def z_near(self, stream):
        return self.link(self.ready.at[2, self.half(stream, 1)], stream, 2, self.spot.over_z)

    def z_far(self, stream):
        return self.link(self.ready.at[3, self.half(stream, 1)], stream, 3, self.spot.over_z)

    def z_relay(self, stream):
        return self.link(self.relayed.at[stream, 0], stream, 4, self.spot.over_z)

    def x_relay(self, stream):
        return self.link(self.relayed.at[stream, 1], stream, 5, self.spot.over_x)

    def core_copy(self, stream, step):
        span = self.span(stream)
        return remote(
            self.for_core.at[step, span],
            self.from_core.at[step, span],
            self.core_send.at[stream, step],
            self.core_recv.at[stream, step],
            self.spot.core,
        )

    def put_other(self, stream, step, values):
        self.for_core[step, self.span(stream)] = values.astype(BF)
        self.core_copy(stream, step).start()

    def put_own(self, stream, step, values):
        self.ready[step, self.span(stream)] = values.astype(BF)

    def flush(self, stream, step):
        self.core_copy(stream, step).wait_recv()
        span = self.span(stream)
        total = self.ready[step, span].astype(F32) + self.from_core[step, span].astype(F32)
        self.ready[step, span] = total.astype(BF)

        pl.when(step == 1)(lambda: self.x_near(stream).start())
        pl.when(step == 2)(lambda: self.z_near(stream).start())

        @pl.when(step == 3)
        def _():
            self.x_far(stream).start()
            self.z_far(stream).start()

    def relay(self, stream):
        self.x_far(stream).wait_recv()
        mine = self.ready[2, self.half(stream, 0)].astype(F32)
        self.relayed[stream, 0] = (mine + self.landed[stream, 1].astype(F32)).astype(BF)
        self.z_relay(stream).start()
        self.z_far(stream).wait_recv()
        mine = self.ready[1, self.half(stream, 1)].astype(F32)
        self.relayed[stream, 1] = (mine + self.landed[stream, 3].astype(F32)).astype(BF)
        self.x_relay(stream).start()

    def result(self, stream):
        self.x_near(stream).wait_recv()
        self.z_near(stream).wait_recv()
        self.z_relay(stream).wait_recv()
        self.x_relay(stream).wait_recv()
        landed = lambda number: self.landed[stream, number].astype(F32)
        return self.ready[0, self.span(stream)].astype(F32) + jnp.concatenate(
            [landed(0) + landed(4), landed(2) + landed(5)], axis=0
        )

    def finish(self):
        for stream in range(2):
            for copy in (self.x_near, self.x_far, self.z_near, self.z_far, self.z_relay, self.x_relay):
                copy(stream).wait_send()
            for step in range(4):
                self.core_copy(stream, step).wait_send()

    def produce(self, term, before=None):
        spot = self.spot

        def visit(index, carry):
            stream, step = index // 4, 3 - lax.rem(index, 4)
            if before is not None:
                before(index)
            self.put_other(stream, step, term(spot.slot(1 - spot.c, step), stream))

            @pl.when(index > 0)
            def _():
                pl.when(index == 5)(lambda: self.relay(0))
                self.flush((index - 1) // 4, 3 - lax.rem(index - 1, 4))

            self.put_own(stream, step, term(spot.slot(spot.c, step), stream))
            return carry

        lax.fori_loop(0, 8, visit, 0)
        self.flush(1, 0)

    def produce_from(self, gather, term, passed=1):
        spot = self.spot

        def visit(index, carry):
            stream, step = index // 4, lax.rem(index, 4)
            gather.arrive(stream, step)
            self.put_own(stream, step, term(spot.slot(spot.c, step), stream))
            pl.when((index >= passed) & (index < 2))(lambda: gather.pass_on(index))
            gather.arrive_core(stream, step)
            self.put_other(stream, step, term(spot.slot(1 - spot.c, step), stream))

            @pl.when(index > 0)
            def _():
                pl.when(index == 6)(lambda: self.relay(0))
                self.flush((index - 1) // 4, lax.rem(index - 1, 4))

            return carry

        lax.fori_loop(0, 8, visit, 0)
        self.flush(1, 3)


class Swap:
    scratch = [DMA((2,))]

    def __init__(self, spot, source, target, refs):
        (sems,) = refs
        self.spot = spot
        self.local = pltpu.make_async_copy(source, target, sems.at[0])
        self.copy = remote(source, target, sems.at[0], sems.at[1], spot.partner)

    def start(self):
        pl.when(self.spot.home)(self.local.start)
        pl.when(self.spot.away)(self.copy.start)

    def arrive(self):
        pl.when(self.spot.home)(self.local.wait)
        pl.when(self.spot.away)(self.copy.wait_recv)

    def finish(self):
        pl.when(self.spot.away)(self.copy.wait_send)


class Move:
    scratch = [DMA((2, 4))]

    def __init__(self, spot, own, got, refs):
        (sems,) = refs
        self.spot, self.own, self.got = spot, own, got
        self.over, self.along = [], []
        for piece in range(2):
            rows = spot.part(got.shape[0], True, piece, 2)
            at = sems.at[piece]
            self.over.append(remote(own.at[rows], got.at[rows], at.at[0], at.at[1], spot.over_h))
            self.along.append(remote(got.at[rows], got.at[rows], at.at[2], at.at[3], spot.over_y))

    def start(self):
        @pl.when(self.spot.home)
        def _():
            for copy in self.over:
                copy.start()

    def relay(self, piece):
        @pl.when(self.spot.away)
        def _():
            self.over[piece].wait_recv()
            self.along[piece].start()

    def finish(self):
        @pl.when(self.spot.away)
        def _():
            for copy in self.along:
                copy.wait_recv()
                copy.wait_send()

        @pl.when(self.spot.home)
        def _():
            for copy in self.over:
                copy.wait_send()

    def pick(self, target, sem):
        copy = pltpu.make_async_copy(self.got, target, sem)
        pl.when(self.spot.home)(pltpu.make_async_copy(self.own, target, sem).start)
        pl.when(self.spot.away)(copy.start)
        return copy


class Total:
    @staticmethod
    def scratch(rows, width):
        half = pltpu.VMEM((rows // 2, width), BF)
        return [half, half, half, DMA((11,))]

    def __init__(self, spot, grad, whole, refs):
        self.landed, self.share, self.later_landed, sems = refs
        self.grad, self.spot = grad, spot
        share = self.share
        if grad is not None:
            other = grad.at[spot.part(grad.shape[0], False)]
            self.first = remote(other, self.landed, sems.at[0], sems.at[1], spot.over_y)
        if self.later_landed is not None:
            self.over = remote(share, self.later_landed, sems.at[2], sems.at[3], spot.over_h)
        if whole is not None:
            size = whole.shape[0]
            mine, other = whole.at[spot.part(size)], whole.at[spot.part(size, False)]
            self.along = remote(share, mine, sems.at[4], sems.at[5], spot.over_y)
            self.near = remote(share, mine, sems.at[6], sems.at[7], spot.core)
            self.later = remote(other, other, sems.at[8], sems.at[9], spot.core)
            self.local = pltpu.make_async_copy(share, mine, sems.at[10])

    def start(self):
        self.first.start()

    def add(self):
        self.first.wait_recv()
        mine = self.grad[self.spot.part(self.grad.shape[0])]
        self.share[...] = (mine.astype(F32) + self.landed[...].astype(F32)).astype(BF)

    def send_over(self):
        pl.when(self.spot.away)(self.over.start)

    def add_over(self):
        @pl.when(self.spot.home)
        def _():
            self.over.wait_recv()
            self.share[...] = (self.share[...].astype(F32) + self.later_landed[...].astype(F32)).astype(BF)

    def spread(self):
        @pl.when(self.spot.home)
        def _():
            self.along.start()
            self.near.start()
            self.local.start()

    def relay(self):
        @pl.when(self.spot.home)
        def _():
            self.along.wait_recv()
            self.later.start()

    def finish_first(self):
        self.first.wait_send()

    def finish_over(self):
        pl.when(self.spot.away)(self.over.wait_send)

    def finish_spread(self):
        @pl.when(self.spot.home)
        def _():
            self.along.wait_send()
            self.near.wait_send()
            self.later.wait_send()
            self.local.wait()

        @pl.when(self.spot.away)
        def _():
            self.near.wait_recv()
            self.later.wait_recv()

    def finish(self):
        self.finish_first()
        self.finish_over()
        self.finish_spread()


class SmallSum:
    @staticmethod
    def scratch(rows, width):
        return [pltpu.VMEM((5, rows, width), F32), DMA((5,)), DMA((5,))]

    def __init__(self, spot, total, refs):
        landed, send, recv = refs
        self.total, self.landed = total, landed
        self.copies = [
            remote(total, landed.at[number], send.at[number], recv.at[number], device)
            for number, device in enumerate((spot.core, spot.over_x, spot.over_z, spot.over_h, spot.over_y))
        ]

    def step(self, number):
        if number > 0:
            self.copies[number - 1].wait()
            self.total[...] += self.landed[number - 1]
        if number < 5:
            self.copies[number].start()


class QuickSum:
    @staticmethod
    def scratch(rows, width):
        return [pltpu.VMEM((8, rows, width), F32), pltpu.VMEM((4, rows, width), F32), DMA((10,)), DMA((10,))]

    def __init__(self, spot, total, refs):
        self.total = total
        self.near, self.far, send, recv = refs
        self.near_place = spot.c * 4 + spot.zl * 2 + spot.x
        self.far_place = spot.sy * 2 + spot.h
        self.near_copies, self.far_copies = [], []
        for number in range(1, 8):
            device = dict(c=spot.c, zl=spot.zl, x=spot.x)
            for bit, name in ((4, "c"), (2, "zl"), (1, "x")):
                if number & bit:
                    device[name] = 1 - device[name]
            target = self.near.at[self.near_place]
            self.near_copies.append(remote(total, target, send.at[number - 1], recv.at[number - 1], device))
        for number in range(1, 4):
            device = dict(sy=spot.sy, h=spot.h)
            for bit, name in ((2, "sy"), (1, "h")):
                if number & bit:
                    device[name] = 1 - device[name]
            target = self.far.at[self.far_place]
            self.far_copies.append(remote(total, target, send.at[number + 6], recv.at[number + 6], device))

    @staticmethod
    def partners(spot):
        flip = lambda **names: {name: 1 - getattr(spot, name) for name in names}
        return [
            flip(c=0, x=0), flip(c=0, zl=0), flip(zl=0, x=0), flip(c=0, zl=0, x=0), flip(sy=0, h=0),
        ]

    def start(self):
        self.near[self.near_place] = self.total[...]
        for copy in self.near_copies:
            copy.start()

    def step(self):
        for copy in self.near_copies:
            copy.wait()
        total = self.near[0]
        for place in range(1, 8):
            total += self.near[place]
        self.total[...] = total
        self.far[self.far_place] = total
        for copy in self.far_copies:
            copy.start()

    def end(self):
        for copy in self.far_copies:
            copy.wait()
        total = self.far[0]
        for place in range(1, 4):
            total += self.far[place]
        self.total[...] = total


def norm_parts(values):
    average = jnp.mean(values, axis=-1, keepdims=True)
    centered = values - average
    scale = lax.rsqrt(jnp.mean(centered * centered, axis=-1, keepdims=True) + EPSILON)
    return centered * scale, scale


def norm_back(grad, gain, normed, scale):
    scaled = grad * gain
    back = scale * (
        scaled
        - jnp.mean(scaled, axis=-1, keepdims=True)
        - normed * jnp.mean(scaled * normed, axis=-1, keepdims=True)
    )
    return back, jnp.sum(grad * normed, axis=0, keepdims=True), jnp.sum(grad, axis=0, keepdims=True)


def gelu_both(values):
    size = jnp.abs(values) * 0.7071067811865476
    bell = jnp.exp(-size * size)
    t = 1.0 / (1.0 + 0.3275911 * size)
    poly = t * (
        0.254829592 + t * (-0.284496736 + t * (1.421413741 + t * (-1.453152027 + t * 1.061405429)))
    )
    tail = 0.5 * poly * bell
    below = jnp.where(values < 0, tail, 1.0 - tail)
    return values * below, below + values * bell * 0.3989422804014327


def lanes_of_head(shape, head):
    lane = lax.broadcasted_iota(jnp.int32, shape, 1)
    return (lane < HD) if head == 0 else (lane >= HD)


def pack_queries_keys(projected):
    one, two, three = (projected[:, part * 2 * HD : (part + 1) * 2 * HD] for part in range(3))
    low = lanes_of_head(one.shape, 0)
    keys = pltpu.roll(jnp.where(low, three, one), HD, 1)
    return jnp.concatenate([jnp.where(low, one, two), keys], axis=1), jnp.where(low, two, three)


def unpack_queries_keys(queries, keys, values):
    low = lanes_of_head(queries.shape, 0)
    keys = pltpu.roll(keys, HD, 1)
    return jnp.where(low, queries, keys), jnp.where(low, values, queries), jnp.where(low, keys, values)


def averager(width):
    row = lax.broadcasted_iota(jnp.int32, (width, width), 0) // HD
    column = lax.broadcasted_iota(jnp.int32, (width, width), 1) // HD
    return jnp.where(row == column, 1.0 / HD, 0.0).astype(BF)


def project(k, block, gather, raw_ref, qk_ref, v_ref, slot, stream):
    rows = pl.ds(pl.multiple_of((slot * 2 + stream) * gather.rows, gather.rows), gather.rows)
    projected = dot(gather.part(slot, stream), k.qkv_weight[...]) + k.biases[block : block + 1, : 6 * HD]
    raw, values = pack_queries_keys(projected)
    raw_ref[rows] = raw
    average = averager(4 * HD)
    centered = raw - dot_fine(raw, average)
    scale = lax.rsqrt(dot_fine(centered * centered, average) + EPSILON)
    gain, offset = k.head_gains[block : block + 1], k.head_offsets[block : block + 1]
    qk_ref[rows] = (centered * scale * gain + offset).astype(BF)
    v_ref[rows] = values.astype(BF)


def in_three(values):
    high = values.astype(BF)
    rest = values - high.astype(F32)
    middle = rest.astype(BF)
    return high.astype(F32), middle.astype(F32), (rest - middle.astype(F32)).astype(BF).astype(F32)


def beside(rows, values, head):
    lane = lax.broadcasted_iota(jnp.int32, rows.shape, 1)
    start = HD if head == 0 else 0
    high, middle, low = in_three(values)
    other = jnp.where(
        lane == start, high, jnp.where(lane == start + 1, middle, jnp.where(lane == start + 2, low, 0.0))
    )
    return jnp.where(lanes_of_head(rows.shape, head), rows.astype(F32), other).astype(BF)


def slice_attend(k, keys, start, size):
    rows = pl.ds(pl.multiple_of(start, size), size)
    span = pl.ds(pl.multiple_of(start // keys * keys, keys), keys)
    queries = k.qk_in[rows, : 2 * HD] * jnp.asarray(HD**-0.5, BF)
    low = lanes_of_head(queries.shape, 0)
    zeros = jnp.zeros_like(queries)
    mine = [jnp.where(low, queries, zeros), jnp.where(low, zeros, queries)]
    scores = dot_rt(jnp.concatenate(mine, axis=0), k.qk_in[span, 2 * HD :])
    largest = jnp.max(scores, axis=-1, keepdims=True)
    weights = jnp.exp(scores - largest)
    total = jnp.sum(weights, axis=-1, keepdims=True)
    found = dot(weights.astype(BF), k.v_in[span, :]) / total
    logs = largest + jnp.log(total)
    for head in range(2):
        k.query[head, rows] = beside(mine[head], logs[head * size : (head + 1) * size], head)
    both = jnp.where(low, found[:size], found[size:])
    k.exact[rows] = both
    k.mixed[rows] = both.astype(BF)


def enter(k):
    spot = k.spot
    gather = Gather(spot, k.gather_first)
    swaps = [
        Swap(spot, k.frames.at[0, gather.span(stream)], k.hidden.at[gather.span(stream)], k.swaps[stream])
        for stream in range(2)
    ]
    swaps.append(Swap(spot, k.own_biases, k.biases, k.swaps[2]))
    cotangent = Swap(spot, k.cotangent.at[0], k.cotangent_here, k.swaps[3])
    weighting = Swap(spot, k.weighting, k.weighting_here, k.swaps[4])
    for swap in swaps:
        swap.start()
    for stream in range(2):
        swaps[stream].arrive()
        rows = k.hidden[gather.span(stream)].astype(F32)
        values = (norm_parts(rows)[0] * k.gains[0, 0:1] + k.offsets[0, 0:1]).astype(BF)
        if stream == 1:
            gather.pass_on(0)
        gather.put(stream, values)
    owns = (k.qkv_own, k.out_own, k.up_own, k.down_own)
    gots = (k.qkv_got, k.out_got, k.up_got, k.down_got)
    qkv, out, up, down = (Move(spot, own.at[0], got, refs) for own, got, refs in zip(owns, gots, k.moves))
    k.saves.hidden()
    gather.pass_on(1)
    for stream in range(2):
        gather.arrive_core(stream, 0)
    for move in (qkv, out, up, down):
        move.start()
    qkv.relay(0)
    qkv.relay(1)
    gather.arrive(0, 1)
    qkv.finish()
    swaps[2].arrive()
    qkv.pick(k.qkv_weight, k.pick.at[0]).wait()

    def visit(index, carry):
        stream, step = index // 4, lax.rem(index, 4)
        pl.when(index > 1)(lambda: gather.arrive(stream, step))
        project(k, 0, gather, k.raw_first, k.qk_in, k.v_in, spot.slot(spot.c, step), stream)
        pl.when(step > 0)(lambda: gather.arrive_core(stream, step))
        project(k, 0, gather, k.raw_first, k.qk_in, k.v_in, spot.slot(1 - spot.c, step), stream)

        @pl.when(index == 3)
        def _():
            out.relay(0)
            out.relay(1)
            cotangent.start()
            weighting.start()

        pl.when(index == 6)(lambda: up.relay(0))
        return carry

    lax.fori_loop(0, 8, visit, 0)
    out.finish()
    out_pick = out.pick(k.out_weight, k.pick.at[1])
    k.saves.gathered_first(gather.held)
    k.saves.raw_first()
    k.saves.qk_in()
    k.saves.v_in()
    for swap in swaps:
        swap.finish()
    gather.finish()
    out_pick.wait()
    return up, down, (cotangent, weighting)


def forward_kernel(is_last, k):
    spot = k.spot
    block = 1 if is_last else 0
    spot.greet(spot.over_x, spot.over_z, spot.core, spot.over_y, spot.over_h, spot.partner)
    if is_last:
        down = Move(spot, k.down_own.at[1], k.down_got, k.moves[0])
        up = Move(spot, k.up_own.at[1], k.up_got, k.moves[1])
        up.start()
        others = []
        k.loads.qk_in.wait()
        k.loads.v_in.wait()
        k.loads.out_weight.wait()
        k.loads.hidden.wait()
    else:
        up, down, swaps = enter(k)
        owns, gots = (k.qkv_own, k.out_own), (k.qkv_got_later, k.out_got_later)
        others = [Move(spot, own.at[1], got, refs) for own, got, refs in zip(owns, gots, k.moves[4:])]
    first, gather, later = Scatter(spot, k.local, k.one), Gather(spot, k.gather), Scatter(spot, k.local, k.two)
    rows_of = gather.span
    size = gather.held.shape[1]
    keys = k.mixed.shape[0] if is_last else FRAME_TOK

    def term_attention(slot, stream):
        start = pl.multiple_of(slot * size + stream * (size // 2), size // 2)
        slice_attend(k, keys, start, size // 2)
        return dot(k.mixed[pl.ds(start, size // 2)], k.out_weight[...])

    def before(index):
        if is_last:

            @pl.when(index == 6)
            def _():
                up.relay(0)
                up.relay(1)
                down.start()

        else:
            pl.when(index == 1)(lambda: up.relay(1))
            pl.when(index == 6)(lambda: down.relay(0))

    first.produce(term_attention, before)
    k.saves.exact()
    k.saves.query()
    for stream in range(2):
        rows = rows_of(stream)
        branch = first.result(stream) + k.offsets[block, 2:3]
        middle = k.hidden[rows].astype(F32) + k.gains[block, 2:3] * branch
        k.branch[rows] = branch
        k.middle[rows] = middle
        gather.put(stream, (norm_parts(middle)[0] * k.gains[block, 1:2] + k.offsets[block, 1:2]).astype(BF))
        if stream == 0:
            first.relay(1)
            down.relay(0 if is_last else 1)
            gather.pass_on(0)
    if is_last:
        down.relay(1)
    up.finish()
    up_pick = up.pick(k.up_weight, k.pick.at[0])
    for move in others:
        move.start()
    k.saves.branch()
    k.saves.middle()
    first.finish()
    gather.pass_on(1)
    down.finish()
    down_pick = down.pick(k.down_weight, k.pick.at[1])
    up_pick.wait()
    down_pick.wait()

    def term(slot, stream):
        bias = k.biases[block : block + 1, 6 * HD :]
        activated, slope = gelu_both(dot(gather.part(slot, stream), k.up_weight[...]) + bias)
        activated = activated.astype(BF)
        k.activated[slot, rows_of(stream)] = activated
        k.slope[slot, rows_of(stream)] = slope.astype(BF)
        return dot(activated, k.down_weight[...])

    later.produce_from(gather, term, 2)
    k.saves.second(gather.held)
    k.saves.activated()
    k.saves.slope()
    if not is_last:
        onward = Gather(spot, k.gather_next)
    for stream in range(2):
        rows = rows_of(stream)
        branch = later.result(stream) + k.offsets[block, 3:4]
        state = k.middle[rows] + k.gains[block, 3:4] * branch
        k.branch_two[rows] = branch
        k.state[rows] = state.astype(k.state.dtype)
        if not is_last:
            onward.put(stream, (norm_parts(state)[0] * k.gains[1, 0:1] + k.offsets[1, 0:1]).astype(BF))
        if stream == 0:
            later.relay(1)
            if not is_last:
                onward.pass_on(0)
            for move in others:
                move.relay(0)
                move.relay(1)
    k.saves.branch_two()
    k.saves.state()
    gather.finish()
    later.finish()
    if is_last:
        return
    for swap in swaps:
        swap.arrive()
        swap.finish()
    for move in others:
        move.finish()
    others[0].pick(k.qkv_weight, k.pick.at[0]).wait()
    onward.consume(functools.partial(project, k, 1, onward, k.raw, k.qk, k.v), 1)
    k.saves.gathered(onward.held)
    k.saves.raw()
    k.saves.qk()
    k.saves.v()
    onward.finish()


def wide(ref):
    return ref[...].reshape(ref.shape[0] * ref.shape[1], ref.shape[2])


def with_bias_row(grad_ref, weight_grad, bias_grad):
    size = weight_grad.shape[0]
    row = lax.broadcasted_iota(jnp.int32, (grad_ref.shape[0] - size, grad_ref.shape[1]), 0)
    grad_ref[:size] = weight_grad.astype(BF)
    grad_ref[size:] = jnp.where(row == 0, bias_grad, 0.0).astype(BF)


def pieces_of(ref):
    cut = ref.shape[0] // 64 * 32
    return pl.ds(0, cut), pl.ds(cut, ref.shape[0] - cut)


def qkv_weight_grad(k, gathered):
    rows = wide(k.above_qkv)
    with_bias_row(k.qkv_grad, dot_lt(wide(gathered), rows), jnp.sum(rows.astype(F32), axis=0, keepdims=True))


def prepare_keys(k, rows):
    shape = (rows.size, 2 * HD)
    lane = lax.broadcasted_iota(jnp.int32, shape, 1)
    for head in range(2):
        own = lanes_of_head(shape, head)
        ones = jnp.where(lane < (HD if head == 0 else 0) + 3, -1.0, 0.0)
        k.key_in[head, rows] = jnp.where(own, k.qk_in[rows, 2 * HD :].astype(F32), ones).astype(BF)
        k.value_in[head, rows] = jnp.where(own, k.v_in[rows].astype(F32), ones).astype(BF)


def slice_back(k, keys, block_keys, start, size, grad):
    width = 2 * HD
    rows = pl.ds(pl.multiple_of(start, size), size)
    row = lax.broadcasted_iota(jnp.int32, (width, width), 0) // HD
    column = lax.broadcasted_iota(jnp.int32, (width, width), 1) // HD
    swap_sum = jnp.where(row != column, 1.0, 0.0).astype(BF)
    delta = dot_fine(grad * k.exact[rows], swap_sum)
    lane = lax.broadcasted_iota(jnp.int32, (size, width), 1)
    high, middle, low = in_three(delta)
    for head in range(2):
        lead = HD if head == 0 else 0
        other = jnp.where(
            lane == lead, high, jnp.where(lane == lead + 1, middle, jnp.where(lane == lead + 2, low, 0.0))
        )
        k.grad_in[head] = jnp.where(lanes_of_head((size, width), head), grad, other).astype(BF)
    k.query_grad[...] = jnp.zeros_like(k.query_grad)
    first = start // keys * keys

    def visit(index, carry):
        key_rows = pl.ds(pl.multiple_of(first + index * block_keys, block_keys), block_keys)
        for head in range(2):
            own = lanes_of_head((size, width), head)
            own_keys = lanes_of_head((block_keys, width), head)
            query = k.query[head, rows]
            grad_rows = k.grad_in[head]
            key = k.key_in[head, key_rows]
            probs = jnp.exp(dot_rt(key, query))
            back = (probs * dot_rt(k.value_in[head, key_rows], grad_rows)).astype(BF)
            zeros = jnp.zeros((size, width), BF)
            k.grads[key_rows, 2 * width :] += dot(probs.astype(BF), jnp.where(own, grad_rows, zeros))
            k.grads[key_rows, width : 2 * width] += dot(back, jnp.where(own, query, zeros))
            k.query_grad[...] += dot_lt(back, jnp.where(own_keys, key, jnp.zeros((block_keys, width), BF)))
        return carry

    lax.fori_loop(0, keys // block_keys, visit, 0)
    k.grads[rows, :width] = k.query_grad[...]


def leave_heads(k, level, rows, target):
    width = 2 * HD
    average = averager(2 * width)
    values = k.raw_in[rows]
    centered = values - dot_fine(values, average)
    scale = lax.rsqrt(dot_fine(centered * centered, average) + EPSILON)
    normed = centered * scale
    lane = lax.broadcasted_iota(jnp.int32, normed.shape, 1)
    found = k.grads[rows, : 2 * width] * jnp.where(lane < width, HD**-0.5, 1.0)
    k.head_small[0:1] += jnp.sum(found * normed, axis=0, keepdims=True)
    k.head_small[1:2] += jnp.sum(found, axis=0, keepdims=True)
    scaled = found * k.head_gains[level : level + 1]
    back = scale * (scaled - dot_fine(scaled, average) - normed * dot_fine(scaled * normed, average))
    parts = unpack_queries_keys(back[:, :width], back[:, width:], k.grads[rows, 2 * width :])
    for number, part in enumerate(parts):
        target[:, number * width : (number + 1) * width] = part.astype(BF)


def backward_kernel(is_first, k):
    spot = k.spot
    block = 1 if is_first else 0
    spot.greet(spot.over_x, spot.over_z, spot.core, spot.over_y, spot.over_h, *((spot.partner,) if is_first else ()))
    gather, scatter, onward = Gather(spot, k.gather), Scatter(spot, k.local, k.one), Gather(spot, k.gather_next)
    rows_of = gather.span
    size = gather.held.shape[1]
    tokens = 8 * size
    keys = tokens if is_first else FRAME_TOK
    sums = [
        Total(spot, grad.at[rows], None if whole is None else whole.at[rows], refs)
        for (grad, whole), pieces in (
            ((k.down_grad, k.down_whole), zip(pieces_of(k.down_grad), k.down_total)),
            ((k.up_grad, k.up_whole if is_first else None), zip(pieces_of(k.up_grad), k.up_total)),
        )
        for rows, refs in pieces
    ]
    k.small[...] = jnp.zeros_like(k.small)
    if is_first:
        layer = Swap(spot, k.state, k.layer_out, k.swap)
        k.loads.cotangent.wait()
    else:
        above = Scatter(spot, k.local, k.two)
        qkv = Total(spot, k.qkv_grad, k.qkv_whole, k.qkv_total)
        out = Total(spot, k.out_grad_in, k.out_whole, k.out_total)
        out.start()
        k.loads.above_qkv.wait()
        k.loads.qkv_weight.wait()
        above.produce(lambda slot, stream: dot_rt(k.above_qkv[slot, rows_of(stream)], k.qkv_weight[...]))
        gathered = pltpu.make_async_copy(k.gathered, k.shared, k.pick.at[0])
        gathered.start()
        out.add()
        out.send_over()
        gathered.wait()
        qkv_weight_grad(k, k.shared)
        qkv.start()
        k.loads.above_hidden.wait()
        k.loads.above_middle_grad.wait()
    k.loads.branch_two.wait()
    for stream in range(2):
        rows = rows_of(stream)
        if is_first:
            grad = k.cotangent[rows].astype(F32) * k.weighting[rows, 0:1]
        else:
            normed, scale = norm_parts(k.above_hidden[rows])
            grad, gain_term, offset_term = norm_back(above.result(stream), k.gains[1, 0:1], normed, scale)
            k.small[6:7] += gain_term
            k.small[7:8] += offset_term
            grad = grad + k.above_middle_grad[rows]
        k.grad_rows[rows] = grad
        scaled = k.gains[block, 3:4] * grad
        gather.put(stream, scaled.astype(BF))
        k.small[0:1] += jnp.sum(grad * k.branch_two[rows], axis=0, keepdims=True)
        k.small[1:2] += jnp.sum(scaled, axis=0, keepdims=True)
        if stream == 0:
            if not is_first:
                above.relay(1)
            gather.pass_on(0)
    second = pltpu.make_async_copy(k.second, k.shared, k.pick.at[1])
    second.start()
    if is_first:
        middle_rows, branch_rows, fetched = k.middle, k.branch, [k.loads.middle, k.loads.branch]
    else:
        middle_rows, branch_rows = k.above_hidden, k.above_middle_grad
        fetched = [
            pltpu.make_async_copy(k.middle, middle_rows, k.pick.at[2]),
            pltpu.make_async_copy(k.branch, branch_rows, k.pick.at[3]),
        ]
        for copy in fetched:
            copy.start()
    if is_first:
        layer.start()
    else:
        above.finish()
        qkv.add()
        qkv.send_over()
        out.add_over()
        out.spread()
    k.loads.down_weight.wait()
    k.loads.up_weight.wait()
    k.loads.slope.wait()

    def term(slot, stream):
        slope = k.slope[slot, rows_of(stream)].astype(F32)
        up_rows = (dot_rt(gather.part(slot, stream), k.down_weight[...]) * slope).astype(BF)
        k.up_rows[slot, rows_of(stream)] = up_rows
        return dot_rt(up_rows, k.up_weight[...])

    scatter.produce_from(gather, term)
    gather.finish()
    for copy in fetched:
        copy.wait()
    k.loads.activated.wait()

    def down_piece(piece):
        cut = k.down_grad.shape[0] // 2
        lanes = slice(piece * cut, (piece + 1) * cut)
        rows = k.activated[:, :, lanes].reshape(tokens, cut)
        k.down_grad[lanes] = dot_lt(rows, wide(gather.held)).astype(BF)
        sums[piece].start()

    def up_piece(piece):
        cut = k.shared.shape[2] // 2
        lanes = slice(piece * cut, (piece + 1) * cut)
        rows = k.shared[:, :, lanes].reshape(tokens, cut)
        k.up_grad[lanes] = dot_lt(rows, wide(k.up_rows)).astype(BF)
        if piece == 1:
            total = jnp.sum(wide(k.up_rows).astype(F32), axis=0, keepdims=True)
            row = lax.broadcasted_iota(jnp.int32, (k.up_grad.shape[0] - 2 * cut, k.up_grad.shape[1]), 0)
            k.up_grad[2 * cut :] = jnp.where(row == 0, total, 0.0).astype(BF)
        sums[2 + piece].start()

    def leave_rows(stream):
        rows = rows_of(stream)
        normed, scale = norm_parts(middle_rows[rows])
        grad, gain_term, offset_term = norm_back(scatter.result(stream), k.gains[block, 1:2], normed, scale)
        grad = grad + k.grad_rows[rows]
        k.middle_grad[rows] = grad
        scaled = k.gains[block, 2:3] * grad
        onward.put(stream, scaled.astype(BF))
        k.small[2:3] += gain_term
        k.small[3:4] += offset_term
        k.small[4:5] += jnp.sum(grad * branch_rows[rows], axis=0, keepdims=True)
        k.small[5:6] += jnp.sum(scaled, axis=0, keepdims=True)

    down_piece(0)
    scatter.relay(1)
    leave_rows(0)
    down_piece(1)
    second.wait()
    up_piece(0)
    up_piece(1)
    if not is_first:
        gathered = pltpu.make_async_copy(k.gathered_first, k.shared, k.pick.at[0])
        gathered.start()
    onward.pass_on(0)
    leave_rows(1)
    if not is_first:
        qkv.add_over()
        qkv.spread()
        out.relay()
    k.saves.middle_grad()
    if not is_first:
        early = SmallSum(spot, k.early, k.early_sum)
        lanes = 4 * HD
        k.early[0:8] = k.small_first[...]
        k.early[8:16] = k.small[...]
        k.early[16:24] = jnp.zeros_like(k.early[16:24])
        k.early[16:17, :lanes] = k.head_first[0:1]
        k.early[16:17, lanes : 2 * lanes] = k.head_first[1:2]
        early.step(0)
    scatter.finish()
    k.loads.out_weight.wait()
    k.loads.qk_in.wait()
    k.loads.v_in.wait()
    k.loads.query.wait()
    k.loads.exact.wait()
    k.grads[...] = jnp.zeros_like(k.grads)

    def prepare(index, carry):
        prepare_keys(k, pl.ds(pl.multiple_of(index * size, size), size))
        return carry

    lax.fori_loop(0, 8, prepare, 0)

    def use(slot):
        grad = dot_rt(onward.held[slot], k.out_weight[...]).astype(BF).astype(F32)
        slice_back(k, keys, 1024, slot * size, size, grad)

    def visit(step, carry):
        for stream in range(2):
            onward.arrive(stream, step)
        use(spot.slot(spot.c, step))

        @pl.when(step == 0)
        def _():
            onward.pass_on(1)
            for part in sums[:2]:
                part.add()
                part.send_over()

        for stream in range(2):
            onward.arrive_core(stream, step)
        use(spot.slot(1 - spot.c, step))

        @pl.when(step == 0)
        def _():
            sums[2].add()
            sums[2].send_over()
            if not is_first:
                qkv.relay()
                early.step(1)

        @pl.when(step == 1)
        def _():
            sums[3].add()
            sums[3].send_over()
            sums[0].add_over()
            sums[0].spread()
            if not is_first:
                early.step(2)

        @pl.when(step == 2)
        def _():
            sums[1].add_over()
            sums[1].spread()
            if not is_first:
                early.step(3)

        @pl.when(step == 3)
        def _():
            sums[2].add_over()
            if is_first:
                sums[2].spread()
            sums[0].relay()
            sums[1].relay()
            if not is_first:
                early.step(4)

        return carry

    lax.fori_loop(0, 4, visit, 0)
    k.out_grad[...] = dot_lt(k.exact[...].astype(BF), wide(onward.held)).astype(BF)
    k.saves.out_grad()
    if not is_first:
        qkv.finish()
        out.finish()
    k.loads.raw_in.wait()
    k.head_small[...] = jnp.zeros_like(k.head_small)
    qkv_rows = k.qkv_rows if is_first else k.above_qkv

    def leave(index, carry):
        leave_heads(k, block, pl.ds(pl.multiple_of(index * size, size), size), qkv_rows.at[index])
        return carry

    lax.fori_loop(0, 8, leave, 0)
    k.saves.grad_qkv(qkv_rows)
    onward.finish()
    if is_first:
        layer.arrive()
        layer.finish()
        sums[3].add_over()
        sums[3].spread()
        for part in sums[2:]:
            part.relay()
        for part in sums:
            part.finish()
        return
    gathered.wait()
    qkv_weight_grad(k, k.shared)
    k.saves.qkv_grad_first(k.qkv_grad)
    early.step(5)
    sums[3].add_over()
    for part, save in zip(sums[2:], (k.saves.up_share, k.saves.up_share_later)):
        save(part.share)
        part.finish_first()
        part.finish_over()
    for part in sums[:2]:
        part.finish()


def last_kernel(k):
    spot = k.spot
    spot.greet(
        spot.over_x, spot.over_z, spot.core, spot.over_y, spot.over_h, spot.partner, *QuickSum.partners(spot)
    )
    scatter = Scatter(spot, k.local, k.one)
    out = Total(spot, k.out_grad_in, k.out_whole, k.out_total)
    qkv = Total(spot, k.qkv_grad, k.qkv_whole, k.qkv_total)
    cut = k.up_share.shape[0] * 2
    up = [
        Total(spot, None, k.up_whole.at[pl.ds(0, cut)], [None, k.up_share, None, k.up_total.at[0]]),
        Total(
            spot,
            None,
            k.up_whole.at[pl.ds(cut, k.up_whole.shape[0] - cut)],
            [None, k.up_share_later, None, k.up_total.at[1]],
        ),
    ]
    k.loads.qkv_grad.wait()
    k.loads.out_grad_in.wait()
    qkv.start()
    out.start()
    k.loads.qkv_weight.wait()
    k.loads.above_qkv.wait()
    scatter.produce(lambda slot, stream: dot_rt(k.above_qkv[slot, scatter.span(stream)], k.qkv_weight[...]))
    k.loads.up_share.wait()
    k.loads.up_share_later.wait()
    for part in up:
        part.spread()
    late = QuickSum(spot, k.late, k.late_sum)
    lanes = 4 * HD
    k.late[...] = jnp.zeros_like(k.late)
    k.late[2:3, :lanes] = k.head_later[0:1]
    k.late[2:3, lanes : 2 * lanes] = k.head_later[1:2]
    scatter.relay(1)
    for part in (qkv, out):
        part.add()
        part.send_over()
    k.loads.hidden.wait()
    k.loads.middle_grad.wait()
    for part in up:
        part.relay()
    swaps = []
    for stream in range(2):
        span = scatter.span(stream)
        normed, scale = norm_parts(k.hidden[span].astype(F32))
        grad, gain_term, offset_term = norm_back(scatter.result(stream), k.gains[0, 0:1], normed, scale)
        k.late[0:1] += gain_term
        k.late[1:2] += offset_term
        k.grad_in[span] = (grad + k.middle_grad[span]).astype(BF)
        swap = Swap(spot, k.grad_in.at[span], k.input_grad.at[span], k.swaps[stream])
        swap.start()
        swaps.append(swap)
    late.start()
    for part in (qkv, out):
        part.add_over()
        part.spread()
    late.step()
    qkv.relay()
    out.relay()
    late.end()
    for swap in swaps:
        swap.arrive()
        swap.finish()
    for part in (out, qkv):
        part.finish()
    for part in up:
        part.finish_spread()
    scatter.finish()


def gather_results(k):
    sums = (
        (k.down, k.saves.down, (k.down_first, k.down_later), (k.loads.down_first, k.loads.down_later), None),
        (k.up, k.saves.up, (k.up_first, k.up_later), (k.loads.up_first, k.loads.up_later), k.up_bias),
        (k.out, k.saves.out, (k.out_first, k.out_later), (k.loads.out_first, k.loads.out_later), None),
        (k.qkv, k.saves.qkv, (k.qkv_first, k.qkv_later), (k.loads.qkv_first, k.loads.qkv_later), k.qkv_bias),
    )
    for whole, save, parts, loads, bias in sums:
        size = whole.shape[1]
        for block in range(2):
            loads[block].wait()
            whole[block] = parts[block][:size].astype(F32)
            if bias is not None:
                bias[block : block + 1] = parts[block][size : size + 16][0:1].astype(F32)
        save()
    early, late = k.early[...], k.late[...]
    gains = (late[0:1], early[10:11], early[12:13], early[8:9], early[14:15], early[2:3], early[4:5], early[0:1])
    offsets = (late[1:2], early[11:12], early[13:14], early[9:10], early[15:16], early[3:4], early[5:6], early[1:2])
    for number in range(8):
        k.gain[number // 4, number % 4 : number % 4 + 1] = gains[number]
        k.offset[number // 4, number % 4 : number % 4 + 1] = offsets[number]
    for block, row in enumerate((late[2:3], early[16:17])):
        for kind, ref in enumerate((k.head_gain, k.head_offset)):
            for part in range(2):
                start = kind * 4 * HD + part * 2 * HD
                ref[block, part : part + 1] = row[:, start : start + HD] + row[:, start + HD : start + 2 * HD]


class Own:
    def __init__(self, own, level, got):
        self.own, self.level, self.got = own, level, got


class Load:
    def __init__(self, values):
        self.values = values


class Outside(Load):
    pass


INSIDE, APART, SAVED, TARGET = range(4)


def run(kernel, number, inputs, outputs, scratch):
    operands, in_specs = [], []
    vmem, outside = pl.BlockSpec(memory_space=pltpu.VMEM), pl.BlockSpec(memory_space=pl.ANY)
    loaded, places = {}, {}

    def give(values, spec):
        operands.append(values)
        in_specs.append(spec)
        return len(operands) - 1

    for key, value in inputs.items():
        if isinstance(value, Own):
            places[key] = (give(value.own, outside), give(value.got, outside))
            loaded[key] = value.own.shape[1:], value.own.dtype
        elif isinstance(value, Load):
            places[key] = give(value.values, outside)
            if not isinstance(value, Outside):
                loaded[key] = value.values.shape, value.values.dtype
        else:
            places[key] = give(value, vmem)
    out_keys = list(outputs)
    kinds = [outputs[key][1] for key in out_keys]
    saved = [key for key, kind in zip(out_keys, kinds) if kind in (SAVED, TARGET)]
    shapes = []

    def hold(item):
        if isinstance(item, list):
            return [hold(part) for part in item]
        shapes.append(item)
        return len(shapes) - 1

    layout = {key: hold(item) for key, item in scratch.items()}
    load_layout = {key: hold(pltpu.VMEM(size, kind)) for key, (size, kind) in loaded.items()}
    for key, kind in zip(out_keys, kinds):
        if kind == SAVED:
            layout[key] = hold(pltpu.VMEM(outputs[key][0].shape, outputs[key][0].dtype))
    load_at, save_at = hold(DMA((max(len(loaded), 1),))), hold(DMA((max(len(saved), 1),)))

    def whole(*refs):
        ins, rest = refs[: len(operands)], refs[len(operands) :]
        outs, held = rest[: len(out_keys)], rest[len(out_keys) :]

        def find(item):
            return [find(part) for part in item] if isinstance(item, list) else held[item]

        k = types.SimpleNamespace(**{key: find(item) for key, item in layout.items()})
        k.spot = None if number is None else Spot()
        saving = []
        loads, saves = {}, {}

        def saver(ref, target, sem):
            def save(source=ref):
                copy = pltpu.make_async_copy(source, target, sem)
                copy.start()
                saving.append(copy)

            return save

        for key, kind, out in zip(out_keys, kinds, outs):
            if kind in (INSIDE, APART):
                setattr(k, key, out)
            else:
                saves[key] = saver(getattr(k, key, None), out, held[save_at].at[saved.index(key)])
        for place, key in enumerate(loaded):
            target, sem = held[load_layout[key]], held[load_at].at[place]
            setattr(k, key, target)
            if isinstance(inputs[key], Own):
                own, got = (ins[at] for at in places[key])
                copy = pltpu.make_async_copy(got, target, sem)
                pl.when(k.spot.home)(pltpu.make_async_copy(own.at[inputs[key].level], target, sem).start)
                pl.when(k.spot.away)(copy.start)
            else:
                copy = pltpu.make_async_copy(ins[places[key]], target, sem)
                copy.start()
            loads[key] = copy
        for key in inputs:
            if key not in loaded:
                setattr(k, key, ins[places[key]])
        k.loads, k.saves = types.SimpleNamespace(**loads), types.SimpleNamespace(**saves)
        kernel(k)
        for copy in saving:
            copy.wait()

    found = pl.pallas_call(
        whole,
        name=getattr(kernel, "func", kernel).__name__,
        out_shape=[outputs[key][0] for key in out_keys],
        in_specs=in_specs,
        out_specs=[vmem if kind == INSIDE else outside for kind in kinds],
        scratch_shapes=shapes,
        compiler_params=pltpu.CompilerParams(
            collective_id=number, has_side_effects=number is not None, vmem_limit_bytes=VMEM_LIMIT
        ),
    )(*operands)
    return types.SimpleNamespace(**dict(zip(out_keys, found)))


def shape(*sizes):
    return jax.ShapeDtypeStruct(sizes[:-1], sizes[-1])


def square_body(
    frames_in,
    qkv_weight,
    qkv_bias,
    out_weight,
    up_weight,
    up_bias,
    down_weight,
    norm_gain,
    norm_offset,
    head_gain,
    head_offset,
    cotangent,
    visible,
    query_count,
):
    rows, width = frames_in.shape[1:]
    tokens = 8 * rows
    inner = 2 * HD
    units = up_weight.shape[2]
    gather = Gather.scratch(rows, width)
    local, scatter = Scatter.local(rows, width), Scatter.scratch(rows, width)
    pad = 32

    def moved(weight):
        return shape(*weight.shape[1:], BF), APART

    biases = jnp.concatenate([qkv_bias, up_bias], axis=1).astype(F32)
    biases = jnp.pad(biases, ((0, 6), (0, 0)))
    weighting = visible[0].astype(F32) * (query_count[0].astype(F32) / QMAX)
    weighting = jnp.broadcast_to(weighting[:, None], (rows, 128))
    head_gains, head_offsets = (
        jnp.concatenate([pair[:, 0], pair[:, 0], pair[:, 1], pair[:, 1]], axis=1) for pair in (head_gain, head_offset)
    )
    norms = dict(gains=norm_gain, offsets=norm_offset)
    heads = dict(head_gains=head_gains, head_offsets=head_offsets)
    def forward(is_last, inputs, outputs, scratch):
        block = 1 if is_last else 0
        return run(
            functools.partial(forward_kernel, is_last),
            1 + block,
            dict(up_own=Outside(up_weight), down_own=Outside(down_weight), **norms, **inputs),
            dict(
                exact=(shape(tokens, inner, F32), SAVED),
                query=(shape(2, tokens, inner, BF), SAVED),
                branch=(shape(rows, width, F32), SAVED),
                middle=(shape(rows, width, F32), SAVED),
                second=(shape(8, rows, width, BF), TARGET),
                activated=(shape(8, rows, units, BF), SAVED),
                slope=(shape(8, rows, units, BF), SAVED),
                branch_two=(shape(rows, width, F32), SAVED),
                state=(shape(rows, width, BF if is_last else F32), SAVED),
                up_got=moved(up_weight),
                down_got=moved(down_weight),
                **outputs,
            ),
            dict(
                local=local,
                one=scatter,
                two=scatter,
                gather=gather,
                pick=DMA((2,)),
                mixed=pltpu.VMEM((tokens, inner), BF),
                up_weight=pltpu.VMEM(up_weight.shape[1:], BF),
                down_weight=pltpu.VMEM(down_weight.shape[1:], BF),
                **scratch,
            ),
        )

    lower = forward(
        False,
        dict(
            frames=Outside(frames_in),
            own_biases=biases,
            qkv_own=Outside(qkv_weight),
            out_own=Outside(out_weight),
            cotangent=Outside(cotangent),
            weighting=weighting,
            **heads,
        ),
        dict(
            hidden=(shape(rows, width, BF), SAVED),
            biases=(shape(*biases.shape, F32), INSIDE),
            cotangent_here=(shape(rows, width, BF), APART),
            weighting_here=(shape(rows, 128, F32), APART),
            qkv_got=moved(qkv_weight),
            out_got=moved(out_weight),
            qkv_got_later=moved(qkv_weight),
            out_got_later=moved(out_weight),
            gathered_first=(shape(8, rows, width, BF), TARGET),
            raw_first=(shape(tokens, 2 * inner, F32), SAVED),
            qk_in=(shape(tokens, 2 * inner, BF), SAVED),
            v_in=(shape(tokens, inner, BF), SAVED),
            gathered=(shape(8, rows, width, BF), TARGET),
            raw=(shape(tokens, 2 * inner, F32), SAVED),
            qk=(shape(tokens, 2 * inner, BF), SAVED),
            v=(shape(tokens, inner, BF), SAVED),
        ),
        dict(
            gather_first=gather,
            gather_next=gather,
            swaps=[Swap.scratch] * 5,
            moves=[Move.scratch] * 6,
            qkv_weight=pltpu.VMEM(qkv_weight.shape[1:], BF),
            out_weight=pltpu.VMEM(out_weight.shape[1:], BF),
        ),
    )
    entry = types.SimpleNamespace(
        hidden=lower.hidden, gathered=lower.gathered_first, raw=lower.raw_first, qk=lower.qk_in, v=lower.v_in
    )
    between = types.SimpleNamespace(
        hidden=lower.state, gathered=lower.gathered, raw=lower.raw, qk=lower.qk, v=lower.v
    )
    upper = forward(
        True,
        dict(
            qk_in=Load(between.qk),
            v_in=Load(between.v),
            hidden=Load(between.hidden),
            biases=lower.biases,
            out_weight=Own(out_weight, 1, lower.out_got_later),
        ),
        dict(),
        dict(moves=[Move.scratch] * 2),
    )

    qkv_grad = pltpu.VMEM((width + pad, 3 * inner), BF)

    def in_pieces(size, lanes):
        cut = size // 64 * 32
        return [Total.scratch(cut, lanes), Total.scratch(size - cut, lanes)]

    qkv_whole = dict(qkv_whole=(shape(width + pad, 3 * inner, BF), APART))
    out_whole = dict(out_whole=(shape(inner, width, BF), APART))
    out_total = dict(out_total=Total.scratch(inner, width))

    def backward(is_first, came, kept, up_got, out_got, inputs, outputs, scratch):
        block = 1 if is_first else 0
        return run(
            functools.partial(backward_kernel, is_first),
            3 + block,
            dict(
                **inputs,
                branch_two=Load(kept.branch_two),
                down_weight=Own(down_weight, block, kept.down_got),
                up_weight=Own(up_weight, block, up_got),
                slope=Load(kept.slope),
                activated=Load(kept.activated),
                second=Outside(kept.second),
                out_weight=Own(out_weight, block, out_got),
                qk_in=Load(came.qk),
                v_in=Load(came.v),
                query=Load(kept.query),
                exact=Load(kept.exact),
                raw_in=Load(came.raw),
                gains=norm_gain,
                head_gains=head_gains,
            ),
            dict(
                middle_grad=(shape(rows, width, F32), SAVED),
                grad_qkv=(shape(8, rows, 3 * inner, BF), TARGET),
                down_whole=(shape(units, width, BF), APART),
                out_grad=(shape(inner, width, BF), SAVED),
                small=(shape(8, width, F32), INSIDE),
                head_small=(shape(2, 2 * inner, F32), INSIDE),
                **outputs,
            ),
            dict(
                local=local,
                one=scatter,
                gather=gather,
                gather_next=gather,
                up_rows=pltpu.VMEM((8, rows, units), BF),
                grad_rows=pltpu.VMEM((rows, width), F32),
                shared=pltpu.VMEM((8, rows, width), BF),
                pick=DMA((4,)),
                down_grad=pltpu.VMEM((units, width), BF),
                up_grad=pltpu.VMEM((width + pad, units), BF),
                down_total=in_pieces(units, width),
                up_total=in_pieces(width + pad, units),
                key_in=pltpu.VMEM((2, tokens, inner), BF),
                value_in=pltpu.VMEM((2, tokens, inner), BF),
                grad_in=pltpu.VMEM((2, rows, inner), BF),
                query_grad=pltpu.VMEM((rows, inner), F32),
                grads=pltpu.VMEM((tokens, 3 * inner), F32),
                **scratch,
            ),
        )

    upper_back = backward(
        True,
        between,
        upper,
        upper.up_got,
        lower.out_got_later,
        dict(
            cotangent=Load(lower.cotangent_here),
            weighting=lower.weighting_here,
            state=Outside(upper.state),
            middle=Load(upper.middle),
            branch=Load(upper.branch),
        ),
        dict(
            layer_out=(shape(rows, width, BF), APART),
            up_whole=(shape(width + pad, units, BF), APART),
        ),
        dict(swap=Swap.scratch, qkv_rows=pltpu.VMEM((8, rows, 3 * inner), BF)),
    )
    lower_back = backward(
        False,
        entry,
        lower,
        lower.up_got,
        lower.out_got,
        dict(
            above_qkv=Load(upper_back.grad_qkv),
            qkv_weight=Own(qkv_weight, 1, lower.qkv_got_later),
            gathered=Outside(between.gathered),
            gathered_first=Outside(entry.gathered),
            above_hidden=Load(between.hidden),
            above_middle_grad=Load(upper_back.middle_grad),
            out_grad_in=upper_back.out_grad,
            middle=Outside(lower.middle),
            branch=Outside(lower.branch),
            small_first=upper_back.small,
            head_first=upper_back.head_small,
        ),
        dict(
            early=(shape(24, width, F32), INSIDE),
            up_share=(shape((width + pad) // 64 * 16, units, BF), TARGET),
            up_share_later=(shape((width + pad) // 2 - (width + pad) // 64 * 16, units, BF), TARGET),
            qkv_grad_first=(shape(width + pad, 3 * inner, BF), TARGET),
            **qkv_whole,
            **out_whole,
        ),
        dict(
            early_sum=SmallSum.scratch(24, width),
            two=scatter,
            qkv_grad=qkv_grad, qkv_total=Total.scratch(width + pad, 3 * inner), **out_total),
    )
    last = run(
        last_kernel,
        5,
        dict(
            above_qkv=Load(lower_back.grad_qkv),
            qkv_weight=Own(qkv_weight, 0, lower.qkv_got),
            hidden=Load(entry.hidden),
            middle_grad=Load(lower_back.middle_grad),
            out_grad_in=Load(lower_back.out_grad),
            qkv_grad=Load(lower_back.qkv_grad_first),
            up_share=Load(lower_back.up_share),
            up_share_later=Load(lower_back.up_share_later),
            gains=norm_gain,
            head_later=lower_back.head_small,
        ),
        dict(
            input_grad=(shape(rows, width, BF), APART),
            late=(shape(8, width, F32), INSIDE),
            up_whole=(shape(width + pad, units, BF), APART),
            **qkv_whole,
            **out_whole,
        ),
        dict(
            local=local,
            one=scatter,
            grad_in=pltpu.VMEM((rows, width), BF),
            swaps=[Swap.scratch] * 2,
            late_sum=QuickSum.scratch(8, width),
            qkv_total=Total.scratch(width + pad, 3 * inner),
            **out_total,
            up_total=DMA((2, 11)),
        ),
    )
    found = run(
        gather_results,
        None,
        dict(
            down_first=Load(lower_back.down_whole),
            down_later=Load(upper_back.down_whole),
            up_first=Load(last.up_whole),
            up_later=Load(upper_back.up_whole),
            out_first=Load(last.out_whole),
            out_later=Load(lower_back.out_whole),
            qkv_first=Load(last.qkv_whole),
            qkv_later=Load(lower_back.qkv_whole),
            early=lower_back.early,
            late=last.late,
        ),
        dict(
            qkv=(shape(2, width, 3 * inner, F32), SAVED),
            qkv_bias=(shape(2, 3 * inner, F32), INSIDE),
            out=(shape(2, inner, width, F32), SAVED),
            up=(shape(2, width, units, F32), SAVED),
            up_bias=(shape(2, units, F32), INSIDE),
            down=(shape(2, units, width, F32), SAVED),
            gain=(shape(2, 4, width, F32), INSIDE),
            offset=(shape(2, 4, width, F32), INSIDE),
            head_gain=(shape(2, 2, HD, F32), INSIDE),
            head_offset=(shape(2, 2, HD, F32), INSIDE),
        ),
        dict(),
    )
    return (
        upper_back.layer_out[None],
        last.input_grad[None],
        found.qkv,
        found.qkv_bias,
        found.out,
        found.up,
        found.up_bias,
        found.down,
        found.gain,
        found.offset,
        found.head_gain,
        found.head_offset,
    )


TP = ("c", "r")


def exchange(values):
    return lax.ppermute(values, ("c", "h"), [(0, 0), (1, 2), (2, 1), (3, 3)])


def layer_norm(values, norm_scale, norm_bias):
    average = jnp.mean(values, axis=-1, keepdims=True)
    centered = values - average
    variance = jnp.mean(centered * centered, axis=-1, keepdims=True)
    return centered * lax.rsqrt(variance + EPSILON) * norm_scale + norm_bias


def exact_gelu(values):
    return jax.nn.gelu(values, approximate=False)


def attend_rows(query_rows, key_rows, value_rows, score_scale):
    scores = (
        jnp.einsum("qhe,khe->hqk", query_rows, key_rows, preferred_element_type=jnp.float32)
        * score_scale
    )
    largest = jnp.max(scores, axis=-1, keepdims=True)
    unnormed = jnp.exp(scores - largest)
    denominator = jnp.sum(unnormed, axis=-1, keepdims=True)
    weights = (unnormed / denominator).astype(jnp.bfloat16)
    mixed = jnp.einsum("hqk,khe->qhe", weights, value_rows, preferred_element_type=jnp.float32)
    return (mixed, (largest + jnp.log(denominator))[:, :, 0])


def attend_back(query_rows, key_rows, value_rows, log_total, grad_rows, score_scale):
    scores = (
        jnp.einsum("qhe,khe->hqk", query_rows, key_rows, preferred_element_type=jnp.float32)
        * score_scale
    )
    probs = jnp.exp(scores - log_total[:, :, None])
    grad_probs = jnp.einsum(
        "qhe,khe->hqk", grad_rows, value_rows, preferred_element_type=jnp.float32
    )
    grad_scores = probs * (grad_probs - jnp.sum(probs * grad_probs, axis=-1, keepdims=True))
    grad_scores = grad_scores.astype(jnp.bfloat16)
    grad_query = (
        jnp.einsum("hqk,khe->qhe", grad_scores, key_rows, preferred_element_type=jnp.float32)
        * score_scale
    )
    grad_key = (
        jnp.einsum("hqk,qhe->khe", grad_scores, query_rows, preferred_element_type=jnp.float32)
        * score_scale
    )
    grad_value = jnp.einsum(
        "hqk,qhe->khe", probs.astype(jnp.bfloat16), grad_rows, preferred_element_type=jnp.float32
    )
    return (grad_query, grad_key, grad_value)


def attention_forward(queries, key_all, value_all, frame_only, score_scale):
    frame_shape = (queries.shape[0] // FRAME_TOK, FRAME_TOK) + queries.shape[1:]
    query_frames = queries.reshape(frame_shape)
    if frame_only:
        mixed, log_total = lax.map(
            lambda triple: attend_rows(triple[0], triple[1], triple[2], score_scale),
            (query_frames, key_all.reshape(frame_shape), value_all.reshape(frame_shape)),
        )
    else:
        mixed, log_total = lax.map(
            lambda query_block: attend_rows(query_block, key_all, value_all, score_scale),
            query_frames,
        )
    return (mixed.reshape(queries.shape), log_total)


def attention_backward(queries, key_all, value_all, log_total, grad_mixed, frame_only, score_scale):
    frame_shape = (queries.shape[0] // FRAME_TOK, FRAME_TOK) + queries.shape[1:]
    query_frames = queries.reshape(frame_shape)
    grad_frames = grad_mixed.reshape(frame_shape)
    if frame_only:
        grad_query, grad_key, grad_value = lax.map(
            lambda group_in: attend_back(
                group_in[0], group_in[1], group_in[2], group_in[3], group_in[4], score_scale
            ),
            (
                query_frames,
                key_all.reshape(frame_shape),
                value_all.reshape(frame_shape),
                log_total,
                grad_frames,
            ),
        )
        return (
            grad_query.reshape(queries.shape),
            grad_key.reshape(queries.shape),
            grad_value.reshape(queries.shape),
        )

    def visit_frame(running, group_in):
        grad_query, grad_key, grad_value = attend_back(
            group_in[0], key_all, value_all, group_in[1], group_in[2], score_scale
        )
        return ((running[0] + grad_key, running[1] + grad_value), grad_query)

    zero_keys = jnp.zeros(key_all.shape, jnp.float32)
    (grad_key, grad_value), grad_query = lax.scan(
        visit_frame, (zero_keys, zero_keys), (query_frames, log_total, grad_frames)
    )
    return (grad_query.reshape(queries.shape), grad_key, grad_value)


def any_body(
    frames_in,
    qkv_weight,
    qkv_bias,
    out_weight,
    up_weight,
    up_bias,
    down_weight,
    norm_gain,
    norm_offset,
    head_gain,
    head_offset,
    cotangent,
    visible,
    query_count,
):
    score_scale = HD ** (-0.5)
    frames = exchange(frames_in[0])
    qkv_weight, out_weight, up_weight, down_weight, qkv_bias, up_bias = (
        [exchange(stacked[block_index]) for block_index in range(2)]
        for stacked in (qkv_weight, out_weight, up_weight, down_weight, qkv_bias, up_bias)
    )
    weighting = visible[0].astype(jnp.float32) * (query_count[0].astype(jnp.float32) / QMAX)
    weighting = exchange(weighting)
    cotangent = exchange(cotangent[0])

    def backward_block(grad_out, block_index, frame_only, saved):
        (
            hidden,
            gathered,
            split,
            queries,
            key_all,
            value_all,
            log_total,
            mixed_flat,
            branch,
            middle,
            gathered_two,
            hidden_up,
            activated,
            branch_two,
        ) = saved
        gains = norm_gain[block_index]
        offsets = norm_offset[block_index]
        total_rows = split.shape[0]
        grad_branch_two = gains[3] * grad_out
        offset_grad_three = jnp.sum(grad_branch_two, axis=0)
        gain_grad_three = jnp.sum(grad_out * branch_two, axis=0)
        shard_rows = lax.all_gather(grad_branch_two.astype(jnp.bfloat16), TP, axis=0, tiled=True)
        down_grad = jnp.einsum(
            "tf,td->fd", activated, shard_rows, preferred_element_type=jnp.float32
        )
        act_grad = jnp.einsum(
            "td,fd->tf", shard_rows, down_weight[block_index], preferred_element_type=jnp.float32
        )
        up_grad = jax.vjp(exact_gelu, hidden_up)[1](act_grad)[0].astype(jnp.bfloat16)
        down_grad, up_grads = (down_grad, up_grad)
        up_weight_grad = jnp.einsum(
            "td,tf->df", gathered_two, up_grads, preferred_element_type=jnp.float32
        )
        up_bias_grad = jnp.sum(up_grads.astype(jnp.float32), axis=0)
        second_grad = lax.psum_scatter(
            jnp.einsum(
                "tf,df->td", up_grads, up_weight[block_index], preferred_element_type=jnp.float32
            ).astype(jnp.bfloat16),
            TP,
            scatter_dimension=0,
            tiled=True,
        ).astype(jnp.float32)
        middle_grad, gain_grad_one, offset_grad_one = jax.vjp(
            layer_norm, middle, gains[1], offsets[1]
        )[1](second_grad)
        middle_grad = middle_grad + grad_out
        grad_branch = gains[2] * middle_grad
        offset_grad_two = jnp.sum(grad_branch, axis=0)
        gain_grad_two = jnp.sum(middle_grad * branch, axis=0)
        shard_rows = lax.all_gather(grad_branch.astype(jnp.bfloat16), TP, axis=0, tiled=True)
        out_grad = jnp.einsum(
            "tc,td->cd", mixed_flat, shard_rows, preferred_element_type=jnp.float32
        )
        mixed_grad = jnp.einsum(
            "td,cd->tc", shard_rows, out_weight[block_index], preferred_element_type=jnp.float32
        ).astype(jnp.bfloat16)
        out_grad, mixed_grads = (out_grad, mixed_grad)
        grad_query, grad_key, grad_value = attention_backward(
            queries,
            key_all,
            value_all,
            log_total,
            mixed_grads.reshape(queries.shape),
            frame_only,
            score_scale,
        )
        raw_query_grad, query_gain_grad, query_offset_grad = jax.vjp(
            layer_norm, split[:, :, 0], head_gain[block_index, 0], head_offset[block_index, 0]
        )[1](grad_query)
        raw_key_grad, key_gain_grad, key_offset_grad = jax.vjp(
            layer_norm, split[:, :, 1], head_gain[block_index, 1], head_offset[block_index, 1]
        )[1](grad_key)
        projected_grad = (
            jnp.stack([raw_query_grad, raw_key_grad, grad_value], axis=2)
            .reshape(total_rows, -1)
            .astype(jnp.bfloat16)
        )
        qkv_weight_grad = jnp.einsum(
            "td,tc->dc", gathered, projected_grad, preferred_element_type=jnp.float32
        )
        qkv_bias_grad = jnp.sum(projected_grad.astype(jnp.float32), axis=0)
        normed_grad = lax.psum_scatter(
            jnp.einsum(
                "tc,dc->td",
                projected_grad,
                qkv_weight[block_index],
                preferred_element_type=jnp.float32,
            ).astype(jnp.bfloat16),
            TP,
            scatter_dimension=0,
            tiled=True,
        ).astype(jnp.float32)
        hidden_grad, gain_grad_zero, offset_grad_zero = jax.vjp(
            layer_norm, hidden, gains[0], offsets[0]
        )[1](normed_grad)
        hidden_grad = hidden_grad + middle_grad
        large_grads = (
            qkv_weight_grad,
            qkv_bias_grad,
            out_grad,
            up_weight_grad,
            up_bias_grad,
            down_grad,
        )
        small_grads = (
            jnp.stack([gain_grad_zero, gain_grad_one, gain_grad_two, gain_grad_three]),
            jnp.stack([offset_grad_zero, offset_grad_one, offset_grad_two, offset_grad_three]),
            jnp.stack([query_gain_grad, key_gain_grad]),
            jnp.stack([query_offset_grad, key_offset_grad]),
        )
        return (hidden_grad, large_grads, small_grads)

    hidden = frames.astype(jnp.float32)
    kept_states = []
    for block_index in range(2):
        forward_frame_only = block_index == 0
        forward_gains = norm_gain[block_index]
        forward_offsets = norm_offset[block_index]
        normed = layer_norm(hidden, forward_gains[0], forward_offsets[0]).astype(jnp.bfloat16)
        forward_gathered = lax.all_gather(normed, TP, axis=0, tiled=True)
        projected = jnp.dot(
            forward_gathered, qkv_weight[block_index], preferred_element_type=jnp.float32
        )
        projected = projected + qkv_bias[block_index].astype(jnp.float32)
        forward_total_rows = projected.shape[0]
        forward_split = projected.reshape(forward_total_rows, -1, 3, HD)
        forward_queries = layer_norm(
            forward_split[:, :, 0], head_gain[block_index, 0], head_offset[block_index, 0]
        ).astype(jnp.bfloat16)
        forward_key_all = layer_norm(
            forward_split[:, :, 1], head_gain[block_index, 1], head_offset[block_index, 1]
        ).astype(jnp.bfloat16)
        forward_value_all = forward_split[:, :, 2].astype(jnp.bfloat16)
        mixed, forward_log_total = attention_forward(
            forward_queries, forward_key_all, forward_value_all, forward_frame_only, score_scale
        )
        forward_mixed_flat = mixed.reshape(forward_total_rows, -1).astype(jnp.bfloat16)
        forward_branch = (
            lax.psum_scatter(
                jnp.dot(
                    forward_mixed_flat, out_weight[block_index], preferred_element_type=jnp.float32
                ).astype(jnp.bfloat16),
                TP,
                scatter_dimension=0,
                tiled=True,
            ).astype(jnp.float32)
            + forward_offsets[2]
        )
        forward_middle = hidden + forward_gains[2] * forward_branch
        second = layer_norm(forward_middle, forward_gains[1], forward_offsets[1]).astype(
            jnp.bfloat16
        )
        forward_gathered_two = lax.all_gather(second, TP, axis=0, tiled=True)
        forward_hidden_up = jnp.dot(
            forward_gathered_two, up_weight[block_index], preferred_element_type=jnp.float32
        )
        forward_hidden_up = forward_hidden_up + up_bias[block_index].astype(jnp.float32)
        forward_activated = exact_gelu(forward_hidden_up).astype(jnp.bfloat16)
        forward_branch_two = (
            lax.psum_scatter(
                jnp.dot(
                    forward_activated, down_weight[block_index], preferred_element_type=jnp.float32
                ).astype(jnp.bfloat16),
                TP,
                scatter_dimension=0,
                tiled=True,
            ).astype(jnp.float32)
            + forward_offsets[3]
        )
        result = forward_middle + forward_gains[3] * forward_branch_two
        forward_saved = (
            hidden,
            forward_gathered,
            forward_split,
            forward_queries,
            forward_key_all,
            forward_value_all,
            forward_log_total,
            forward_mixed_flat,
            forward_branch,
            forward_middle,
            forward_gathered_two,
            forward_hidden_up,
            forward_activated,
            forward_branch_two,
        )
        hidden = result
        saved = forward_saved
        kept_states.append(saved)
    layer_out = exchange(hidden.astype(jnp.bfloat16))[None]
    grad_hidden = cotangent.astype(jnp.float32) * weighting[:, None]
    grad_hidden, large_one, small_one = backward_block(grad_hidden, 1, False, kept_states[1])
    grad_hidden, large_zero, small_zero = backward_block(grad_hidden, 0, True, kept_states[0])
    input_grad = exchange(grad_hidden.astype(jnp.bfloat16))[None]

    def over_scenes(grads):
        shapes = [grad.shape for grad in grads]
        parts = lax.axis_size("sy")
        flat = [grad.astype(jnp.bfloat16).reshape(parts, -1) for grad in grads]
        sizes = [part.shape[1] for part in flat]
        joined = jnp.concatenate(flat, axis=1)
        share = lax.psum_scatter(joined, "sy", scatter_dimension=0, tiled=True)
        share = lax.psum(share, "h")
        whole = exchange(lax.all_gather(share, "sy", axis=0, tiled=True))
        found = []
        start = 0
        for shape, size in zip(shapes, sizes):
            found.append(whole[:, start : start + size].reshape(shape).astype(jnp.float32))
            start += size
        return found

    summed_one = over_scenes(large_one)
    summed_zero = over_scenes(large_zero)
    summed = [jnp.stack(pair) for pair in zip(summed_zero, summed_one)]
    small = jax.tree.map(lambda first, later: jnp.stack([first, later]), small_zero, small_one)
    summed = tuple(summed) + tuple(lax.psum(small, ("sy", "c", "h", "r")))
    return (
        layer_out,
        input_grad,
        summed[0],
        summed[1],
        summed[2],
        summed[3],
        summed[4],
        summed[5],
        summed[6],
        summed[7],
        summed[8],
        summed[9],
    )


def solution(mesh):
    scenes, shards = mesh.shape["scene"], mesh.shape["tp"]
    if (scenes, shards) == (4, 8):
        body, sizes, axes, tp = square_body, (2, 2, 2, 2, 2), AXES, ("h", "zl", "x")
    else:
        body, sizes, axes, tp = any_body, (scenes // 2, 2, 2, shards // 2), ("sy", "c", "h", "r"), ("h", "r")
    scene = ("sy", "c")
    return jax.shard_map(
        body,
        mesh=jax.sharding.Mesh(mesh.devices.reshape(sizes), axes),
        in_specs=(
            P(scene, tp, None),
            P(None, None, tp),
            P(None, tp),
            P(None, tp, None),
            P(None, None, tp),
            P(None, tp),
            P(None, tp, None),
            P(),
            P(),
            P(),
            P(),
            P(scene, tp, None),
            P(scene, tp),
            P(scene),
        ),
        out_specs=(
            P(scene, tp, None),
            P(scene, tp, None),
            P(None, None, tp),
            P(None, tp),
            P(None, tp, None),
            P(None, None, tp),
            P(None, tp),
            P(None, tp, None),
            P(),
            P(),
            P(),
            P(),
        ),
        check_vma=False,
    )
```

```python
import functools
import types

import jax
import jax.numpy as jnp
from jax import lax
from jax.experimental import pallas as pl
from jax.experimental.pallas import tpu as pltpu
from jax.sharding import PartitionSpec as P

HD = 64
QMAX = 512
FRAME_TOK = 1024
EPSILON = 1e-06
BF = jnp.bfloat16
F32 = jnp.float32
MESH = pl.DeviceIdType.MESH
DMA = pltpu.SemaphoreType.DMA
VMEM_LIMIT = 63 * 1024 * 1024

AXES = ("sy", "c", "h", "zl", "x")


def dot(left, right):
    return lax.dot_general(left, right, (((1,), (0,)), ((), ())), preferred_element_type=F32)


def dot_rt(left, right):
    return lax.dot_general(left, right, (((1,), (1,)), ((), ())), preferred_element_type=F32)


def dot_lt(left, right):
    return lax.dot_general(left, right, (((0,), (0,)), ((), ())), preferred_element_type=F32)


def dot_fine(left, right):
    high = left.astype(BF)
    return dot(high, right) + dot((left - high.astype(F32)).astype(BF), right)


def remote(source, target, send, recv, device):
    return pltpu.make_async_remote_copy(
        src_ref=source, dst_ref=target, send_sem=send, recv_sem=recv, device_id=device, device_id_type=MESH
    )


class Spot:
    def __init__(self):
        self.sy, self.c, self.h, self.zl, self.x = (lax.axis_index(name) for name in AXES)
        self.over_x = dict(x=1 - self.x)
        self.over_z = dict(zl=1 - self.zl)
        self.core = dict(c=1 - self.c)
        self.over_y = dict(sy=1 - self.sy)
        self.over_h = dict(h=1 - self.h)
        self.partner = dict(c=1 - self.c, h=1 - self.h)
        self.home = self.c == self.h
        self.away = self.c != self.h

    def greet(self, *devices):
        barrier = pltpu.get_barrier_semaphore()
        for device in devices:
            pl.semaphore_signal(barrier, inc=1, device_id=device, device_id_type=MESH)
        pl.semaphore_wait(barrier, len(devices))

    def slot(self, core, step):
        zl = lax.rem(self.zl + step // 2, 2)
        x = lax.rem(self.x + step % 2, 2)
        return core * 4 + zl * 2 + x

    def part(self, size, own=True, piece=0, pieces=1):
        half = size // 2
        rows = half // pieces
        return pl.ds(pl.multiple_of((self.sy if own else 1 - self.sy) * half + piece * rows, rows), rows)


class Gather:
    @staticmethod
    def scratch(rows, width):
        return [pltpu.VMEM((8, rows, width), BF), DMA((2, 6)), DMA((2, 6)), DMA((2, 4)), DMA((2, 4))]

    def __init__(self, spot, refs):
        self.spot = spot
        self.held, self.send, self.recv, self.core_send, self.core_recv = refs
        self.rows = self.held.shape[1] // 2

    def link(self, stream, step, part, number, device):
        half = self.rows // 2
        start = pl.multiple_of(stream * self.rows + part * half, half)
        ref = self.held.at[self.spot.slot(self.spot.c, step), pl.ds(start, half)]
        return remote(ref, ref, self.send.at[stream, number], self.recv.at[stream, number], device)

    def x_first(self, stream):
        return self.link(stream, 0, 0, 0, self.spot.over_x)

    def x_later(self, stream):
        return self.link(stream, 0, 1, 1, self.spot.over_x)

    def z_later(self, stream):
        return self.link(stream, 0, 0, 2, self.spot.over_z)

    def z_first(self, stream):
        return self.link(stream, 0, 1, 3, self.spot.over_z)

    def z_relay(self, stream):
        return self.link(stream, 1, 0, 4, self.spot.over_z)

    def x_relay(self, stream):
        return self.link(stream, 2, 1, 5, self.spot.over_x)

    def core_copy(self, stream, step):
        ref = self.held.at[self.spot.slot(self.spot.c, step), self.span(stream)]
        return remote(
            ref, ref, self.core_send.at[stream, step], self.core_recv.at[stream, step], self.spot.core
        )

    def span(self, stream):
        return pl.ds(pl.multiple_of(stream * self.rows, self.rows), self.rows)

    def part(self, slot, stream):
        return self.held[slot, self.span(stream)]

    def put(self, stream, values):
        self.held[self.spot.slot(self.spot.c, 0), self.span(stream)] = values
        self.x_first(stream).start()
        self.z_first(stream).start()
        self.core_copy(stream, 0).start()
        self.z_later(stream).start()
        self.x_later(stream).start()

    def pass_on(self, stream):
        self.x_first(stream).wait_recv()
        self.z_relay(stream).start()
        self.z_first(stream).wait_recv()
        self.x_relay(stream).start()

    def arrive(self, stream, step):
        pl.when(step == 1)(lambda: self.x_later(stream).wait_recv())
        pl.when(step == 2)(lambda: self.z_later(stream).wait_recv())

        @pl.when(step == 3)
        def _():
            self.z_relay(stream).wait_recv()
            self.x_relay(stream).wait_recv()

        pl.when(step > 0)(lambda: self.core_copy(stream, step).start())

    def arrive_core(self, stream, step):
        self.core_copy(stream, step).wait_recv()

    def finish(self):
        for stream in range(2):
            for copy in (self.x_first, self.x_later, self.z_first, self.z_later, self.z_relay, self.x_relay):
                copy(stream).wait_send()
            for step in range(4):
                self.core_copy(stream, step).wait_send()

    def consume(self, use, passed=0, before=None):
        def visit(index, carry):
            stream, step = index // 4, lax.rem(index, 4)
            if before is not None:
                before(index)
            self.arrive(stream, step)
            use(self.spot.slot(self.spot.c, step), stream)
            pl.when((index >= passed) & (index < 2))(lambda: self.pass_on(index))
            self.arrive_core(stream, step)
            use(self.spot.slot(1 - self.spot.c, step), stream)
            return carry

        lax.fori_loop(0, 8, visit, 0)


class Scatter:
    @staticmethod
    def local(rows, width):
        return [
            pltpu.VMEM((4, rows, width), BF),
            pltpu.VMEM((4, rows, width), BF),
            pltpu.VMEM((2, 2, rows // 4, width), BF),
        ]

    @staticmethod
    def scratch(rows, width):
        return [
            pltpu.VMEM((4, rows, width), BF),
            pltpu.VMEM((2, 6, rows // 4, width), BF),
            DMA((2, 4)),
            DMA((2, 4)),
            DMA((2, 6)),
            DMA((2, 6)),
        ]

    def __init__(self, spot, local, refs):
        self.spot = spot
        self.for_core, self.ready, self.relayed = local
        self.from_core, self.landed, self.core_send, self.core_recv, self.send, self.recv = refs
        self.rows = self.for_core.shape[1] // 2

    def span(self, stream):
        return pl.ds(pl.multiple_of(stream * self.rows, self.rows), self.rows)

    def half(self, stream, part):
        half = self.rows // 2
        return pl.ds(pl.multiple_of(stream * self.rows + part * half, half), half)

    def link(self, source, stream, number, device):
        return remote(
            source, self.landed.at[stream, number], self.send.at[stream, number], self.recv.at[stream, number], device
        )

    def x_near(self, stream):
        return self.link(self.ready.at[1, self.half(stream, 0)], stream, 0, self.spot.over_x)

    def x_far(self, stream):
        return self.link(self.ready.at[3, self.half(stream, 0)], stream, 1, self.spot.over_x)

    def z_near(self, stream):
        return self.link(self.ready.at[2, self.half(stream, 1)], stream, 2, self.spot.over_z)

    def z_far(self, stream):
        return self.link(self.ready.at[3, self.half(stream, 1)], stream, 3, self.spot.over_z)

    def z_relay(self, stream):
        return self.link(self.relayed.at[stream, 0], stream, 4, self.spot.over_z)

    def x_relay(self, stream):
        return self.link(self.relayed.at[stream, 1], stream, 5, self.spot.over_x)

    def core_copy(self, stream, step):
        span = self.span(stream)
        return remote(
            self.for_core.at[step, span],
            self.from_core.at[step, span],
            self.core_send.at[stream, step],
            self.core_recv.at[stream, step],
            self.spot.core,
        )

    def put_other(self, stream, step, values):
        self.for_core[step, self.span(stream)] = values.astype(BF)
        self.core_copy(stream, step).start()

    def put_own(self, stream, step, values):
        self.ready[step, self.span(stream)] = values.astype(BF)

    def flush(self, stream, step):
        self.core_copy(stream, step).wait_recv()
        span = self.span(stream)
        total = self.ready[step, span].astype(F32) + self.from_core[step, span].astype(F32)
        self.ready[step, span] = total.astype(BF)

        pl.when(step == 1)(lambda: self.x_near(stream).start())
        pl.when(step == 2)(lambda: self.z_near(stream).start())

        @pl.when(step == 3)
        def _():
            self.x_far(stream).start()
            self.z_far(stream).start()

    def relay(self, stream):
        self.x_far(stream).wait_recv()
        mine = self.ready[2, self.half(stream, 0)].astype(F32)
        self.relayed[stream, 0] = (mine + self.landed[stream, 1].astype(F32)).astype(BF)
        self.z_relay(stream).start()
        self.z_far(stream).wait_recv()
        mine = self.ready[1, self.half(stream, 1)].astype(F32)
        self.relayed[stream, 1] = (mine + self.landed[stream, 3].astype(F32)).astype(BF)
        self.x_relay(stream).start()

    def result(self, stream):
        self.x_near(stream).wait_recv()
        self.z_near(stream).wait_recv()
        self.z_relay(stream).wait_recv()
        self.x_relay(stream).wait_recv()
        landed = lambda number: self.landed[stream, number].astype(F32)
        return self.ready[0, self.span(stream)].astype(F32) + jnp.concatenate(
            [landed(0) + landed(4), landed(2) + landed(5)], axis=0
        )

    def finish(self):
        for stream in range(2):
            for copy in (self.x_near, self.x_far, self.z_near, self.z_far, self.z_relay, self.x_relay):
                copy(stream).wait_send()
            for step in range(4):
                self.core_copy(stream, step).wait_send()

    def produce(self, term, before=None):
        spot = self.spot

        def visit(index, carry):
            stream, step = index // 4, 3 - lax.rem(index, 4)
            if before is not None:
                before(index)
            self.put_other(stream, step, term(spot.slot(1 - spot.c, step), stream))

            @pl.when(index > 0)
            def _():
                pl.when(index == 5)(lambda: self.relay(0))
                self.flush((index - 1) // 4, 3 - lax.rem(index - 1, 4))

            self.put_own(stream, step, term(spot.slot(spot.c, step), stream))
            return carry

        lax.fori_loop(0, 8, visit, 0)
        self.flush(1, 0)

    def produce_from(self, gather, term, passed=1):
        spot = self.spot

        def visit(index, carry):
            stream, step = index // 4, lax.rem(index, 4)
            gather.arrive(stream, step)
            self.put_own(stream, step, term(spot.slot(spot.c, step), stream))
            pl.when((index >= passed) & (index < 2))(lambda: gather.pass_on(index))
            gather.arrive_core(stream, step)
            self.put_other(stream, step, term(spot.slot(1 - spot.c, step), stream))

            @pl.when(index > 0)
            def _():
                pl.when(index == 6)(lambda: self.relay(0))
                self.flush((index - 1) // 4, lax.rem(index - 1, 4))

            return carry

        lax.fori_loop(0, 8, visit, 0)
        self.flush(1, 3)


class Swap:
    scratch = [DMA((2,))]

    def __init__(self, spot, source, target, refs):
        (sems,) = refs
        self.spot = spot
        self.local = pltpu.make_async_copy(source, target, sems.at[0])
        self.copy = remote(source, target, sems.at[0], sems.at[1], spot.partner)

    def start(self):
        pl.when(self.spot.home)(self.local.start)
        pl.when(self.spot.away)(self.copy.start)

    def arrive(self):
        pl.when(self.spot.home)(self.local.wait)
        pl.when(self.spot.away)(self.copy.wait_recv)

    def finish(self):
        pl.when(self.spot.away)(self.copy.wait_send)


class Move:
    scratch = [DMA((2, 4))]

    def __init__(self, spot, own, got, refs):
        (sems,) = refs
        self.spot, self.own, self.got = spot, own, got
        self.over, self.along = [], []
        for piece in range(2):
            rows = spot.part(got.shape[0], True, piece, 2)
            at = sems.at[piece]
            self.over.append(remote(own.at[rows], got.at[rows], at.at[0], at.at[1], spot.over_h))
            self.along.append(remote(got.at[rows], got.at[rows], at.at[2], at.at[3], spot.over_y))

    def start(self):
        @pl.when(self.spot.home)
        def _():
            for copy in self.over:
                copy.start()

    def relay(self, piece):
        @pl.when(self.spot.away)
        def _():
            self.over[piece].wait_recv()
            self.along[piece].start()

    def finish(self):
        @pl.when(self.spot.away)
        def _():
            for copy in self.along:
                copy.wait_recv()
                copy.wait_send()

        @pl.when(self.spot.home)
        def _():
            for copy in self.over:
                copy.wait_send()

    def pick(self, target, sem):
        copy = pltpu.make_async_copy(self.got, target, sem)
        pl.when(self.spot.home)(pltpu.make_async_copy(self.own, target, sem).start)
        pl.when(self.spot.away)(copy.start)
        return copy


class Total:
    @staticmethod
    def scratch(rows, width):
        half = pltpu.VMEM((rows // 2, width), BF)
        return [half, half, half, DMA((11,))]

    def __init__(self, spot, grad, whole, refs):
        self.landed, self.share, self.later_landed, sems = refs
        self.grad, self.spot = grad, spot
        share = self.share
        if grad is not None:
            other = grad.at[spot.part(grad.shape[0], False)]
            self.first = remote(other, self.landed, sems.at[0], sems.at[1], spot.over_y)
        if self.later_landed is not None:
            self.over = remote(share, self.later_landed, sems.at[2], sems.at[3], spot.over_h)
        if whole is not None:
            size = whole.shape[0]
            mine, other = whole.at[spot.part(size)], whole.at[spot.part(size, False)]
            self.along = remote(share, mine, sems.at[4], sems.at[5], spot.over_y)
            self.near = remote(share, mine, sems.at[6], sems.at[7], spot.core)
            self.later = remote(other, other, sems.at[8], sems.at[9], spot.core)
            self.local = pltpu.make_async_copy(share, mine, sems.at[10])

    def start(self):
        self.first.start()

    def add(self):
        self.first.wait_recv()
        mine = self.grad[self.spot.part(self.grad.shape[0])]
        self.share[...] = (mine.astype(F32) + self.landed[...].astype(F32)).astype(BF)

    def send_over(self):
        pl.when(self.spot.away)(self.over.start)

    def add_over(self):
        @pl.when(self.spot.home)
        def _():
            self.over.wait_recv()
            self.share[...] = (self.share[...].astype(F32) + self.later_landed[...].astype(F32)).astype(BF)

    def spread(self):
        @pl.when(self.spot.home)
        def _():
            self.along.start()
            self.near.start()
            self.local.start()

    def relay(self):
        @pl.when(self.spot.home)
        def _():
            self.along.wait_recv()
            self.later.start()

    def finish_first(self):
        self.first.wait_send()

    def finish_over(self):
        pl.when(self.spot.away)(self.over.wait_send)

    def finish_spread(self):
        @pl.when(self.spot.home)
        def _():
            self.along.wait_send()
            self.near.wait_send()
            self.later.wait_send()
            self.local.wait()

        @pl.when(self.spot.away)
        def _():
            self.near.wait_recv()
            self.later.wait_recv()

    def finish(self):
        self.finish_first()
        self.finish_over()
        self.finish_spread()


class SmallSum:
    @staticmethod
    def scratch(rows, width):
        return [pltpu.VMEM((5, rows, width), F32), DMA((5,)), DMA((5,))]

    def __init__(self, spot, total, refs):
        landed, send, recv = refs
        self.total, self.landed = total, landed
        self.copies = [
            remote(total, landed.at[number], send.at[number], recv.at[number], device)
            for number, device in enumerate((spot.core, spot.over_x, spot.over_z, spot.over_h, spot.over_y))
        ]

    def step(self, number):
        if number > 0:
            self.copies[number - 1].wait()
            self.total[...] += self.landed[number - 1]
        if number < 5:
            self.copies[number].start()


class QuickSum:
    @staticmethod
    def scratch(rows, width):
        return [pltpu.VMEM((8, rows, width), F32), pltpu.VMEM((4, rows, width), F32), DMA((10,)), DMA((10,))]

    def __init__(self, spot, total, refs):
        self.total = total
        self.near, self.far, send, recv = refs
        self.near_place = spot.c * 4 + spot.zl * 2 + spot.x
        self.far_place = spot.sy * 2 + spot.h
        self.near_copies, self.far_copies = [], []
        for number in range(1, 8):
            device = dict(c=spot.c, zl=spot.zl, x=spot.x)
            for bit, name in ((4, "c"), (2, "zl"), (1, "x")):
                if number & bit:
                    device[name] = 1 - device[name]
            target = self.near.at[self.near_place]
            self.near_copies.append(remote(total, target, send.at[number - 1], recv.at[number - 1], device))
        for number in range(1, 4):
            device = dict(sy=spot.sy, h=spot.h)
            for bit, name in ((2, "sy"), (1, "h")):
                if number & bit:
                    device[name] = 1 - device[name]
            target = self.far.at[self.far_place]
            self.far_copies.append(remote(total, target, send.at[number + 6], recv.at[number + 6], device))

    @staticmethod
    def partners(spot):
        flip = lambda **names: {name: 1 - getattr(spot, name) for name in names}
        return [
            flip(c=0, x=0), flip(c=0, zl=0), flip(zl=0, x=0), flip(c=0, zl=0, x=0), flip(sy=0, h=0),
        ]

    def start(self):
        self.near[self.near_place] = self.total[...]
        for copy in self.near_copies:
            copy.start()

    def step(self):
        for copy in self.near_copies:
            copy.wait()
        total = self.near[0]
        for place in range(1, 8):
            total += self.near[place]
        self.total[...] = total
        self.far[self.far_place] = total
        for copy in self.far_copies:
            copy.start()

    def end(self):
        for copy in self.far_copies:
            copy.wait()
        total = self.far[0]
        for place in range(1, 4):
            total += self.far[place]
        self.total[...] = total


def norm_parts(values):
    average = jnp.mean(values, axis=-1, keepdims=True)
    centered = values - average
    scale = lax.rsqrt(jnp.mean(centered * centered, axis=-1, keepdims=True) + EPSILON)
    return centered * scale, scale


def norm_back(grad, gain, normed, scale):
    scaled = grad * gain
    back = scale * (
        scaled
        - jnp.mean(scaled, axis=-1, keepdims=True)
        - normed * jnp.mean(scaled * normed, axis=-1, keepdims=True)
    )
    return back, jnp.sum(grad * normed, axis=0, keepdims=True), jnp.sum(grad, axis=0, keepdims=True)


def gelu_both(values):
    size = jnp.abs(values) * 0.7071067811865476
    bell = jnp.exp(-size * size)
    t = 1.0 / (1.0 + 0.3275911 * size)
    poly = t * (
        0.254829592 + t * (-0.284496736 + t * (1.421413741 + t * (-1.453152027 + t * 1.061405429)))
    )
    tail = 0.5 * poly * bell
    below = jnp.where(values < 0, tail, 1.0 - tail)
    return values * below, below + values * bell * 0.3989422804014327


def lanes_of_head(shape, head):
    lane = lax.broadcasted_iota(jnp.int32, shape, 1)
    return (lane < HD) if head == 0 else (lane >= HD)


def pack_queries_keys(projected):
    one, two, three = (projected[:, part * 2 * HD : (part + 1) * 2 * HD] for part in range(3))
    low = lanes_of_head(one.shape, 0)
    keys = pltpu.roll(jnp.where(low, three, one), HD, 1)
    return jnp.concatenate([jnp.where(low, one, two), keys], axis=1), jnp.where(low, two, three)


def unpack_queries_keys(queries, keys, values):
    low = lanes_of_head(queries.shape, 0)
    keys = pltpu.roll(keys, HD, 1)
    return jnp.where(low, queries, keys), jnp.where(low, values, queries), jnp.where(low, keys, values)


def averager(width):
    row = lax.broadcasted_iota(jnp.int32, (width, width), 0) // HD
    column = lax.broadcasted_iota(jnp.int32, (width, width), 1) // HD
    return jnp.where(row == column, 1.0 / HD, 0.0).astype(BF)


def project(k, block, gather, raw_ref, qk_ref, v_ref, slot, stream):
    rows = pl.ds(pl.multiple_of((slot * 2 + stream) * gather.rows, gather.rows), gather.rows)
    projected = dot(gather.part(slot, stream), k.qkv_weight[...]) + k.biases[block : block + 1, : 6 * HD]
    raw, values = pack_queries_keys(projected)
    raw_ref[rows] = raw
    average = averager(4 * HD)
    centered = raw - dot_fine(raw, average)
    scale = lax.rsqrt(dot_fine(centered * centered, average) + EPSILON)
    gain, offset = k.head_gains[block : block + 1], k.head_offsets[block : block + 1]
    qk_ref[rows] = (centered * scale * gain + offset).astype(BF)
    v_ref[rows] = values.astype(BF)


def in_three(values):
    high = values.astype(BF)
    rest = values - high.astype(F32)
    middle = rest.astype(BF)
    return high.astype(F32), middle.astype(F32), (rest - middle.astype(F32)).astype(BF).astype(F32)


def beside(rows, values, head):
    lane = lax.broadcasted_iota(jnp.int32, rows.shape, 1)
    start = HD if head == 0 else 0
    high, middle, low = in_three(values)
    other = jnp.where(
        lane == start, high, jnp.where(lane == start + 1, middle, jnp.where(lane == start + 2, low, 0.0))
    )
    return jnp.where(lanes_of_head(rows.shape, head), rows.astype(F32), other).astype(BF)


def slice_attend(k, keys, start, size):
    rows = pl.ds(pl.multiple_of(start, size), size)
    span = pl.ds(pl.multiple_of(start // keys * keys, keys), keys)
    queries = k.qk_in[rows, : 2 * HD] * jnp.asarray(HD**-0.5, BF)
    low = lanes_of_head(queries.shape, 0)
    zeros = jnp.zeros_like(queries)
    mine = [jnp.where(low, queries, zeros), jnp.where(low, zeros, queries)]
    scores = dot_rt(jnp.concatenate(mine, axis=0), k.qk_in[span, 2 * HD :])
    largest = jnp.max(scores, axis=-1, keepdims=True)
    weights = jnp.exp(scores - largest)
    total = jnp.sum(weights, axis=-1, keepdims=True)
    found = dot(weights.astype(BF), k.v_in[span, :]) / total
    logs = largest + jnp.log(total)
    for head in range(2):
        k.query[head, rows] = beside(mine[head], logs[head * size : (head + 1) * size], head)
    both = jnp.where(low, found[:size], found[size:])
    k.exact[rows] = both
    k.mixed[rows] = both.astype(BF)


def enter(k):
    spot = k.spot
    gather = Gather(spot, k.gather_first)
    swaps = [
        Swap(spot, k.frames.at[0, gather.span(stream)], k.hidden.at[gather.span(stream)], k.swaps[stream])
        for stream in range(2)
    ]
    swaps.append(Swap(spot, k.own_biases, k.biases, k.swaps[2]))
    cotangent = Swap(spot, k.cotangent.at[0], k.cotangent_here, k.swaps[3])
    weighting = Swap(spot, k.weighting, k.weighting_here, k.swaps[4])
    for swap in swaps:
        swap.start()
    for stream in range(2):
        swaps[stream].arrive()
        rows = k.hidden[gather.span(stream)].astype(F32)
        values = (norm_parts(rows)[0] * k.gains[0, 0:1] + k.offsets[0, 0:1]).astype(BF)
        if stream == 1:
            gather.pass_on(0)
        gather.put(stream, values)
    owns = (k.qkv_own, k.out_own, k.up_own, k.down_own)
    gots = (k.qkv_got, k.out_got, k.up_got, k.down_got)
    qkv, out, up, down = (Move(spot, own.at[0], got, refs) for own, got, refs in zip(owns, gots, k.moves))
    k.saves.hidden()
    gather.pass_on(1)
    for stream in range(2):
        gather.arrive_core(stream, 0)
    for move in (qkv, out, up, down):
        move.start()
    qkv.relay(0)
    qkv.relay(1)
    gather.arrive(0, 1)
    qkv.finish()
    swaps[2].arrive()
    qkv.pick(k.qkv_weight, k.pick.at[0]).wait()

    def visit(index, carry):
        stream, step = index // 4, lax.rem(index, 4)
        pl.when(index > 1)(lambda: gather.arrive(stream, step))
        project(k, 0, gather, k.raw_first, k.qk_in, k.v_in, spot.slot(spot.c, step), stream)
        pl.when(step > 0)(lambda: gather.arrive_core(stream, step))
        project(k, 0, gather, k.raw_first, k.qk_in, k.v_in, spot.slot(1 - spot.c, step), stream)

        @pl.when(index == 3)
        def _():
            out.relay(0)
            out.relay(1)

        pl.when(index == 6)(lambda: up.relay(0))
        return carry

    lax.fori_loop(0, 8, visit, 0)
    out.finish()
    out_pick = out.pick(k.out_weight, k.pick.at[1])
    k.saves.gathered_first(gather.held)
    k.saves.raw_first()
    k.saves.qk_in()
    k.saves.v_in()
    for swap in swaps:
        swap.finish()
    gather.finish()
    out_pick.wait()
    return up, down, (cotangent, weighting)


def forward_kernel(is_last, k):
    spot = k.spot
    block = 1 if is_last else 0
    spot.greet(spot.over_x, spot.over_z, spot.core, spot.over_y, spot.over_h, spot.partner)
    if is_last:
        down = Move(spot, k.down_own.at[1], k.down_got, k.moves[0])
        up = Move(spot, k.up_own.at[1], k.up_got, k.moves[1])
        up.start()
        others = []
        k.loads.qk_in.wait()
        k.loads.v_in.wait()
        k.loads.out_weight.wait()
        k.loads.hidden.wait()
    else:
        up, down, swaps = enter(k)
        owns, gots = (k.qkv_own, k.out_own), (k.qkv_got_later, k.out_got_later)
        others = [Move(spot, own.at[1], got, refs) for own, got, refs in zip(owns, gots, k.moves[4:])]
    first, gather, later = Scatter(spot, k.local, k.one), Gather(spot, k.gather), Scatter(spot, k.local, k.two)
    rows_of = gather.span
    size = gather.held.shape[1]
    keys = k.mixed.shape[0] if is_last else FRAME_TOK

    def term_attention(slot, stream):
        start = pl.multiple_of(slot * size + stream * (size // 2), size // 2)
        slice_attend(k, keys, start, size // 2)
        return dot(k.mixed[pl.ds(start, size // 2)], k.out_weight[...])

    def before(index):
        if is_last:

            @pl.when(index == 6)
            def _():
                up.relay(0)
                up.relay(1)
                down.start()

        else:
            pl.when(index == 1)(lambda: up.relay(1))
            pl.when(index == 6)(lambda: (down.relay(0), swaps[0].start(), swaps[1].start()) and None)

    first.produce(term_attention, before)
    k.saves.exact()
    k.saves.query()
    for stream in range(2):
        rows = rows_of(stream)
        branch = first.result(stream) + k.offsets[block, 2:3]
        middle = k.hidden[rows].astype(F32) + k.gains[block, 2:3] * branch
        k.branch[rows] = branch
        k.middle[rows] = middle
        gather.put(stream, (norm_parts(middle)[0] * k.gains[block, 1:2] + k.offsets[block, 1:2]).astype(BF))
        if stream == 0:
            first.relay(1)
            down.relay(0 if is_last else 1)
            gather.pass_on(0)
    if is_last:
        down.relay(1)
    up.finish()
    up_pick = up.pick(k.up_weight, k.pick.at[0])
    for move in others:
        move.start()
    k.saves.branch()
    k.saves.middle()
    first.finish()
    gather.pass_on(1)
    down.finish()
    down_pick = down.pick(k.down_weight, k.pick.at[1])
    up_pick.wait()
    down_pick.wait()

    def term(slot, stream):
        bias = k.biases[block : block + 1, 6 * HD :]
        activated, slope = gelu_both(dot(gather.part(slot, stream), k.up_weight[...]) + bias)
        activated = activated.astype(BF)
        k.activated[slot, rows_of(stream)] = activated
        k.slope[slot, rows_of(stream)] = slope.astype(BF)
        return dot(activated, k.down_weight[...])

    later.produce_from(gather, term, 2)
    k.saves.second(gather.held)
    k.saves.activated()
    k.saves.slope()
    if not is_last:
        onward = Gather(spot, k.gather_next)
    for stream in range(2):
        rows = rows_of(stream)
        branch = later.result(stream) + k.offsets[block, 3:4]
        state = k.middle[rows] + k.gains[block, 3:4] * branch
        k.branch_two[rows] = branch
        k.state[rows] = state.astype(k.state.dtype)
        if not is_last:
            onward.put(stream, (norm_parts(state)[0] * k.gains[1, 0:1] + k.offsets[1, 0:1]).astype(BF))
        if stream == 0:
            later.relay(1)
            if not is_last:
                onward.pass_on(0)
            for move in others:
                move.relay(0)
                move.relay(1)
    k.saves.branch_two()
    k.saves.state()
    gather.finish()
    later.finish()
    if is_last:
        return
    for swap in swaps:
        swap.arrive()
        swap.finish()
    for move in others:
        move.finish()
    others[0].pick(k.qkv_weight, k.pick.at[0]).wait()
    onward.consume(functools.partial(project, k, 1, onward, k.raw, k.qk, k.v), 1)
    k.saves.gathered(onward.held)
    k.saves.raw()
    k.saves.qk()
    k.saves.v()
    onward.finish()


def wide(ref):
    return ref[...].reshape(ref.shape[0] * ref.shape[1], ref.shape[2])


def with_bias_row(grad_ref, weight_grad, bias_grad):
    size = weight_grad.shape[0]
    row = lax.broadcasted_iota(jnp.int32, (grad_ref.shape[0] - size, grad_ref.shape[1]), 0)
    grad_ref[:size] = weight_grad.astype(BF)
    grad_ref[size:] = jnp.where(row == 0, bias_grad, 0.0).astype(BF)


def pieces_of(ref):
    cut = ref.shape[0] // 64 * 32
    return pl.ds(0, cut), pl.ds(cut, ref.shape[0] - cut)


def qkv_weight_grad(k, gathered):
    rows = wide(k.above_qkv)
    with_bias_row(k.qkv_grad, dot_lt(wide(gathered), rows), jnp.sum(rows.astype(F32), axis=0, keepdims=True))


def prepare_keys(k, rows):
    shape = (rows.size, 2 * HD)
    lane = lax.broadcasted_iota(jnp.int32, shape, 1)
    for head in range(2):
        own = lanes_of_head(shape, head)
        ones = jnp.where(lane < (HD if head == 0 else 0) + 3, -1.0, 0.0)
        k.key_in[head, rows] = jnp.where(own, k.qk_in[rows, 2 * HD :].astype(F32), ones).astype(BF)
        k.value_in[head, rows] = jnp.where(own, k.v_in[rows].astype(F32), ones).astype(BF)
    k.key_turned[:, rows] = k.qk_in[rows, 2 * HD :].astype(F32).T.astype(BF)


def slice_back(k, keys, block_keys, start, size, grad):
    width = 2 * HD
    rows = pl.ds(pl.multiple_of(start, size), size)
    row = lax.broadcasted_iota(jnp.int32, (width, width), 0) // HD
    column = lax.broadcasted_iota(jnp.int32, (width, width), 1) // HD
    swap_sum = jnp.where(row != column, 1.0, 0.0).astype(BF)
    delta = dot_fine(grad * k.exact[rows], swap_sum)
    lane = lax.broadcasted_iota(jnp.int32, (size, width), 1)
    high, middle, low = in_three(delta)
    for head in range(2):
        lead = HD if head == 0 else 0
        other = jnp.where(
            lane == lead, high, jnp.where(lane == lead + 1, middle, jnp.where(lane == lead + 2, low, 0.0))
        )
        k.grad_in[head] = jnp.where(lanes_of_head((size, width), head), grad, other).astype(BF)
    k.query_grad[...] = jnp.zeros_like(k.query_grad)
    first = start // keys * keys

    def visit(index, carry):
        key_rows = pl.ds(pl.multiple_of(first + index * block_keys, block_keys), block_keys)
        for head in range(2):
            own = lanes_of_head((size, width), head)
            mine = pl.ds(head * HD, HD)
            query = k.query[head, rows]
            grad_rows = k.grad_in[head]
            key = k.key_in[head, key_rows]
            probs = jnp.exp(dot_rt(key, query))
            back = (probs * dot_rt(k.value_in[head, key_rows], grad_rows)).astype(BF)
            zeros = jnp.zeros((size, width), BF)
            k.grads[key_rows, 2 * width :] += dot(probs.astype(BF), jnp.where(own, grad_rows, zeros))
            k.grads[key_rows, width : 2 * width] += dot(back, jnp.where(own, query, zeros))
            k.query_grad[mine] += dot(k.key_turned[mine, key_rows], back)
        return carry

    lax.fori_loop(0, keys // block_keys, visit, 0)
    k.grads[rows, :width] = k.query_grad[...].T


def leave_heads(k, level, rows, target):
    width = 2 * HD
    average = averager(2 * width)
    values = k.raw_in[rows]
    centered = values - dot_fine(values, average)
    scale = lax.rsqrt(dot_fine(centered * centered, average) + EPSILON)
    normed = centered * scale
    lane = lax.broadcasted_iota(jnp.int32, normed.shape, 1)
    found = k.grads[rows, : 2 * width] * jnp.where(lane < width, HD**-0.5, 1.0)
    k.head_small[0:1] += jnp.sum(found * normed, axis=0, keepdims=True)
    k.head_small[1:2] += jnp.sum(found, axis=0, keepdims=True)
    scaled = found * k.head_gains[level : level + 1]
    back = scale * (scaled - dot_fine(scaled, average) - normed * dot_fine(scaled * normed, average))
    parts = unpack_queries_keys(back[:, :width], back[:, width:], k.grads[rows, 2 * width :])
    for number, part in enumerate(parts):
        target[:, number * width : (number + 1) * width] = part.astype(BF)


def backward_kernel(is_first, k):
    spot = k.spot
    block = 1 if is_first else 0
    spot.greet(spot.over_x, spot.over_z, spot.core, spot.over_y, spot.over_h, *((spot.partner,) if is_first else ()))
    gather, scatter, onward = Gather(spot, k.gather), Scatter(spot, k.local, k.one), Gather(spot, k.gather_next)
    rows_of = gather.span
    size = gather.held.shape[1]
    tokens = 8 * size
    keys = tokens if is_first else FRAME_TOK
    sums = [
        Total(spot, grad.at[rows], None if whole is None else whole.at[rows], refs)
        for (grad, whole), pieces in (
            ((k.down_grad, k.down_whole), zip(pieces_of(k.down_grad), k.down_total)),
            ((k.up_grad, k.up_whole if is_first else None), zip(pieces_of(k.up_grad), k.up_total)),
        )
        for rows, refs in pieces
    ]
    k.small[...] = jnp.zeros_like(k.small)
    if is_first:
        layer = Swap(spot, k.state, k.layer_out, k.swap)
        k.loads.cotangent.wait()
    else:
        above = Scatter(spot, k.local, k.two)
        qkv = Total(spot, k.qkv_grad, k.qkv_whole, k.qkv_total)
        out = Total(spot, k.out_grad_in, k.out_whole, k.out_total)
        out.start()
        k.loads.above_qkv.wait()
        k.loads.qkv_weight.wait()
        above.produce(lambda slot, stream: dot_rt(k.above_qkv[slot, rows_of(stream)], k.qkv_weight[...]))
        gathered = pltpu.make_async_copy(k.gathered, k.shared, k.pick.at[0])
        gathered.start()
        out.add()
        out.send_over()
        gathered.wait()
        qkv_weight_grad(k, k.shared)
        qkv.start()
        k.loads.above_hidden.wait()
        k.loads.above_middle_grad.wait()
    k.loads.branch_two.wait()
    for stream in range(2):
        rows = rows_of(stream)
        if is_first:
            grad = k.cotangent[rows].astype(F32) * k.weighting[rows, 0:1]
        else:
            normed, scale = norm_parts(k.above_hidden[rows])
            grad, gain_term, offset_term = norm_back(above.result(stream), k.gains[1, 0:1], normed, scale)
            k.small[6:7] += gain_term
            k.small[7:8] += offset_term
            grad = grad + k.above_middle_grad[rows]
        k.grad_rows[rows] = grad
        scaled = k.gains[block, 3:4] * grad
        gather.put(stream, scaled.astype(BF))
        k.small[0:1] += jnp.sum(grad * k.branch_two[rows], axis=0, keepdims=True)
        k.small[1:2] += jnp.sum(scaled, axis=0, keepdims=True)
        if stream == 0:
            if not is_first:
                above.relay(1)
            gather.pass_on(0)
    second = pltpu.make_async_copy(k.second, k.shared, k.pick.at[1])
    second.start()
    if is_first:
        middle_rows, branch_rows, fetched = k.middle, k.branch, [k.loads.middle, k.loads.branch]
    else:
        middle_rows, branch_rows = k.above_hidden, k.above_middle_grad
        fetched = [
            pltpu.make_async_copy(k.middle, middle_rows, k.pick.at[2]),
            pltpu.make_async_copy(k.branch, branch_rows, k.pick.at[3]),
        ]
        for copy in fetched:
            copy.start()
    if is_first:
        layer.start()
    else:
        above.finish()
        qkv.add()
        qkv.send_over()
        out.add_over()
        out.spread()
    k.loads.down_weight.wait()
    k.loads.up_weight.wait()
    k.loads.slope.wait()

    def term(slot, stream):
        slope = k.slope[slot, rows_of(stream)].astype(F32)
        up_rows = (dot_rt(gather.part(slot, stream), k.down_weight[...]) * slope).astype(BF)
        k.up_rows[slot, rows_of(stream)] = up_rows
        return dot_rt(up_rows, k.up_weight[...])

    scatter.produce_from(gather, term)
    gather.finish()
    for copy in fetched:
        copy.wait()
    k.loads.activated.wait()

    def down_piece(piece):
        cut = k.down_grad.shape[0] // 2
        lanes = slice(piece * cut, (piece + 1) * cut)
        rows = k.activated[:, :, lanes].reshape(tokens, cut)
        k.down_grad[lanes] = dot_lt(rows, wide(gather.held)).astype(BF)
        sums[piece].start()

    def up_piece(piece):
        cut = k.shared.shape[2] // 2
        lanes = slice(piece * cut, (piece + 1) * cut)
        rows = k.shared[:, :, lanes].reshape(tokens, cut)
        k.up_grad[lanes] = dot_lt(rows, wide(k.up_rows)).astype(BF)
        if piece == 1:
            total = jnp.sum(wide(k.up_rows).astype(F32), axis=0, keepdims=True)
            row = lax.broadcasted_iota(jnp.int32, (k.up_grad.shape[0] - 2 * cut, k.up_grad.shape[1]), 0)
            k.up_grad[2 * cut :] = jnp.where(row == 0, total, 0.0).astype(BF)
        sums[2 + piece].start()

    def leave_rows(stream):
        rows = rows_of(stream)
        normed, scale = norm_parts(middle_rows[rows])
        grad, gain_term, offset_term = norm_back(scatter.result(stream), k.gains[block, 1:2], normed, scale)
        grad = grad + k.grad_rows[rows]
        k.middle_grad[rows] = grad
        scaled = k.gains[block, 2:3] * grad
        onward.put(stream, scaled.astype(BF))
        k.small[2:3] += gain_term
        k.small[3:4] += offset_term
        k.small[4:5] += jnp.sum(grad * branch_rows[rows], axis=0, keepdims=True)
        k.small[5:6] += jnp.sum(scaled, axis=0, keepdims=True)

    down_piece(0)
    scatter.relay(1)
    leave_rows(0)
    down_piece(1)
    second.wait()
    up_piece(0)
    up_piece(1)
    if not is_first:
        gathered = pltpu.make_async_copy(k.gathered_first, k.shared, k.pick.at[0])
        gathered.start()
    onward.pass_on(0)
    leave_rows(1)
    if not is_first:
        qkv.add_over()
        qkv.spread()
        out.relay()
    k.saves.middle_grad()
    if not is_first:
        early = SmallSum(spot, k.early, k.early_sum)
        lanes = 4 * HD
        k.early[0:8] = k.small_first[...]
        k.early[8:16] = k.small[...]
        k.early[16:24] = jnp.zeros_like(k.early[16:24])
        k.early[16:17, :lanes] = k.head_first[0:1]
        k.early[16:17, lanes : 2 * lanes] = k.head_first[1:2]
        early.step(0)
    scatter.finish()
    k.loads.out_weight.wait()
    k.loads.qk_in.wait()
    k.loads.v_in.wait()
    k.loads.query.wait()
    k.loads.exact.wait()
    k.grads[...] = jnp.zeros_like(k.grads)

    def prepare(index, carry):
        prepare_keys(k, pl.ds(pl.multiple_of(index * size, size), size))
        return carry

    lax.fori_loop(0, 8, prepare, 0)

    def use(slot):
        grad = dot_rt(onward.held[slot], k.out_weight[...]).astype(BF).astype(F32)
        slice_back(k, keys, 1024, slot * size, size, grad)

    def visit(step, carry):
        for stream in range(2):
            onward.arrive(stream, step)
        use(spot.slot(spot.c, step))

        @pl.when(step == 0)
        def _():
            onward.pass_on(1)
            for part in sums[:2]:
                part.add()
                part.send_over()

        for stream in range(2):
            onward.arrive_core(stream, step)
        use(spot.slot(1 - spot.c, step))

        @pl.when(step == 0)
        def _():
            sums[2].add()
            sums[2].send_over()
            if not is_first:
                qkv.relay()
                early.step(1)

        @pl.when(step == 1)
        def _():
            sums[3].add()
            sums[3].send_over()
            sums[0].add_over()
            sums[0].spread()
            if not is_first:
                early.step(2)

        @pl.when(step == 2)
        def _():
            sums[1].add_over()
            sums[1].spread()
            if not is_first:
                early.step(3)

        @pl.when(step == 3)
        def _():
            sums[2].add_over()
            if is_first:
                sums[2].spread()
            sums[0].relay()
            sums[1].relay()
            if not is_first:
                early.step(4)

        return carry

    lax.fori_loop(0, 4, visit, 0)
    k.out_grad[...] = dot_lt(k.exact[...].astype(BF), wide(onward.held)).astype(BF)
    k.saves.out_grad()
    if not is_first:
        qkv.finish()
        out.finish()
    k.loads.raw_in.wait()
    k.head_small[...] = jnp.zeros_like(k.head_small)
    qkv_rows = k.qkv_rows if is_first else k.above_qkv

    def leave(index, carry):
        leave_heads(k, block, pl.ds(pl.multiple_of(index * size, size), size), qkv_rows.at[index])
        return carry

    lax.fori_loop(0, 8, leave, 0)
    k.saves.grad_qkv(qkv_rows)
    onward.finish()
    if is_first:
        layer.arrive()
        layer.finish()
        sums[3].add_over()
        sums[3].spread()
        for part in sums[2:]:
            part.relay()
        for part in sums:
            part.finish()
        return
    gathered.wait()
    qkv_weight_grad(k, k.shared)
    k.saves.qkv_grad_first(k.qkv_grad)
    early.step(5)
    sums[3].add_over()
    for part, save in zip(sums[2:], (k.saves.up_share, k.saves.up_share_later)):
        save(part.share)
        part.finish_first()
        part.finish_over()
    for part in sums[:2]:
        part.finish()


def last_kernel(k):
    spot = k.spot
    spot.greet(
        spot.over_x, spot.over_z, spot.core, spot.over_y, spot.over_h, spot.partner, *QuickSum.partners(spot)
    )
    scatter = Scatter(spot, k.local, k.one)
    out = Total(spot, k.out_grad_in, k.out_whole, k.out_total)
    qkv = Total(spot, k.qkv_grad, k.qkv_whole, k.qkv_total)
    cut = k.up_share.shape[0] * 2
    up = [
        Total(spot, None, k.up_whole.at[pl.ds(0, cut)], [None, k.up_share, None, k.up_total.at[0]]),
        Total(
            spot,
            None,
            k.up_whole.at[pl.ds(cut, k.up_whole.shape[0] - cut)],
            [None, k.up_share_later, None, k.up_total.at[1]],
        ),
    ]
    k.loads.qkv_grad.wait()
    k.loads.out_grad_in.wait()
    qkv.start()
    out.start()
    k.loads.qkv_weight.wait()
    k.loads.above_qkv.wait()
    scatter.produce(lambda slot, stream: dot_rt(k.above_qkv[slot, scatter.span(stream)], k.qkv_weight[...]))
    k.loads.up_share.wait()
    k.loads.up_share_later.wait()
    for part in up:
        part.spread()
    late = QuickSum(spot, k.late, k.late_sum)
    lanes = 4 * HD
    k.late[...] = jnp.zeros_like(k.late)
    k.late[2:3, :lanes] = k.head_later[0:1]
    k.late[2:3, lanes : 2 * lanes] = k.head_later[1:2]
    scatter.relay(1)
    for part in (qkv, out):
        part.add()
        part.send_over()
    k.loads.hidden.wait()
    k.loads.middle_grad.wait()
    for part in up:
        part.relay()
    swaps = []
    for stream in range(2):
        span = scatter.span(stream)
        normed, scale = norm_parts(k.hidden[span].astype(F32))
        grad, gain_term, offset_term = norm_back(scatter.result(stream), k.gains[0, 0:1], normed, scale)
        k.late[0:1] += gain_term
        k.late[1:2] += offset_term
        k.grad_in[span] = (grad + k.middle_grad[span]).astype(BF)
        swap = Swap(spot, k.grad_in.at[span], k.input_grad.at[span], k.swaps[stream])
        swap.start()
        swaps.append(swap)
    late.start()
    for part in (qkv, out):
        part.add_over()
        part.spread()
    late.step()
    qkv.relay()
    out.relay()
    late.end()
    for swap in swaps:
        swap.arrive()
        swap.finish()
    for part in (out, qkv):
        part.finish()
    for part in up:
        part.finish_spread()
    scatter.finish()


def gather_results(k):
    k.loads.layer_in.wait()
    k.saves.layer_out(k.layer_in)
    k.loads.grad_in.wait()
    k.saves.input_grad(k.grad_in)
    sums = (
        (k.down, k.saves.down, (k.down_first, k.down_later), (k.loads.down_first, k.loads.down_later), None),
        (k.up, k.saves.up, (k.up_first, k.up_later), (k.loads.up_first, k.loads.up_later), k.up_bias),
        (k.out, k.saves.out, (k.out_first, k.out_later), (k.loads.out_first, k.loads.out_later), None),
        (k.qkv, k.saves.qkv, (k.qkv_first, k.qkv_later), (k.loads.qkv_first, k.loads.qkv_later), k.qkv_bias),
    )
    for whole, save, parts, loads, bias in sums:
        size = whole.shape[1]
        for block in range(2):
            loads[block].wait()
            whole[block] = parts[block][:size].astype(F32)
            if bias is not None:
                bias[block : block + 1] = parts[block][size : size + 16][0:1].astype(F32)
        save()
    early, late = k.early[...], k.late[...]
    gains = (late[0:1], early[10:11], early[12:13], early[8:9], early[14:15], early[2:3], early[4:5], early[0:1])
    offsets = (late[1:2], early[11:12], early[13:14], early[9:10], early[15:16], early[3:4], early[5:6], early[1:2])
    for number in range(8):
        k.gain[number // 4, number % 4 : number % 4 + 1] = gains[number]
        k.offset[number // 4, number % 4 : number % 4 + 1] = offsets[number]
    for block, row in enumerate((late[2:3], early[16:17])):
        for kind, ref in enumerate((k.head_gain, k.head_offset)):
            for part in range(2):
                start = kind * 4 * HD + part * 2 * HD
                ref[block, part : part + 1] = row[:, start : start + HD] + row[:, start + HD : start + 2 * HD]


class Own:
    def __init__(self, own, level, got):
        self.own, self.level, self.got = own, level, got


class Load:
    def __init__(self, values):
        self.values = values


class Outside(Load):
    pass


INSIDE, APART, SAVED, TARGET = range(4)


def run(kernel, number, inputs, outputs, scratch):
    operands, in_specs = [], []
    vmem, outside = pl.BlockSpec(memory_space=pltpu.VMEM), pl.BlockSpec(memory_space=pl.ANY)
    loaded, places = {}, {}

    def give(values, spec):
        operands.append(values)
        in_specs.append(spec)
        return len(operands) - 1

    for key, value in inputs.items():
        if isinstance(value, Own):
            places[key] = (give(value.own, outside), give(value.got, outside))
            loaded[key] = value.own.shape[1:], value.own.dtype
        elif isinstance(value, Load):
            places[key] = give(value.values, outside)
            if not isinstance(value, Outside):
                loaded[key] = value.values.shape, value.values.dtype
        else:
            places[key] = give(value, vmem)
    out_keys = list(outputs)
    kinds = [outputs[key][1] for key in out_keys]
    saved = [key for key, kind in zip(out_keys, kinds) if kind in (SAVED, TARGET)]
    shapes = []

    def hold(item):
        if isinstance(item, list):
            return [hold(part) for part in item]
        shapes.append(item)
        return len(shapes) - 1

    layout = {key: hold(item) for key, item in scratch.items()}
    load_layout = {key: hold(pltpu.VMEM(size, kind)) for key, (size, kind) in loaded.items()}
    for key, kind in zip(out_keys, kinds):
        if kind == SAVED:
            layout[key] = hold(pltpu.VMEM(outputs[key][0].shape, outputs[key][0].dtype))
    load_at, save_at = hold(DMA((max(len(loaded), 1),))), hold(DMA((max(len(saved), 1),)))

    def whole(*refs):
        ins, rest = refs[: len(operands)], refs[len(operands) :]
        outs, held = rest[: len(out_keys)], rest[len(out_keys) :]

        def find(item):
            return [find(part) for part in item] if isinstance(item, list) else held[item]

        k = types.SimpleNamespace(**{key: find(item) for key, item in layout.items()})
        k.spot = None if number is None else Spot()
        saving = []
        loads, saves = {}, {}

        def saver(ref, target, sem):
            def save(source=ref):
                copy = pltpu.make_async_copy(source, target, sem)
                copy.start()
                saving.append(copy)

            return save

        for key, kind, out in zip(out_keys, kinds, outs):
            if kind in (INSIDE, APART):
                setattr(k, key, out)
            else:
                saves[key] = saver(getattr(k, key, None), out, held[save_at].at[saved.index(key)])
        for place, key in enumerate(loaded):
            target, sem = held[load_layout[key]], held[load_at].at[place]
            setattr(k, key, target)
            if isinstance(inputs[key], Own):
                own, got = (ins[at] for at in places[key])
                copy = pltpu.make_async_copy(got, target, sem)
                pl.when(k.spot.home)(pltpu.make_async_copy(own.at[inputs[key].level], target, sem).start)
                pl.when(k.spot.away)(copy.start)
            else:
                copy = pltpu.make_async_copy(ins[places[key]], target, sem)
                copy.start()
            loads[key] = copy
        for key in inputs:
            if key not in loaded:
                setattr(k, key, ins[places[key]])
        k.loads, k.saves = types.SimpleNamespace(**loads), types.SimpleNamespace(**saves)
        kernel(k)
        for copy in saving:
            copy.wait()

    found = pl.pallas_call(
        whole,
        name=getattr(kernel, "func", kernel).__name__,
        out_shape=[outputs[key][0] for key in out_keys],
        in_specs=in_specs,
        out_specs=[vmem if kind == INSIDE else outside for kind in kinds],
        scratch_shapes=shapes,
        compiler_params=pltpu.CompilerParams(
            collective_id=number, has_side_effects=number is not None, vmem_limit_bytes=VMEM_LIMIT
        ),
    )(*operands)
    return types.SimpleNamespace(**dict(zip(out_keys, found)))


def shape(*sizes):
    return jax.ShapeDtypeStruct(sizes[:-1], sizes[-1])


def square_body(
    frames_in,
    qkv_weight,
    qkv_bias,
    out_weight,
    up_weight,
    up_bias,
    down_weight,
    norm_gain,
    norm_offset,
    head_gain,
    head_offset,
    cotangent,
    visible,
    query_count,
):
    rows, width = frames_in.shape[1:]
    tokens = 8 * rows
    inner = 2 * HD
    units = up_weight.shape[2]
    gather = Gather.scratch(rows, width)
    local, scatter = Scatter.local(rows, width), Scatter.scratch(rows, width)
    pad = 32

    def moved(weight):
        return shape(*weight.shape[1:], BF), APART

    biases = jnp.concatenate([qkv_bias, up_bias], axis=1).astype(F32)
    biases = jnp.pad(biases, ((0, 6), (0, 0)))
    weighting = visible[0].astype(F32) * (query_count[0].astype(F32) / QMAX)
    weighting = jnp.broadcast_to(weighting[:, None], (rows, 128))
    head_gains, head_offsets = (
        jnp.concatenate([pair[:, 0], pair[:, 0], pair[:, 1], pair[:, 1]], axis=1) for pair in (head_gain, head_offset)
    )
    norms = dict(gains=norm_gain, offsets=norm_offset)
    heads = dict(head_gains=head_gains, head_offsets=head_offsets)
    def forward(is_last, inputs, outputs, scratch):
        block = 1 if is_last else 0
        return run(
            functools.partial(forward_kernel, is_last),
            1 + block,
            dict(up_own=Outside(up_weight), down_own=Outside(down_weight), **norms, **inputs),
            dict(
                exact=(shape(tokens, inner, F32), SAVED),
                query=(shape(2, tokens, inner, BF), SAVED),
                branch=(shape(rows, width, F32), SAVED),
                middle=(shape(rows, width, F32), SAVED),
                second=(shape(8, rows, width, BF), TARGET),
                activated=(shape(8, rows, units, BF), SAVED),
                slope=(shape(8, rows, units, BF), SAVED),
                branch_two=(shape(rows, width, F32), SAVED),
                state=(shape(rows, width, BF if is_last else F32), SAVED),
                up_got=moved(up_weight),
                down_got=moved(down_weight),
                **outputs,
            ),
            dict(
                local=local,
                one=scatter,
                two=scatter,
                gather=gather,
                pick=DMA((2,)),
                mixed=pltpu.VMEM((tokens, inner), BF),
                up_weight=pltpu.VMEM(up_weight.shape[1:], BF),
                down_weight=pltpu.VMEM(down_weight.shape[1:], BF),
                **scratch,
            ),
        )

    lower = forward(
        False,
        dict(
            frames=Outside(frames_in),
            own_biases=biases,
            qkv_own=Outside(qkv_weight),
            out_own=Outside(out_weight),
            cotangent=Outside(cotangent),
            weighting=weighting,
            **heads,
        ),
        dict(
            hidden=(shape(rows, width, BF), SAVED),
            biases=(shape(*biases.shape, F32), INSIDE),
            cotangent_here=(shape(rows, width, BF), APART),
            weighting_here=(shape(rows, 128, F32), APART),
            qkv_got=moved(qkv_weight),
            out_got=moved(out_weight),
            qkv_got_later=moved(qkv_weight),
            out_got_later=moved(out_weight),
            gathered_first=(shape(8, rows, width, BF), TARGET),
            raw_first=(shape(tokens, 2 * inner, F32), SAVED),
            qk_in=(shape(tokens, 2 * inner, BF), SAVED),
            v_in=(shape(tokens, inner, BF), SAVED),
            gathered=(shape(8, rows, width, BF), TARGET),
            raw=(shape(tokens, 2 * inner, F32), SAVED),
            qk=(shape(tokens, 2 * inner, BF), SAVED),
            v=(shape(tokens, inner, BF), SAVED),
        ),
        dict(
            gather_first=gather,
            gather_next=gather,
            swaps=[Swap.scratch] * 5,
            moves=[Move.scratch] * 6,
            qkv_weight=pltpu.VMEM(qkv_weight.shape[1:], BF),
            out_weight=pltpu.VMEM(out_weight.shape[1:], BF),
        ),
    )
    entry = types.SimpleNamespace(
        hidden=lower.hidden, gathered=lower.gathered_first, raw=lower.raw_first, qk=lower.qk_in, v=lower.v_in
    )
    between = types.SimpleNamespace(
        hidden=lower.state, gathered=lower.gathered, raw=lower.raw, qk=lower.qk, v=lower.v
    )
    upper = forward(
        True,
        dict(
            qk_in=Load(between.qk),
            v_in=Load(between.v),
            hidden=Load(between.hidden),
            biases=lower.biases,
            out_weight=Own(out_weight, 1, lower.out_got_later),
        ),
        dict(),
        dict(moves=[Move.scratch] * 2),
    )

    qkv_grad = pltpu.VMEM((width + pad, 3 * inner), BF)

    def in_pieces(size, lanes):
        cut = size // 64 * 32
        return [Total.scratch(cut, lanes), Total.scratch(size - cut, lanes)]

    qkv_whole = dict(qkv_whole=(shape(width + pad, 3 * inner, BF), APART))
    out_whole = dict(out_whole=(shape(inner, width, BF), APART))
    out_total = dict(out_total=Total.scratch(inner, width))

    def backward(is_first, came, kept, up_got, out_got, inputs, outputs, scratch):
        block = 1 if is_first else 0
        return run(
            functools.partial(backward_kernel, is_first),
            3 + block,
            dict(
                **inputs,
                branch_two=Load(kept.branch_two),
                down_weight=Own(down_weight, block, kept.down_got),
                up_weight=Own(up_weight, block, up_got),
                slope=Load(kept.slope),
                activated=Load(kept.activated),
                second=Outside(kept.second),
                out_weight=Own(out_weight, block, out_got),
                qk_in=Load(came.qk),
                v_in=Load(came.v),
                query=Load(kept.query),
                exact=Load(kept.exact),
                raw_in=Load(came.raw),
                gains=norm_gain,
                head_gains=head_gains,
            ),
            dict(
                middle_grad=(shape(rows, width, F32), SAVED),
                grad_qkv=(shape(8, rows, 3 * inner, BF), TARGET),
                down_whole=(shape(units, width, BF), APART),
                out_grad=(shape(inner, width, BF), SAVED),
                small=(shape(8, width, F32), INSIDE),
                head_small=(shape(2, 2 * inner, F32), INSIDE),
                **outputs,
            ),
            dict(
                local=local,
                one=scatter,
                gather=gather,
                gather_next=gather,
                up_rows=pltpu.VMEM((8, rows, units), BF),
                grad_rows=pltpu.VMEM((rows, width), F32),
                shared=pltpu.VMEM((8, rows, width), BF),
                pick=DMA((4,)),
                down_grad=pltpu.VMEM((units, width), BF),
                up_grad=pltpu.VMEM((width + pad, units), BF),
                down_total=in_pieces(units, width),
                up_total=in_pieces(width + pad, units),
                key_in=pltpu.VMEM((2, tokens, inner), BF),
                value_in=pltpu.VMEM((2, tokens, inner), BF),
                grad_in=pltpu.VMEM((2, rows, inner), BF),
                query_grad=pltpu.VMEM((inner, rows), F32),
                key_turned=pltpu.VMEM((inner, tokens), BF),
                grads=pltpu.VMEM((tokens, 3 * inner), F32),
                **scratch,
            ),
        )

    upper_back = backward(
        True,
        between,
        upper,
        upper.up_got,
        lower.out_got_later,
        dict(
            cotangent=Load(lower.cotangent_here),
            weighting=lower.weighting_here,
            state=Outside(upper.state),
            middle=Load(upper.middle),
            branch=Load(upper.branch),
        ),
        dict(
            layer_out=(shape(rows, width, BF), APART),
            up_whole=(shape(width + pad, units, BF), APART),
        ),
        dict(swap=Swap.scratch, qkv_rows=pltpu.VMEM((8, rows, 3 * inner), BF)),
    )
    lower_back = backward(
        False,
        entry,
        lower,
        lower.up_got,
        lower.out_got,
        dict(
            above_qkv=Load(upper_back.grad_qkv),
            qkv_weight=Own(qkv_weight, 1, lower.qkv_got_later),
            gathered=Outside(between.gathered),
            gathered_first=Outside(entry.gathered),
            above_hidden=Load(between.hidden),
            above_middle_grad=Load(upper_back.middle_grad),
            out_grad_in=upper_back.out_grad,
            middle=Outside(lower.middle),
            branch=Outside(lower.branch),
            small_first=upper_back.small,
            head_first=upper_back.head_small,
        ),
        dict(
            early=(shape(24, width, F32), INSIDE),
            up_share=(shape((width + pad) // 64 * 16, units, BF), TARGET),
            up_share_later=(shape((width + pad) // 2 - (width + pad) // 64 * 16, units, BF), TARGET),
            qkv_grad_first=(shape(width + pad, 3 * inner, BF), TARGET),
            **qkv_whole,
            **out_whole,
        ),
        dict(
            early_sum=SmallSum.scratch(24, width),
            two=scatter,
            qkv_grad=qkv_grad, qkv_total=Total.scratch(width + pad, 3 * inner), **out_total),
    )
    last = run(
        last_kernel,
        5,
        dict(
            above_qkv=Load(lower_back.grad_qkv),
            qkv_weight=Own(qkv_weight, 0, lower.qkv_got),
            hidden=Load(entry.hidden),
            middle_grad=Load(lower_back.middle_grad),
            out_grad_in=Load(lower_back.out_grad),
            qkv_grad=Load(lower_back.qkv_grad_first),
            up_share=Load(lower_back.up_share),
            up_share_later=Load(lower_back.up_share_later),
            gains=norm_gain,
            head_later=lower_back.head_small,
        ),
        dict(
            input_grad=(shape(rows, width, BF), APART),
            late=(shape(8, width, F32), INSIDE),
            up_whole=(shape(width + pad, units, BF), APART),
            **qkv_whole,
            **out_whole,
        ),
        dict(
            local=local,
            one=scatter,
            grad_in=pltpu.VMEM((rows, width), BF),
            swaps=[Swap.scratch] * 2,
            late_sum=QuickSum.scratch(8, width),
            qkv_total=Total.scratch(width + pad, 3 * inner),
            **out_total,
            up_total=DMA((2, 11)),
        ),
    )
    found = run(
        gather_results,
        None,
        dict(
            layer_in=Load(upper_back.layer_out),
            grad_in=Load(last.input_grad),
            down_first=Load(lower_back.down_whole),
            down_later=Load(upper_back.down_whole),
            up_first=Load(last.up_whole),
            up_later=Load(upper_back.up_whole),
            out_first=Load(last.out_whole),
            out_later=Load(lower_back.out_whole),
            qkv_first=Load(last.qkv_whole),
            qkv_later=Load(lower_back.qkv_whole),
            early=lower_back.early,
            late=last.late,
        ),
        dict(
            qkv=(shape(2, width, 3 * inner, F32), SAVED),
            qkv_bias=(shape(2, 3 * inner, F32), INSIDE),
            out=(shape(2, inner, width, F32), SAVED),
            up=(shape(2, width, units, F32), SAVED),
            up_bias=(shape(2, units, F32), INSIDE),
            down=(shape(2, units, width, F32), SAVED),
            gain=(shape(2, 4, width, F32), INSIDE),
            offset=(shape(2, 4, width, F32), INSIDE),
            head_gain=(shape(2, 2, HD, F32), INSIDE),
            head_offset=(shape(2, 2, HD, F32), INSIDE),
            layer_out=(shape(rows, width, BF), TARGET),
            input_grad=(shape(rows, width, BF), TARGET),
        ),
        dict(),
    )
    return (
        found.layer_out[None],
        found.input_grad[None],
        found.qkv,
        found.qkv_bias,
        found.out,
        found.up,
        found.up_bias,
        found.down,
        found.gain,
        found.offset,
        found.head_gain,
        found.head_offset,
    )


TP = ("c", "r")


def exchange(values):
    return lax.ppermute(values, ("c", "h"), [(0, 0), (1, 2), (2, 1), (3, 3)])


def layer_norm(values, norm_scale, norm_bias):
    average = jnp.mean(values, axis=-1, keepdims=True)
    centered = values - average
    variance = jnp.mean(centered * centered, axis=-1, keepdims=True)
    return centered * lax.rsqrt(variance + EPSILON) * norm_scale + norm_bias


def exact_gelu(values):
    return jax.nn.gelu(values, approximate=False)


def attend_rows(query_rows, key_rows, value_rows, score_scale):
    scores = (
        jnp.einsum("qhe,khe->hqk", query_rows, key_rows, preferred_element_type=jnp.float32)
        * score_scale
    )
    largest = jnp.max(scores, axis=-1, keepdims=True)
    unnormed = jnp.exp(scores - largest)
    denominator = jnp.sum(unnormed, axis=-1, keepdims=True)
    weights = (unnormed / denominator).astype(jnp.bfloat16)
    mixed = jnp.einsum("hqk,khe->qhe", weights, value_rows, preferred_element_type=jnp.float32)
    return (mixed, (largest + jnp.log(denominator))[:, :, 0])


def attend_back(query_rows, key_rows, value_rows, log_total, grad_rows, score_scale):
    scores = (
        jnp.einsum("qhe,khe->hqk", query_rows, key_rows, preferred_element_type=jnp.float32)
        * score_scale
    )
    probs = jnp.exp(scores - log_total[:, :, None])
    grad_probs = jnp.einsum(
        "qhe,khe->hqk", grad_rows, value_rows, preferred_element_type=jnp.float32
    )
    grad_scores = probs * (grad_probs - jnp.sum(probs * grad_probs, axis=-1, keepdims=True))
    grad_scores = grad_scores.astype(jnp.bfloat16)
    grad_query = (
        jnp.einsum("hqk,khe->qhe", grad_scores, key_rows, preferred_element_type=jnp.float32)
        * score_scale
    )
    grad_key = (
        jnp.einsum("hqk,qhe->khe", grad_scores, query_rows, preferred_element_type=jnp.float32)
        * score_scale
    )
    grad_value = jnp.einsum(
        "hqk,qhe->khe", probs.astype(jnp.bfloat16), grad_rows, preferred_element_type=jnp.float32
    )
    return (grad_query, grad_key, grad_value)


def attention_forward(queries, key_all, value_all, frame_only, score_scale):
    frame_shape = (queries.shape[0] // FRAME_TOK, FRAME_TOK) + queries.shape[1:]
    query_frames = queries.reshape(frame_shape)
    if frame_only:
        mixed, log_total = lax.map(
            lambda triple: attend_rows(triple[0], triple[1], triple[2], score_scale),
            (query_frames, key_all.reshape(frame_shape), value_all.reshape(frame_shape)),
        )
    else:
        mixed, log_total = lax.map(
            lambda query_block: attend_rows(query_block, key_all, value_all, score_scale),
            query_frames,
        )
    return (mixed.reshape(queries.shape), log_total)


def attention_backward(queries, key_all, value_all, log_total, grad_mixed, frame_only, score_scale):
    frame_shape = (queries.shape[0] // FRAME_TOK, FRAME_TOK) + queries.shape[1:]
    query_frames = queries.reshape(frame_shape)
    grad_frames = grad_mixed.reshape(frame_shape)
    if frame_only:
        grad_query, grad_key, grad_value = lax.map(
            lambda group_in: attend_back(
                group_in[0], group_in[1], group_in[2], group_in[3], group_in[4], score_scale
            ),
            (
                query_frames,
                key_all.reshape(frame_shape),
                value_all.reshape(frame_shape),
                log_total,
                grad_frames,
            ),
        )
        return (
            grad_query.reshape(queries.shape),
            grad_key.reshape(queries.shape),
            grad_value.reshape(queries.shape),
        )

    def visit_frame(running, group_in):
        grad_query, grad_key, grad_value = attend_back(
            group_in[0], key_all, value_all, group_in[1], group_in[2], score_scale
        )
        return ((running[0] + grad_key, running[1] + grad_value), grad_query)

    zero_keys = jnp.zeros(key_all.shape, jnp.float32)
    (grad_key, grad_value), grad_query = lax.scan(
        visit_frame, (zero_keys, zero_keys), (query_frames, log_total, grad_frames)
    )
    return (grad_query.reshape(queries.shape), grad_key, grad_value)


def any_body(
    frames_in,
    qkv_weight,
    qkv_bias,
    out_weight,
    up_weight,
    up_bias,
    down_weight,
    norm_gain,
    norm_offset,
    head_gain,
    head_offset,
    cotangent,
    visible,
    query_count,
):
    score_scale = HD ** (-0.5)
    frames = exchange(frames_in[0])
    qkv_weight, out_weight, up_weight, down_weight, qkv_bias, up_bias = (
        [exchange(stacked[block_index]) for block_index in range(2)]
        for stacked in (qkv_weight, out_weight, up_weight, down_weight, qkv_bias, up_bias)
    )
    weighting = visible[0].astype(jnp.float32) * (query_count[0].astype(jnp.float32) / QMAX)
    weighting = exchange(weighting)
    cotangent = exchange(cotangent[0])

    def backward_block(grad_out, block_index, frame_only, saved):
        (
            hidden,
            gathered,
            split,
            queries,
            key_all,
            value_all,
            log_total,
            mixed_flat,
            branch,
            middle,
            gathered_two,
            hidden_up,
            activated,
            branch_two,
        ) = saved
        gains = norm_gain[block_index]
        offsets = norm_offset[block_index]
        total_rows = split.shape[0]
        grad_branch_two = gains[3] * grad_out
        offset_grad_three = jnp.sum(grad_branch_two, axis=0)
        gain_grad_three = jnp.sum(grad_out * branch_two, axis=0)
        shard_rows = lax.all_gather(grad_branch_two.astype(jnp.bfloat16), TP, axis=0, tiled=True)
        down_grad = jnp.einsum(
            "tf,td->fd", activated, shard_rows, preferred_element_type=jnp.float32
        )
        act_grad = jnp.einsum(
            "td,fd->tf", shard_rows, down_weight[block_index], preferred_element_type=jnp.float32
        )
        up_grad = jax.vjp(exact_gelu, hidden_up)[1](act_grad)[0].astype(jnp.bfloat16)
        down_grad, up_grads = (down_grad, up_grad)
        up_weight_grad = jnp.einsum(
            "td,tf->df", gathered_two, up_grads, preferred_element_type=jnp.float32
        )
        up_bias_grad = jnp.sum(up_grads.astype(jnp.float32), axis=0)
        second_grad = lax.psum_scatter(
            jnp.einsum(
                "tf,df->td", up_grads, up_weight[block_index], preferred_element_type=jnp.float32
            ).astype(jnp.bfloat16),
            TP,
            scatter_dimension=0,
            tiled=True,
        ).astype(jnp.float32)
        middle_grad, gain_grad_one, offset_grad_one = jax.vjp(
            layer_norm, middle, gains[1], offsets[1]
        )[1](second_grad)
        middle_grad = middle_grad + grad_out
        grad_branch = gains[2] * middle_grad
        offset_grad_two = jnp.sum(grad_branch, axis=0)
        gain_grad_two = jnp.sum(middle_grad * branch, axis=0)
        shard_rows = lax.all_gather(grad_branch.astype(jnp.bfloat16), TP, axis=0, tiled=True)
        out_grad = jnp.einsum(
            "tc,td->cd", mixed_flat, shard_rows, preferred_element_type=jnp.float32
        )
        mixed_grad = jnp.einsum(
            "td,cd->tc", shard_rows, out_weight[block_index], preferred_element_type=jnp.float32
        ).astype(jnp.bfloat16)
        out_grad, mixed_grads = (out_grad, mixed_grad)
        grad_query, grad_key, grad_value = attention_backward(
            queries,
            key_all,
            value_all,
            log_total,
            mixed_grads.reshape(queries.shape),
            frame_only,
            score_scale,
        )
        raw_query_grad, query_gain_grad, query_offset_grad = jax.vjp(
            layer_norm, split[:, :, 0], head_gain[block_index, 0], head_offset[block_index, 0]
        )[1](grad_query)
        raw_key_grad, key_gain_grad, key_offset_grad = jax.vjp(
            layer_norm, split[:, :, 1], head_gain[block_index, 1], head_offset[block_index, 1]
        )[1](grad_key)
        projected_grad = (
            jnp.stack([raw_query_grad, raw_key_grad, grad_value], axis=2)
            .reshape(total_rows, -1)
            .astype(jnp.bfloat16)
        )
        qkv_weight_grad = jnp.einsum(
            "td,tc->dc", gathered, projected_grad, preferred_element_type=jnp.float32
        )
        qkv_bias_grad = jnp.sum(projected_grad.astype(jnp.float32), axis=0)
        normed_grad = lax.psum_scatter(
            jnp.einsum(
                "tc,dc->td",
                projected_grad,
                qkv_weight[block_index],
                preferred_element_type=jnp.float32,
            ).astype(jnp.bfloat16),
            TP,
            scatter_dimension=0,
            tiled=True,
        ).astype(jnp.float32)
        hidden_grad, gain_grad_zero, offset_grad_zero = jax.vjp(
            layer_norm, hidden, gains[0], offsets[0]
        )[1](normed_grad)
        hidden_grad = hidden_grad + middle_grad
        large_grads = (
            qkv_weight_grad,
            qkv_bias_grad,
            out_grad,
            up_weight_grad,
            up_bias_grad,
            down_grad,
        )
        small_grads = (
            jnp.stack([gain_grad_zero, gain_grad_one, gain_grad_two, gain_grad_three]),
            jnp.stack([offset_grad_zero, offset_grad_one, offset_grad_two, offset_grad_three]),
            jnp.stack([query_gain_grad, key_gain_grad]),
            jnp.stack([query_offset_grad, key_offset_grad]),
        )
        return (hidden_grad, large_grads, small_grads)

    hidden = frames.astype(jnp.float32)
    kept_states = []
    for block_index in range(2):
        forward_frame_only = block_index == 0
        forward_gains = norm_gain[block_index]
        forward_offsets = norm_offset[block_index]
        normed = layer_norm(hidden, forward_gains[0], forward_offsets[0]).astype(jnp.bfloat16)
        forward_gathered = lax.all_gather(normed, TP, axis=0, tiled=True)
        projected = jnp.dot(
            forward_gathered, qkv_weight[block_index], preferred_element_type=jnp.float32
        )
        projected = projected + qkv_bias[block_index].astype(jnp.float32)
        forward_total_rows = projected.shape[0]
        forward_split = projected.reshape(forward_total_rows, -1, 3, HD)
        forward_queries = layer_norm(
            forward_split[:, :, 0], head_gain[block_index, 0], head_offset[block_index, 0]
        ).astype(jnp.bfloat16)
        forward_key_all = layer_norm(
            forward_split[:, :, 1], head_gain[block_index, 1], head_offset[block_index, 1]
        ).astype(jnp.bfloat16)
        forward_value_all = forward_split[:, :, 2].astype(jnp.bfloat16)
        mixed, forward_log_total = attention_forward(
            forward_queries, forward_key_all, forward_value_all, forward_frame_only, score_scale
        )
        forward_mixed_flat = mixed.reshape(forward_total_rows, -1).astype(jnp.bfloat16)
        forward_branch = (
            lax.psum_scatter(
                jnp.dot(
                    forward_mixed_flat, out_weight[block_index], preferred_element_type=jnp.float32
                ).astype(jnp.bfloat16),
                TP,
                scatter_dimension=0,
                tiled=True,
            ).astype(jnp.float32)
            + forward_offsets[2]
        )
        forward_middle = hidden + forward_gains[2] * forward_branch
        second = layer_norm(forward_middle, forward_gains[1], forward_offsets[1]).astype(
            jnp.bfloat16
        )
        forward_gathered_two = lax.all_gather(second, TP, axis=0, tiled=True)
        forward_hidden_up = jnp.dot(
            forward_gathered_two, up_weight[block_index], preferred_element_type=jnp.float32
        )
        forward_hidden_up = forward_hidden_up + up_bias[block_index].astype(jnp.float32)
        forward_activated = exact_gelu(forward_hidden_up).astype(jnp.bfloat16)
        forward_branch_two = (
            lax.psum_scatter(
                jnp.dot(
                    forward_activated, down_weight[block_index], preferred_element_type=jnp.float32
                ).astype(jnp.bfloat16),
                TP,
                scatter_dimension=0,
                tiled=True,
            ).astype(jnp.float32)
            + forward_offsets[3]
        )
        result = forward_middle + forward_gains[3] * forward_branch_two
        forward_saved = (
            hidden,
            forward_gathered,
            forward_split,
            forward_queries,
            forward_key_all,
            forward_value_all,
            forward_log_total,
            forward_mixed_flat,
            forward_branch,
            forward_middle,
            forward_gathered_two,
            forward_hidden_up,
            forward_activated,
            forward_branch_two,
        )
        hidden = result
        saved = forward_saved
        kept_states.append(saved)
    layer_out = exchange(hidden.astype(jnp.bfloat16))[None]
    grad_hidden = cotangent.astype(jnp.float32) * weighting[:, None]
    grad_hidden, large_one, small_one = backward_block(grad_hidden, 1, False, kept_states[1])
    grad_hidden, large_zero, small_zero = backward_block(grad_hidden, 0, True, kept_states[0])
    input_grad = exchange(grad_hidden.astype(jnp.bfloat16))[None]

    def over_scenes(grads):
        shapes = [grad.shape for grad in grads]
        parts = lax.axis_size("sy")
        flat = [grad.astype(jnp.bfloat16).reshape(parts, -1) for grad in grads]
        sizes = [part.shape[1] for part in flat]
        joined = jnp.concatenate(flat, axis=1)
        share = lax.psum_scatter(joined, "sy", scatter_dimension=0, tiled=True)
        share = lax.psum(share, "h")
        whole = exchange(lax.all_gather(share, "sy", axis=0, tiled=True))
        found = []
        start = 0
        for shape, size in zip(shapes, sizes):
            found.append(whole[:, start : start + size].reshape(shape).astype(jnp.float32))
            start += size
        return found

    summed_one = over_scenes(large_one)
    summed_zero = over_scenes(large_zero)
    summed = [jnp.stack(pair) for pair in zip(summed_zero, summed_one)]
    small = jax.tree.map(lambda first, later: jnp.stack([first, later]), small_zero, small_one)
    summed = tuple(summed) + tuple(lax.psum(small, ("sy", "c", "h", "r")))
    return (
        layer_out,
        input_grad,
        summed[0],
        summed[1],
        summed[2],
        summed[3],
        summed[4],
        summed[5],
        summed[6],
        summed[7],
        summed[8],
        summed[9],
    )


def solution(mesh):
    scenes, shards = mesh.shape["scene"], mesh.shape["tp"]
    if (scenes, shards) == (4, 8):
        body, sizes, axes, tp = square_body, (2, 2, 2, 2, 2), AXES, ("h", "zl", "x")
    else:
        body, sizes, axes, tp = any_body, (scenes // 2, 2, 2, shards // 2), ("sy", "c", "h", "r"), ("h", "r")
    scene = ("sy", "c")
    return jax.shard_map(
        body,
        mesh=jax.sharding.Mesh(mesh.devices.reshape(sizes), axes),
        in_specs=(
            P(scene, tp, None),
            P(None, None, tp),
            P(None, tp),
            P(None, tp, None),
            P(None, None, tp),
            P(None, tp),
            P(None, tp, None),
            P(),
            P(),
            P(),
            P(),
            P(scene, tp, None),
            P(scene, tp),
            P(scene),
        ),
        out_specs=(
            P(scene, tp, None),
            P(scene, tp, None),
            P(None, None, tp),
            P(None, tp),
            P(None, tp, None),
            P(None, None, tp),
            P(None, tp),
            P(None, tp, None),
            P(),
            P(),
            P(),
            P(),
        ),
        check_vma=False,
    )
```
